128 devices in a mesh: row: 16 (over x, y_hi, core), col: 8 (over y_lo, z).
Axes of the slice: x: 4, y: 4 (y_hi: 2, y_lo: 2; y = y_hi * 2 + y_lo), z: 4, core: 2. Of those that a mesh axis runs over, the one named last changes fastest.
Arguments:
- pair: bfloat16 [768, 768, 128], P('row', 'col'), may hold values from -6 to 6
- residue_mask: int32 [768], replicated, may hold values 0 or 1
- left_weight: bfloat16 [128, 256], replicated, may hold values from -0.5 to 0.5
- right_weight: bfloat16 [128, 256], replicated, may hold values from -0.5 to 0.5
- gate_weight: bfloat16 [128, 128], replicated, may hold values from -0.5 to 0.5
- out_weight: bfloat16 [128, 128], replicated, may hold values from -0.5 to 0.5
- attn_weight: bfloat16 [128, 128], replicated, may hold values from -0.5 to 0.5
- bias_weight: bfloat16 [128], replicated
- attn_out_weight: bfloat16 [32, 128], replicated, may hold values from -1 to 1
Outputs:
- updated: bfloat16 [768, 768, 128], P('row', 'col')
The draws below stay inside these ranges and needn't reach their ends.
All inputs are finite; a program needn't handle non-finite values.
Results may differ from the reference program's by a relative error of at most 0.035.
Values may be sent and summed in bfloat16 or wider, within the bound.
No kernel may reach another device: no remote copies, remote signals or barrier semaphores. Data moves between devices by JAX's collectives and lax.ppermute only.
A program may use at most 128 MiB of HBM per device.

```python
import math
import jax
import jax.numpy as jnp
from jax import lax

C = 128
HD = 32
NRES = 768


def draw_bias_weight(key, part):
    key = jax.random.fold_in(key, 11)
    base = jax.random.normal(key, (C,), jnp.float32)
    return (base * (2.0 / math.sqrt(C))).astype(jnp.bfloat16)


def set_ends(entries, own_key, smallest, top_value):
    place = [jax.random.randint(jax.random.fold_in(own_key, axis), (), 0, length) for axis, length in enumerate(entries.shape)]
    main_axis = entries.shape.index(max(entries.shape))
    next_to = place[:main_axis] + [(place[main_axis] + 1) % entries.shape[main_axis]] + place[main_axis + 1:]
    return entries.at[tuple(place)].set(smallest).at[tuple(next_to)].set(top_value)


def block_levels(stream_key, extent, pieces, low, top_value):
    gain, own = 1.0, jax.random.fold_in(stream_key, 6)
    for axis_at, parts in pieces:
        steps = jnp.exp(jax.random.uniform(jax.random.fold_in(own, axis_at), (parts,), jnp.float32, low / len(pieces), top_value / len(pieces)))
        gain = gain * jnp.repeat(steps, extent[axis_at] // parts).reshape([-1 if axis == axis_at else 1 for axis in range(len(extent))])
    return gain


def scatter_about(stream_key, dims, width, most, cuts=(), held_as=jnp.bfloat16):
    array = jax.random.normal(stream_key, dims, jnp.float32) * width
    if len(cuts) > 0:
        array = block_levels(stream_key, dims, cuts, -0.22, 0.18) * array
    return jnp.clip(array, min=-most, max=most).astype(held_as)


def setup_inputs(seed: int = 0) -> dict:
    seeds = jax.random.split(jax.random.key(seed), 10)
    pair = scatter_about(seeds[0], (NRES, NRES, C), 1.0, 6.0, ((0, 16), (1, 8)))
    residue_mask = set_ends((jax.random.randint(seeds[1], (NRES,), 0, 8) < 7).astype(jnp.int32), jax.random.fold_in(seeds[1], 1), 0, 1)
    left_weight = scatter_about(seeds[2], (C, 2 * C), C ** -0.5, 0.5)
    right_weight = scatter_about(seeds[3], (C, 2 * C), C ** -0.5, 0.5)
    gate_weight = scatter_about(seeds[4], (C, C), C ** -0.5, 0.5)
    out_weight = scatter_about(seeds[5], (C, C), C ** -0.5, 0.5)
    attn_weight = scatter_about(seeds[6], (C, 4 * HD), C ** -0.5, 0.5)
    bias_weight = draw_bias_weight(jax.random.fold_in(seeds[9], 71), 0)
    attn_out_weight = scatter_about(seeds[8], (HD, C), HD ** -0.5, 1.0)
    return {"pair": pair, "residue_mask": residue_mask, "left_weight": left_weight, "right_weight": right_weight, "gate_weight": gate_weight, "out_weight": out_weight, "attn_weight": attn_weight, "bias_weight": bias_weight, "attn_out_weight": attn_out_weight}


def layer_norm(values):
    center = values - lax.optimization_barrier(jnp.mean(values, axis=-1, keepdims=True))
    spread = lax.optimization_barrier(jnp.mean(center * center, axis=-1, keepdims=True))
    return center * lax.rsqrt(spread + 1e-05)

def gated_side(normed, weight, mvec):
    proj = jnp.dot(normed, weight, preferred_element_type=jnp.float32)
    value = jax.nn.sigmoid(proj[..., C:]) * proj[..., :C]
    return (value * mvec[:, None, None] * mvec[None, :, None]).astype(jnp.bfloat16)

def reference(pair, residue_mask, left_weight, right_weight, gate_weight, out_weight, attn_weight, bias_weight, attn_out_weight):
    pair_f = pair.astype(jnp.float32)
    mvec = residue_mask.astype(jnp.float32)
    normed = layer_norm(pair_f).astype(jnp.bfloat16)
    left = gated_side(normed, left_weight, mvec)
    right = gated_side(normed, right_weight, mvec)
    tri_sum = jnp.einsum('ikc,jkc->ijc', left.astype(jnp.float32), right.astype(jnp.float32), precision=lax.Precision.HIGHEST)
    tri_normed = layer_norm(tri_sum).astype(jnp.bfloat16)
    gate = jax.nn.sigmoid(jnp.dot(normed, gate_weight, preferred_element_type=jnp.float32))
    first = pair_f + gate * jnp.dot(tri_normed, out_weight, preferred_element_type=jnp.float32)
    normed2 = layer_norm(first).astype(jnp.bfloat16)
    proj = jnp.dot(normed2, attn_weight, preferred_element_type=jnp.float32)
    query = proj[..., :HD].astype(jnp.bfloat16)
    keys = proj[..., HD:2 * HD].astype(jnp.bfloat16)
    values = proj[..., 2 * HD:3 * HD].astype(jnp.bfloat16)
    agate = proj[..., 3 * HD:]
    bias = jnp.dot(normed2, bias_weight, preferred_element_type=jnp.float32).astype(jnp.bfloat16)
    extra = bias.astype(jnp.float32) + 1000000000.0 * (mvec[None, :] - 1.0)
    scale = 1.0 / math.sqrt(HD)

    def one_row(items):
        q_row, k_row, v_row = items
        scores = jnp.dot(q_row, k_row.T, preferred_element_type=jnp.float32) * scale + extra
        expw = jnp.exp(scores - lax.optimization_barrier(jnp.max(scores, axis=-1, keepdims=True)))
        total = lax.optimization_barrier(jnp.sum(expw, axis=-1, keepdims=True))
        return jnp.dot(expw.astype(jnp.bfloat16), v_row, preferred_element_type=jnp.float32) / total
    attended = lax.map(one_row, (query, keys, values))
    gated = (jax.nn.sigmoid(agate) * attended).astype(jnp.bfloat16)
    return (first + jnp.dot(gated, attn_out_weight, preferred_element_type=jnp.float32)).astype(jnp.bfloat16)
```

```python
import functools
import math

import jax
import jax.numpy as jnp
from jax import lax
from jax.experimental import pallas as pl
from jax.experimental.pallas import tpu as pltpu
from jax.sharding import Mesh
from jax.sharding import PartitionSpec as P

F32 = jnp.float32
BF16 = jnp.bfloat16
LOG2E = math.log2(math.e)
ALL = ("x", "yh", "core", "yl", "z")
COL = ("yl", "z")
VMEM = pl.BlockSpec(memory_space=pltpu.VMEM)


def sigmoid(values):
    return 0.5 * jnp.tanh(0.5 * values) + 0.5


def layer_norm_rows(values):
    center = values - jnp.mean(values, axis=-1, keepdims=True)
    spread = jnp.mean(center * center, axis=-1, keepdims=True)
    return center * lax.rsqrt(spread + 1e-05)


def swap_blocks(parts):
    lane = lax.broadcasted_iota(jnp.int32, parts[0].shape, 1)
    odd = (lane // 32) % 2 == 1
    high = lane >= 64
    v0, v1, v2, v3 = parts
    a0 = jnp.where(odd, pltpu.roll(v1, 32, 1), v0)
    a1 = jnp.where(odd, v1, pltpu.roll(v0, 96, 1))
    a2 = jnp.where(odd, pltpu.roll(v3, 32, 1), v2)
    a3 = jnp.where(odd, v3, pltpu.roll(v2, 96, 1))
    return (
        jnp.where(high, pltpu.roll(a2, 64, 1), a0),
        jnp.where(high, pltpu.roll(a3, 64, 1), a1),
        jnp.where(high, a2, pltpu.roll(a0, 64, 1)),
        jnp.where(high, a3, pltpu.roll(a1, 64, 1)),
    )


def project_kernel(pair_ref, mask_ref, sides_ref, gate_w_ref, wire_ref, gate_ref, slab_ref):
    lane = lax.broadcasted_iota(jnp.int32, (128, 128), 1)

    def step(ii, carry):
        values = jnp.concatenate([pair_ref[s * 8 + ii] for s in range(6)], axis=0).astype(F32)
        normed = layer_norm_rows(values).astype(BF16)
        gate = jnp.dot(normed, gate_w_ref[...], preferred_element_type=F32)
        gate_ref[ii] = sigmoid(gate).astype(BF16)
        piece = lambda s, kc: normed[s * 96 + kc * 32 : s * 96 + kc * 32 + 32]
        for kc in range(3):
            rows = jnp.concatenate([piece(s, kc) for s in range(4)], axis=0)
            proj = lax.dot_general(
                sides_ref[...], rows, (((1,), (1,)), ((), ())), preferred_element_type=F32
            )
            left = sigmoid(proj[128:256]) * proj[0:128]
            right = sigmoid(proj[384:512]) * proj[256:384]
            slab_ref[pl.ds(pl.multiple_of((kc * 8 + ii) * 128, 128), 128), :] = left
            slab_ref[pl.ds(pl.multiple_of((24 + kc * 8 + ii) * 128, 128), 128), :] = right
        for kc in range(3):
            rows = jnp.concatenate([piece(s, kc) for s in (4, 5, 4, 5)], axis=0)
            proj = lax.dot_general(
                sides_ref[...], rows, (((1,), (1,)), ((), ())), preferred_element_type=F32
            )
            value = jnp.where(lane < 64, proj[0:128], proj[256:384])
            gating = jnp.where(lane < 64, proj[128:256], proj[384:512])
            slab_ref[pl.ds(pl.multiple_of((48 + kc * 8 + ii) * 128, 128), 128), :] = (
                sigmoid(gating) * value
            )
        return carry

    lax.fori_loop(0, 8, step, 0)

    def emit(ch, carry):
        wire_ref[ch] = (slab_ref[pl.ds(ch, 72, stride=128), :] * mask_ref[...]).astype(BF16)
        return carry

    lax.fori_loop(0, 128, emit, 0, unroll=4)


def triangle_kernel(wire_ref, out_ref, left_ref, right_ref, sums_ref):
    def unpack(c_pair, carry):
        for half in range(2):
            r = c_pair * 2 + half
            for yl in range(2):
                parts = [wire_ref[r * 8 + yl * 4 + z].astype(F32) for z in range(4)]
                w = swap_blocks(parts)
                for kc in range(3):
                    cols = pl.ds((yl * 3 + kc) * 128, 128)
                    at = lambda k, base: w[k][base + kc * 8 : base + kc * 8 + 8]
                    left = jnp.concatenate(
                        [at(s, 0) for s in range(4)] + [at(0, 48), at(1, 48)], axis=0
                    ).astype(BF16)
                    right = jnp.concatenate(
                        [at(s, 24) for s in range(4)] + [at(2, 48), at(3, 48)], axis=0
                    ).astype(BF16)
                    left_ref[pl.ds(pl.multiple_of(r * 48, 16), 48), cols] = left
                    for g3 in range(3):
                        g = half * 3 + g3
                        base = ((c_pair // 4) * 3 + g // 2) * 128 + (c_pair % 4) * 32 + (g % 2) * 16
                        right_ref[pl.ds(pl.multiple_of(base, 16), 16), cols] = right[
                            g3 * 16 : g3 * 16 + 16
                        ]
        return carry

    lax.fori_loop(0, 8, unpack, 0)
    for n in range(3):
        sums_ref[:, n * 256 : (n + 1) * 256] = lax.dot_general(
            left_ref[...],
            right_ref[n * 256 : (n + 1) * 256, :],
            (((1,), (1,)), ((), ())),
            preferred_element_type=F32,
        )

    def pack(r, carry):
        base = pl.multiple_of(r * 48, 16)
        rows = [sums_ref[pl.ds(pl.multiple_of(base + s * 8, 8), 8), :] for s in range(6)]
        for yl in range(2):
            tile = lambda s, jc: rows[s][:, (yl * 3 + jc) * 128 : (yl * 3 + jc + 1) * 128]
            outs = [swap_blocks([tile(s, jc) for s in range(4)]) for jc in range(3)]
            outs.append(swap_blocks([tile(4, 0), tile(5, 0), tile(4, 1), tile(5, 1)]))
            outs.append(swap_blocks([tile(4, 2), tile(5, 2), tile(4, 2), tile(5, 2)]))
            for z in range(4):
                out_ref[r * 8 + yl * 4 + z] = jnp.concatenate([o[z] for o in outs], axis=0).astype(
                    BF16
                )
        return carry

    lax.fori_loop(0, 16, pack, 0)


def first_kernel(
    wire_ref, pair_ref, gate_ref, out_w_ref, attn_w_ref, bias_w_ref, first_ref, send_ref, norm_ref, bias_ref
):
    def add(ch, total):
        return total + wire_ref[ch].astype(F32)

    zero = jnp.zeros((40, 128), F32)
    mean = lax.fori_loop(0, 128, add, zero, unroll=8) * (1.0 / 128)

    def add_square(ch, total):
        center = wire_ref[ch].astype(F32) - mean
        return total + center * center

    spread = lax.fori_loop(0, 128, add_square, zero, unroll=8) * (1.0 / 128)
    scale = lax.rsqrt(spread + 1e-05)

    def write(ch, carry):
        norm_ref[pl.ds(pl.multiple_of(ch * 40, 8), 40), :] = (
            wire_ref[ch].astype(F32) - mean
        ) * scale
        return carry

    lax.fori_loop(0, 128, write, 0, unroll=8)

    lane = lax.broadcasted_iota(jnp.int32, (1, 128), 1)
    query_scale = jnp.where(lane < 32, LOG2E / math.sqrt(32), 1.0)

    def step(ii, carry):
        slabs = []
        for base in (0, 8, 16, 24, 32):
            tn = norm_ref[pl.ds(base + ii, 128, stride=40), :]
            slabs.append(
                jnp.dot(tn.T.astype(BF16), out_w_ref[...], preferred_element_type=F32)
            )
        chunks = []
        for s in range(6):
            for jc in range(3):
                if s < 4:
                    slab, at = jc, s
                elif jc < 2:
                    slab, at = 3, jc * 2 + s - 4
                else:
                    slab, at = 4, s - 4
                chunks.append(slabs[slab][at * 32 : at * 32 + 32])
        update = jnp.concatenate(chunks, axis=0)
        values = jnp.concatenate([pair_ref[s * 8 + ii] for s in range(6)], axis=0).astype(F32)
        first = values + gate_ref[ii].astype(F32) * update
        first_ref[ii] = first
        normed = layer_norm_rows(first).astype(BF16)
        proj = jnp.dot(normed, attn_w_ref[...], preferred_element_type=F32)
        send_ref[ii, 0:576, :] = (proj * query_scale).astype(BF16)
        for s in range(6):
            row = jnp.concatenate(
                [normed[s * 96 : s * 96 + 96], normed[s * 96 : s * 96 + 32]], axis=0
            )
            bias = lax.dot_general(
                bias_w_ref[...], row, (((1,), (1,)), ((), ())), preferred_element_type=F32
            )
            bias_ref[pl.ds(s * 8 + ii, 1), :] = bias[0:1]
        return carry

    lax.fori_loop(0, 8, step, 0)
    bias = bias_ref[...].astype(BF16)
    for ii in range(8):
        send_ref[ii, 576:624, :] = bias


def bias_kernel(held_ref, out_ref):
    lane = lax.broadcasted_iota(jnp.int32, (48, 128), 1)
    tiles = []
    for yl in range(2):
        b = [held_ref[yl * 4 + z].astype(F32) for z in range(4)]
        r1, r2, r3 = pltpu.roll(b[1], 96, 1), pltpu.roll(b[2], 64, 1), pltpu.roll(b[3], 32, 1)
        tiles.append(jnp.where(lane < 96, b[0], r1))
        tiles.append(jnp.where(lane < 64, r1, r2))
        tiles.append(jnp.where(lane < 32, r2, r3))
    whole = jnp.concatenate(tiles, axis=1).astype(BF16)
    for copy in range(8):
        out_ref[copy] = whole


def attend_kernel(held_ref, bias_ref, mask_ref, spread_ref, out_ref, extra_ref, packed_ref):
    def fill(r, carry):
        extra_ref[pl.ds(pl.multiple_of(r * 48, 16), 48), :] = (
            bias_ref[r].astype(F32) * LOG2E + mask_ref[...]
        )
        return carry

    lax.fori_loop(0, 16, fill, 0)
    lane = lax.broadcasted_iota(jnp.int32, (24, 128), 1)

    def step(s, carry):
        rows = jnp.concatenate(
            [held_ref[c, pl.ds(pl.multiple_of(s * 96, 32), 96), :] for c in range(8)], axis=0
        )
        moved = jnp.dot(rows, spread_ref[...], preferred_element_type=F32)
        key = moved[:, 0:128].astype(BF16)
        value = jnp.concatenate([moved[:, 128:256].astype(BF16), jnp.ones((768, 128), BF16)], axis=1)
        for t in range(4):
            scores = lax.dot_general(
                rows[t * 192 : (t + 1) * 192],
                key,
                (((1,), (1,)), ((), ())),
                preferred_element_type=F32,
            )
            scores = scores + extra_ref[t * 192 : (t + 1) * 192, :]
            top = jnp.max(scores, axis=-1, keepdims=True)
            weights = jnp.exp2(scores - top).astype(BF16)
            summed = jnp.dot(weights, value, preferred_element_type=F32)
            gated = sigmoid(moved[t * 192 : (t + 1) * 192, 256:384]) * (
                summed[:, 0:128] / summed[:, 128:256]
            )
            for h in range(2):
                c = t * 2 + h
                g = [gated[h * 96 + k * 24 : h * 96 + k * 24 + 24] for k in range(4)]
                low = jnp.where(lane < 32, g[0], g[1])
                high = jnp.where(lane < 96, g[2], g[3])
                packed_ref[pl.ds(pl.multiple_of(c * 144 + s * 24, 8), 24), :] = jnp.where(
                    lane < 64, low, high
                )
        return carry

    lax.fori_loop(0, 6, step, 0)
    for c in range(8):
        out_ref[c] = packed_ref[c * 144 : (c + 1) * 144, :].astype(BF16)


def update_kernel(held_ref, first_ref, weight_ref, out_ref):
    def step(ii, carry):
        add = jnp.dot(held_ref[ii], weight_ref[...], preferred_element_type=F32)
        for s in range(6):
            rows = jnp.concatenate(
                [add[s * 24 : s * 24 + 24, g * 128 : (g + 1) * 128] for g in range(4)], axis=0
            )
            out_ref[s * 8 + ii] = (first_ref[ii, s * 96 : (s + 1) * 96, :] + rows).astype(BF16)
        return carry

    lax.fori_loop(0, 8, step, 0)


def call(kernel, outs, n_in, scratch=()):
    return pl.pallas_call(
        kernel,
        out_shape=outs,
        in_specs=[VMEM] * n_in,
        out_specs=jax.tree.map(lambda _: VMEM, outs),
        scratch_shapes=list(scratch),
        compiler_params=pltpu.CompilerParams(vmem_limit_bytes=48 * 1024 * 1024),
    )


def shape(dims, dtype=BF16):
    return jax.ShapeDtypeStruct(dims, dtype)


def exchange(values, axes):
    return lax.all_to_all(values, axes, 0, 0, tiled=True)


def body(
    pair,
    residue_mask,
    left_weight,
    right_weight,
    gate_weight,
    out_weight,
    attn_weight,
    bias_weight,
    attn_out_weight,
):
    row_pos = lax.axis_index(("x", "yh", "core"))
    col_pos = lax.axis_index(COL)
    mvec = residue_mask.astype(F32)
    row_mask = lax.dynamic_slice_in_dim(mvec, row_pos * 48, 48)
    col_mask = lax.dynamic_slice_in_dim(mvec, col_pos * 96, 96)
    main = (
        row_mask[:32].reshape(4, 8).T[None, :, :, None] * col_mask.reshape(3, 1, 1, 32)
    ).reshape(24, 128)
    rest_rows = jnp.concatenate([row_mask[32:].reshape(2, 8)] * 2, axis=0)
    rest = (rest_rows.T[None, :, :, None] * col_mask.reshape(3, 1, 1, 32)).reshape(24, 128)
    mask_wire = jnp.concatenate([main, main, rest], axis=0)

    sides = jnp.concatenate([left_weight, right_weight], axis=1).T
    wire, gate = call(
        project_kernel,
        (shape((128, 72, 128)), shape((8, 576, 128))),
        4,
        [pltpu.VMEM((72 * 128, 128), F32)],
    )(pair, mask_wire, sides, gate_weight)
    wire = exchange(wire, ALL)
    sums = call(
        triangle_kernel,
        shape((128, 40, 128)),
        1,
        [pltpu.VMEM((768, 768), BF16), pltpu.VMEM((768, 768), BF16), pltpu.VMEM((768, 768), F32)],
    )(wire)
    sums = exchange(sums, ALL)

    lane = jnp.arange(128)
    bias_w = jnp.concatenate([bias_weight[None, :], jnp.zeros((15, 128), BF16)], axis=0)
    first, send = call(
        first_kernel,
        (shape((8, 576, 128), F32), shape((8, 624, 128))),
        6,
        [pltpu.VMEM((128 * 40, 128), F32), pltpu.VMEM((48, 128), F32)],
    )(sums, pair, gate, out_weight, attn_weight, bias_w)
    held = exchange(send, COL)

    bias = call(bias_kernel, shape((8, 48, 768)), 1)(held[:, 576:624, :])
    bias = exchange(bias, ("x", "yh"))
    other = lax.ppermute(bias, "core", [(0, 1), (1, 0)])
    core = lax.axis_index("core")
    bias = jnp.where(
        core == 0, jnp.stack([bias, other], axis=1), jnp.stack([other, bias], axis=1)
    ).reshape(16, 48, 768)

    row = jnp.arange(128)[:, None]
    key_move = (row == lane[None, :] + 32) & (lane[None, :] < 32)
    value_move = row == lane[None, :] % 32 + 64
    gate_move = row == lane[None, :] % 32 + 96
    spread = jnp.concatenate([key_move, value_move, gate_move], axis=1).astype(BF16)
    mask_add = (1e9 * LOG2E) * (mvec[None, :] - 1.0)
    gated = call(
        attend_kernel,
        shape((8, 144, 128)),
        4,
        [pltpu.VMEM((768, 768), F32), pltpu.VMEM((8 * 144, 128), F32)],
    )(held, bias, mask_add, spread)
    gated = exchange(gated, COL)

    out_w = jnp.concatenate(
        [jnp.pad(attn_out_weight, ((g * 32, 96 - g * 32), (0, 0))) for g in range(4)], axis=1
    )
    return call(update_kernel, shape((48, 96, 128)), 3)(gated, first, out_w)


def solution(mesh):
    parts = Mesh(mesh.devices.reshape(4, 2, 2, 2, 4), ALL)
    spec = P(("x", "yh", "core"), COL, None)
    return jax.shard_map(
        body,
        mesh=parts,
        in_specs=(spec, P(), P(), P(), P(), P(), P(), P(), P()),
        out_specs=spec,
        check_vma=False,
    )
```

```python
import math

import jax
import jax.numpy as jnp
import numpy as np
from jax import lax
from jax.experimental import pallas as pl
from jax.experimental.pallas import tpu as pltpu
from jax.sharding import Mesh
from jax.sharding import PartitionSpec as P

F32 = jnp.float32
BF16 = jnp.bfloat16
LOG2E = math.log2(math.e)
PITCH = 136
UNROLL_PROJECT = 2
LIMIT_PROJECT = 60
LIMIT_TRIANGLE = 20
LIMIT_FIRST = 20
LIMIT_UPDATE = 20
UNROLL_UNPACK = 2
UNROLL_PACK = 2
UNROLL_FIRST = 2
UNROLL_ATTEND = 2
UNROLL_UPDATE = 4
ALL = ("x", "yh", "core", "yl", "z")
COL = ("yl", "z")
VMEM = pl.BlockSpec(memory_space=pltpu.VMEM)
HBM = pl.BlockSpec(memory_space=pltpu.HBM)


def swap_matrix():
    at = np.arange(512)
    target = at % 128 // 32 * 128 + at // 128 * 32 + at % 32
    return (target[:, None] == at[None, :]).astype(np.float32)


def move_matrix():
    row, lane = np.arange(128)[:, None], np.arange(128)[None, :]
    key = (row == lane + 32) & (lane < 32)
    return np.concatenate([key, row == lane % 32 + 64, row == lane % 32 + 96], axis=1).astype(
        np.float32
    )


SWAP = swap_matrix()
MOVE = move_matrix()


def sigmoid(values):
    return 0.5 * jnp.tanh(0.5 * values) + 0.5


def layer_norm_rows(values):
    center = values - jnp.mean(values, axis=-1, keepdims=True)
    spread = jnp.mean(center * center, axis=-1, keepdims=True)
    return center * lax.rsqrt(spread + 1e-05)


def swap_blocks(parts):
    lane = lax.broadcasted_iota(jnp.int32, parts[0].shape, 1)
    odd = jnp.bitwise_and(lane, 32) != 0
    high = lane >= 64
    v0, v1, v2, v3 = parts
    a0 = jnp.where(odd, pltpu.roll(v1, 32, 1), v0)
    a1 = jnp.where(odd, v1, pltpu.roll(v0, 96, 1))
    a2 = jnp.where(odd, pltpu.roll(v3, 32, 1), v2)
    a3 = jnp.where(odd, v3, pltpu.roll(v2, 96, 1))
    return (
        jnp.where(high, pltpu.roll(a2, 64, 1), a0),
        jnp.where(high, pltpu.roll(a3, 64, 1), a1),
        jnp.where(high, a2, pltpu.roll(a0, 64, 1)),
        jnp.where(high, a3, pltpu.roll(a1, 64, 1)),
    )


def project_kernel(
    pair_hbm, mask_ref, left_hbm, right_hbm, gate_hbm, wire_ref, gate_out, held_ref, slab_ref,
    left_ref, right_ref, gate_w_ref, sides_ref, col_ref, gated_ref, sems, w_sems, out_sems,
):
    loads = [
        pltpu.make_async_copy(
            pair_hbm.at[:, 2 * q : 2 * q + 2], held_ref.at[:, 2 * q : 2 * q + 2], sems.at[q]
        )
        for q in range(4)
    ]
    weights = [
        pltpu.make_async_copy(left_hbm, left_ref, w_sems.at[0]),
        pltpu.make_async_copy(right_hbm, right_ref, w_sems.at[1]),
        pltpu.make_async_copy(gate_hbm, gate_w_ref, w_sems.at[2]),
    ]
    for copy in weights + loads:
        copy.start()
    row_base = lax.axis_index(("x", "yh", "core")) * 48
    col_base = lax.axis_index(COL) * 96

    def mask_row(k, carry):
        col_ref[pl.ds(k, 1), :] = jnp.full((1, 128), mask_ref[col_base + k].astype(F32))
        return carry

    lax.fori_loop(0, 96, mask_row, 0, unroll=8)
    for copy in weights:
        copy.wait()
    sides_ref[0:256, :] = left_ref[...].T
    sides_ref[256:512, :] = right_ref[...].T
    lane = lax.broadcasted_iota(jnp.int32, (128, 128), 1)

    def step(ii, carry):
        values = jnp.concatenate([held_ref[s, ii] for s in range(6)], axis=0).astype(F32)
        normed = layer_norm_rows(values)
        gate = jnp.dot(normed.astype(BF16), gate_w_ref[...], preferred_element_type=F32)
        gated_ref[ii] = sigmoid(gate).astype(BF16)
        pltpu.make_async_copy(gated_ref.at[ii], gate_out.at[ii], out_sems.at[ii]).start()
        kept = [
            (
                normed[s * 96 : s * 96 + 96]
                * (col_ref[...] * mask_ref[row_base + s * 8 + ii].astype(F32))
            ).astype(BF16)
            for s in range(6)
        ]
        piece = lambda s, kc: kept[s][kc * 32 : kc * 32 + 32]
        store = lambda row: pl.ds(pl.multiple_of(row * PITCH, 8), 128)
        for kc in range(3):
            rows = jnp.concatenate([piece(s, kc) for s in range(4)], axis=0)
            proj = lax.dot_general(
                sides_ref[...], rows, (((1,), (1,)), ((), ())), preferred_element_type=F32
            )
            slab_ref[store(kc * 8 + ii), :] = sigmoid(proj[128:256]) * proj[0:128]
            slab_ref[store(24 + kc * 8 + ii), :] = sigmoid(proj[384:512]) * proj[256:384]
        for kc in range(3):
            rows = jnp.concatenate([piece(s, kc) for s in (4, 5, 4, 5)], axis=0)
            proj = lax.dot_general(
                sides_ref[...], rows, (((1,), (1,)), ((), ())), preferred_element_type=F32
            )
            value = jnp.where(lane < 64, proj[0:128], proj[256:384])
            gating = jnp.where(lane < 64, proj[128:256], proj[384:512])
            slab_ref[store(48 + kc * 8 + ii), :] = sigmoid(gating) * value
        return carry

    for q in range(4):
        loads[q].wait()
        lax.fori_loop(2 * q, 2 * q + 2, step, 0, unroll=UNROLL_PROJECT)

    def emit(ch, carry):
        wire_ref[ch] = slab_ref[pl.ds(ch, 72, stride=PITCH), :].astype(BF16)
        return carry

    lax.fori_loop(0, 128, emit, 0, unroll=4)
    for ii in range(8):
        pltpu.make_async_copy(gated_ref.at[ii], gate_out.at[ii], out_sems.at[ii]).wait()


def triangle_kernel(wire_ref, perm_ref, out_ref, left_ref, right_ref, sums_ref):
    def unpack(c_pair, carry):
        groups = [(half, yl) for half in range(2) for yl in range(2)]
        source = lambda half, yl, z: wire_ref[(c_pair * 2 + half) * 8 + yl * 4 + z]
        rows = jnp.concatenate(
            [
                jnp.concatenate([source(half, yl, z) for z in range(4)], axis=1)
                for half, yl in groups
            ],
            axis=0,
        )
        swapped = jnp.dot(rows, perm_ref[...], preferred_element_type=F32)
        for n, (half, yl) in enumerate(groups):
            at = lambda k, base: swapped[
                n * 72 + base + kc * 8 : n * 72 + base + kc * 8 + 8, k * 128 : k * 128 + 128
            ]
            for kc in range(3):
                cols = pl.ds((yl * 3 + kc) * 128, 128)
                left = jnp.concatenate(
                    [at(s, 0) for s in range(4)] + [at(0, 48), at(1, 48)], axis=0
                ).astype(BF16)
                right = jnp.concatenate(
                    [at(s, 24) for s in range(4)] + [at(2, 48), at(3, 48)], axis=0
                ).astype(BF16)
                row = pl.multiple_of((c_pair * 2 + half) * 48, 16)
                left_ref[pl.ds(row, 48), cols] = left
                for g3 in range(3):
                    g = half * 3 + g3
                    base = ((c_pair // 4) * 3 + g // 2) * 128 + (c_pair % 4) * 32 + (g % 2) * 16
                    right_ref[pl.ds(pl.multiple_of(base, 16), 16), cols] = right[
                        g3 * 16 : g3 * 16 + 16
                    ]
        return carry

    lax.fori_loop(0, 8, unpack, 0, unroll=UNROLL_UNPACK)
    for n in range(3):
        sums_ref[:, n * 256 : (n + 1) * 256] = lax.dot_general(
            left_ref[...],
            right_ref[n * 256 : (n + 1) * 256, :],
            (((1,), (1,)), ((), ())),
            preferred_element_type=F32,
        )

    def pack(r, carry):
        base = pl.multiple_of(r * 48, 16)
        order = (
            [(s, 0) for s in range(4)],
            [(s, 1) for s in range(4)],
            [(s, 2) for s in range(4)],
            [(4, 0), (5, 0), (4, 1), (5, 1)],
            [(4, 2), (5, 2), (4, 2), (5, 2)],
        )
        for yl in range(2):
            tile = lambda s, jc: sums_ref[
                pl.ds(pl.multiple_of(base + s * 8, 8), 8),
                (yl * 3 + jc) * 128 : (yl * 3 + jc + 1) * 128,
            ]
            parts = [
                jnp.concatenate([tile(*entry[a]) for entry in order], axis=0) for a in range(4)
            ]
            outs = swap_blocks(parts)
            for z in range(4):
                out_ref[r * 8 + yl * 4 + z] = outs[z].astype(BF16)
        return carry

    lax.fori_loop(0, 16, pack, 0, unroll=UNROLL_PACK)


def first_kernel(
    wire_ref, pair_hbm, gate_hbm, out_w_ref, attn_w_ref, bias_w_ref, mask_ref,
    first_out, send_ref, held_ref, gate_ref, first_ref, norm_ref, bias_ref, sems, out_sems,
):
    loads = [
        pltpu.make_async_copy(pair_hbm, held_ref, sems.at[0]),
        pltpu.make_async_copy(gate_hbm, gate_ref, sems.at[1]),
    ]
    for copy in loads:
        copy.start()

    def add(ch, total):
        return total + wire_ref[ch].astype(F32)

    zero = jnp.zeros((40, 128), F32)
    mean = lax.fori_loop(0, 128, add, zero, unroll=8) * (1.0 / 128)

    def add_square(ch, total):
        center = wire_ref[ch].astype(F32) - mean
        return total + center * center

    spread = lax.fori_loop(0, 128, add_square, zero, unroll=8) * (1.0 / 128)
    scale = lax.rsqrt(spread + 1e-05)

    def write(ch, carry):
        norm_ref[pl.ds(pl.multiple_of(ch * 40, 8), 40), :] = (
            wire_ref[ch].astype(F32) - mean
        ) * scale
        return carry

    lax.fori_loop(0, 128, write, 0, unroll=8)
    lane = lax.broadcasted_iota(jnp.int32, (1, 128), 1)
    query_scale = jnp.where(lane < 32, LOG2E / math.sqrt(32), 1.0)
    bias_w = jnp.broadcast_to(bias_w_ref[...], (16, 128))

    def step(ii, carry):
        slabs = []
        for base in (0, 8, 16, 24, 32):
            tn = norm_ref[pl.ds(base + ii, 128, stride=40), :]
            slabs.append(
                jnp.dot(tn.T.astype(BF16), out_w_ref[...], preferred_element_type=F32)
            )
        chunks = []
        for s in range(6):
            for jc in range(3):
                if s < 4:
                    slab, at = jc, s
                elif jc < 2:
                    slab, at = 3, jc * 2 + s - 4
                else:
                    slab, at = 4, s - 4
                chunks.append(slabs[slab][at * 32 : at * 32 + 32])
        update = jnp.concatenate(chunks, axis=0)
        values = jnp.concatenate([held_ref[s, ii] for s in range(6)], axis=0).astype(F32)
        first = values + gate_ref[ii].astype(F32) * update
        first_ref[ii] = first
        pltpu.make_async_copy(first_ref.at[ii], first_out.at[ii], out_sems.at[ii]).start()
        normed = layer_norm_rows(first).astype(BF16)
        proj = jnp.dot(normed, attn_w_ref[...], preferred_element_type=F32)
        send_ref[ii, 0:576, :] = (proj * query_scale).astype(BF16)
        for s in range(6):
            row = jnp.concatenate(
                [normed[s * 96 : s * 96 + 96], normed[s * 96 : s * 96 + 32]], axis=0
            )
            bias = lax.dot_general(
                bias_w, row, (((1,), (1,)), ((), ())), preferred_element_type=F32
            )
            bias_ref[pl.ds(s * 8 + ii, 1), :] = bias[0:1]
        return carry

    for copy in loads:
        copy.wait()
    lax.fori_loop(0, 8, step, 0, unroll=UNROLL_FIRST)
    bias = jnp.where(mask_ref[...] > 0, bias_ref[...] * LOG2E, -1e9 * LOG2E).astype(BF16)
    for ii in range(8):
        send_ref[ii, 576:624, :] = bias
    for ii in range(8):
        pltpu.make_async_copy(first_ref.at[ii], first_out.at[ii], out_sems.at[ii]).wait()


def bias_kernel(held_ref, out_ref):
    lane = lax.broadcasted_iota(jnp.int32, (48, 128), 1)
    tiles = []
    for yl in range(2):
        b = [held_ref[yl * 4 + z, 576:624, :].astype(F32) for z in range(4)]
        r1, r2, r3 = pltpu.roll(b[1], 96, 1), pltpu.roll(b[2], 64, 1), pltpu.roll(b[3], 32, 1)
        tiles.append(jnp.where(lane < 96, b[0], r1))
        tiles.append(jnp.where(lane < 64, r1, r2))
        tiles.append(jnp.where(lane < 32, r2, r3))
    whole = jnp.concatenate(tiles, axis=1).astype(BF16)
    for copy in range(8):
        out_ref[copy] = whole


def attend_kernel(held_ref, mine_ref, other_ref, move_ref, out_ref, extra_ref, packed_ref):
    core = lax.axis_index("core")

    def fill(chip, carry):
        for ref, at in ((mine_ref, core), (other_ref, 1 - core)):
            rows = pl.ds(pl.multiple_of(chip * 96 + at * 48, 16), 48)
            extra_ref[rows, :] = ref[chip].astype(F32)
        return carry

    lax.fori_loop(0, 8, fill, 0)
    lane = lax.broadcasted_iota(jnp.int32, (24, 128), 1)

    def step(s, carry):
        rows = jnp.concatenate(
            [held_ref[c, pl.ds(pl.multiple_of(s * 96, 32), 96), :] for c in range(8)], axis=0
        )
        moved = jnp.dot(rows, move_ref[...], preferred_element_type=F32)
        key = moved[:, 0:128].astype(BF16)
        value = jnp.concatenate([moved[:, 128:256].astype(BF16), jnp.ones((768, 128), BF16)], axis=1)
        for t in range(4):
            scores = lax.dot_general(
                rows[t * 192 : (t + 1) * 192],
                key,
                (((1,), (1,)), ((), ())),
                preferred_element_type=F32,
            )
            scores = scores + extra_ref[t * 192 : (t + 1) * 192, :]
            top = jnp.max(scores, axis=-1, keepdims=True)
            weights = jnp.exp2(scores - top).astype(BF16)
            summed = jnp.dot(weights, value, preferred_element_type=F32)
            gated = sigmoid(moved[t * 192 : (t + 1) * 192, 256:384]) * (
                summed[:, 0:128] / summed[:, 128:256]
            )
            for h in range(2):
                c = t * 2 + h
                g = [gated[h * 96 + k * 24 : h * 96 + k * 24 + 24] for k in range(4)]
                low = jnp.where(lane < 32, g[0], g[1])
                high = jnp.where(lane < 96, g[2], g[3])
                packed_ref[pl.ds(pl.multiple_of(c * 144 + s * 24, 8), 24), :] = jnp.where(
                    lane < 64, low, high
                )
        return carry

    lax.fori_loop(0, 6, step, 0, unroll=UNROLL_ATTEND)
    for c in range(8):
        out_ref[c] = packed_ref[c * 144 : (c + 1) * 144, :].astype(BF16)


def update_kernel(
    held_ref, first_hbm, weight_ref, out_hbm, first_ref, wide_ref, done_ref, sems, out_sems
):
    def load(ii):
        return pltpu.make_async_copy(first_hbm.at[ii], first_ref.at[ii], sems.at[ii])

    def store(ii):
        return pltpu.make_async_copy(done_ref.at[:, ii], out_hbm.at[:, ii], out_sems.at[ii])

    for ii in range(8):
        load(ii).start()
    wide_ref[...] = jnp.zeros((128, 512), BF16)
    for g in range(4):
        wide_ref[g * 32 : g * 32 + 32, g * 128 : g * 128 + 128] = weight_ref[...]

    def step(ii, carry):
        load(ii).wait()
        add = jnp.dot(held_ref[ii], wide_ref[...], preferred_element_type=F32)
        for s in range(6):
            rows = jnp.concatenate(
                [add[s * 24 : s * 24 + 24, g * 128 : (g + 1) * 128] for g in range(4)], axis=0
            )
            done_ref[s, ii] = (first_ref[ii, s * 96 : (s + 1) * 96, :] + rows).astype(BF16)
        store(ii).start()
        return carry

    lax.fori_loop(0, 8, step, 0, unroll=UNROLL_UPDATE)
    for ii in range(8):
        store(ii).wait()


def call(kernel, outs, in_specs, out_specs, scratch, limit=20):
    return pl.pallas_call(
        kernel,
        out_shape=outs,
        in_specs=in_specs,
        out_specs=out_specs,
        scratch_shapes=scratch,
        compiler_params=pltpu.CompilerParams(vmem_limit_bytes=limit * 1024 * 1024),
    )


def shape(dims, dtype=BF16):
    return jax.ShapeDtypeStruct(dims, dtype)


def exchange(values, axes):
    return lax.all_to_all(values, axes, 0, 0, tiled=True)


def body(
    pair,
    residue_mask,
    left_weight,
    right_weight,
    gate_weight,
    out_weight,
    attn_weight,
    bias_weight,
    attn_out_weight,
):
    pair = pair.reshape(6, 8, 96, 128)
    wire, gate = call(
        project_kernel,
        (shape((128, 72, 128)), shape((8, 576, 128))),
        [HBM, pl.BlockSpec(memory_space=pltpu.SMEM), HBM, HBM, HBM],
        (VMEM, HBM),
        [
            pltpu.VMEM((6, 8, 96, 128), BF16),
            pltpu.VMEM((72 * PITCH, 128), F32),
            pltpu.VMEM((128, 256), BF16),
            pltpu.VMEM((128, 256), BF16),
            pltpu.VMEM((128, 128), BF16),
            pltpu.VMEM((512, 128), BF16),
            pltpu.VMEM((96, 128), F32),
            pltpu.VMEM((8, 576, 128), BF16),
            pltpu.SemaphoreType.DMA((4,)),
            pltpu.SemaphoreType.DMA((3,)),
            pltpu.SemaphoreType.DMA((8,)),
        ],
        LIMIT_PROJECT,
    )(pair, residue_mask, left_weight, right_weight, gate_weight)
    wire = exchange(wire, ALL)
    sums = call(
        triangle_kernel,
        shape((128, 40, 128)),
        [VMEM, VMEM],
        VMEM,
        [pltpu.VMEM((768, 768), BF16), pltpu.VMEM((768, 768), BF16), pltpu.VMEM((768, 768), F32)],
        LIMIT_TRIANGLE,
    )(wire, jnp.asarray(SWAP, BF16))
    sums = exchange(sums, ALL)

    col_mask = lax.dynamic_slice_in_dim(residue_mask, lax.axis_index(COL) * 96, 96)
    col_mask = jnp.pad(col_mask, (0, 32))[None, :]
    first, send = call(
        first_kernel,
        (shape((8, 576, 128), F32), shape((8, 624, 128))),
        [VMEM, HBM, HBM] + [VMEM] * 4,
        (HBM, VMEM),
        [
            pltpu.VMEM((6, 8, 96, 128), BF16),
            pltpu.VMEM((8, 576, 128), BF16),
            pltpu.VMEM((8, 576, 128), F32),
            pltpu.VMEM((128 * 40, 128), F32),
            pltpu.VMEM((48, 128), F32),
            pltpu.SemaphoreType.DMA((2,)),
            pltpu.SemaphoreType.DMA((8,)),
        ],
        LIMIT_FIRST,
    )(sums, pair, gate, out_weight, attn_weight, bias_weight[None, :], col_mask)
    held = exchange(send, COL)
    bias = call(bias_kernel, shape((8, 48, 768)), [VMEM], VMEM, [])(held)
    bias = exchange(bias, ("x", "yh"))
    other = lax.ppermute(bias, "core", [(0, 1), (1, 0)])
    gated = call(
        attend_kernel,
        shape((8, 144, 128)),
        [VMEM] * 4,
        VMEM,
        [pltpu.VMEM((768, 768), F32), pltpu.VMEM((8 * 144, 128), F32)],
    )(held, bias, other, jnp.asarray(MOVE, BF16))
    gated = exchange(gated, COL)
    updated = call(
        update_kernel,
        shape((6, 8, 96, 128)),
        [VMEM, HBM, VMEM],
        HBM,
        [
            pltpu.VMEM((8, 576, 128), F32),
            pltpu.VMEM((128, 512), BF16),
            pltpu.VMEM((6, 8, 96, 128), BF16),
            pltpu.SemaphoreType.DMA((8,)),
            pltpu.SemaphoreType.DMA((8,)),
        ],
        LIMIT_UPDATE,
    )(gated, first, attn_out_weight)
    return updated.reshape(48, 96, 128)


def solution(mesh):
    parts = Mesh(mesh.devices.reshape(4, 2, 2, 2, 4), ALL)
    spec = P(("x", "yh", "core"), COL, None)
    return jax.shard_map(
        body,
        mesh=parts,
        in_specs=(spec, P(), P(), P(), P(), P(), P(), P(), P()),
        out_specs=spec,
        check_vma=False,
    )
```

```python
import math

import jax
import jax.numpy as jnp
import numpy as np
from jax import lax
from jax.experimental import pallas as pl
from jax.experimental.pallas import tpu as pltpu
from jax.sharding import Mesh
from jax.sharding import PartitionSpec as P

F32 = jnp.float32
BF16 = jnp.bfloat16
LOG2E = math.log2(math.e)
PITCH = 136
UNROLL_PROJECT = 2
WORK_MINE = 30
WORK_SCORE = 30
LIMIT_OTHER = 20
LIMIT_PROJECT = 60
LIMIT_TRIANGLE = 20
LIMIT_FIRST = 20
LIMIT_UPDATE = 20
UNROLL_UNPACK = 4
UNROLL_PACK = 2
UNROLL_FIRST = 2
UNROLL_ATTEND = 6
UNROLL_UPDATE = 4
ALL = ("x", "yh", "core", "yl", "z")
COL = ("yl", "z")
VMEM = pl.BlockSpec(memory_space=pltpu.VMEM)
HBM = pl.BlockSpec(memory_space=pltpu.HBM)


def swap_matrix():
    at = np.arange(512)
    target = at % 128 // 32 * 128 + at // 128 * 32 + at % 32
    return (target[:, None] == at[None, :]).astype(np.float32)


def move_matrix():
    row, lane = np.arange(128)[:, None], np.arange(128)[None, :]
    key = (row == lane + 32) & (lane < 32)
    return np.concatenate([key, row == lane % 32 + 64, row == lane % 32 + 96], axis=1).astype(
        np.float32
    )


SWAP = swap_matrix()
MOVE = move_matrix()


def sigmoid(values):
    return 0.5 * jnp.tanh(0.5 * values) + 0.5


def layer_norm_rows(values):
    center = values - jnp.mean(values, axis=-1, keepdims=True)
    spread = jnp.mean(center * center, axis=-1, keepdims=True)
    return center * lax.rsqrt(spread + 1e-05)


def swap_blocks(parts):
    lane = lax.broadcasted_iota(jnp.int32, parts[0].shape, 1)
    odd = jnp.bitwise_and(lane, 32) != 0
    high = lane >= 64
    v0, v1, v2, v3 = parts
    a0 = jnp.where(odd, pltpu.roll(v1, 32, 1), v0)
    a1 = jnp.where(odd, v1, pltpu.roll(v0, 96, 1))
    a2 = jnp.where(odd, pltpu.roll(v3, 32, 1), v2)
    a3 = jnp.where(odd, v3, pltpu.roll(v2, 96, 1))
    return (
        jnp.where(high, pltpu.roll(a2, 64, 1), a0),
        jnp.where(high, pltpu.roll(a3, 64, 1), a1),
        jnp.where(high, a2, pltpu.roll(a0, 64, 1)),
        jnp.where(high, a3, pltpu.roll(a1, 64, 1)),
    )


def project_kernel(
    pair_hbm, mask_ref, left_hbm, right_hbm, wire_out, held_ref, slab_ref,
    left_ref, right_ref, sides_ref, col_ref, wire_ref, sems, w_sems, out_sems,
):
    loads = [
        pltpu.make_async_copy(
            pair_hbm.at[:, 2 * q : 2 * q + 2], held_ref.at[:, 2 * q : 2 * q + 2], sems.at[q]
        )
        for q in range(4)
    ]
    weights = [
        pltpu.make_async_copy(left_hbm, left_ref, w_sems.at[0]),
        pltpu.make_async_copy(right_hbm, right_ref, w_sems.at[1]),
    ]
    for copy in weights + loads:
        copy.start()
    row_base = lax.axis_index(("x", "yh", "core")) * 48
    col_base = lax.axis_index(COL) * 96

    def mask_row(k, carry):
        col_ref[pl.ds(k, 1), :] = jnp.full((1, 128), mask_ref[col_base + k].astype(F32))
        return carry

    lax.fori_loop(0, 96, mask_row, 0, unroll=8)
    for copy in weights:
        copy.wait()
    sides_ref[0:256, :] = left_ref[...].T
    sides_ref[256:512, :] = right_ref[...].T
    lane = lax.broadcasted_iota(jnp.int32, (128, 128), 1)

    def step(ii, carry):
        values = jnp.concatenate([held_ref[s, ii] for s in range(6)], axis=0).astype(F32)
        normed = layer_norm_rows(values)
        kept = [
            (
                normed[s * 96 : s * 96 + 96]
                * (col_ref[...] * mask_ref[row_base + s * 8 + ii].astype(F32))
            ).astype(BF16)
            for s in range(6)
        ]
        piece = lambda s, kc: kept[s][kc * 32 : kc * 32 + 32]
        store = lambda row: pl.ds(pl.multiple_of(row * PITCH, 8), 128)
        blocks = [(kc, s) for kc in range(3) for s in range(4)]
        blocks += [(kc, s) for kc in range(3) for s in (4, 5, 4, 5)]
        rows = jnp.concatenate([piece(s, kc) for kc, s in blocks], axis=0)
        for n in range(6):
            if n % 2 == 0:
                pair_of = lax.dot_general(
                    sides_ref[...],
                    rows[n * 128 : n * 128 + 256],
                    (((1,), (1,)), ((), ())),
                    preferred_element_type=F32,
                )
            proj = pair_of[:, n % 2 * 128 : n % 2 * 128 + 128]
            if n < 3:
                slab_ref[store(n * 8 + ii), :] = sigmoid(proj[128:256]) * proj[0:128]
                slab_ref[store(24 + n * 8 + ii), :] = sigmoid(proj[384:512]) * proj[256:384]
            else:
                value = jnp.where(lane < 64, proj[0:128], proj[256:384])
                gating = jnp.where(lane < 64, proj[128:256], proj[384:512])
                slab_ref[store(24 + n * 8 + ii), :] = sigmoid(gating) * value
        return carry

    for q in range(4):
        loads[q].wait()
        lax.fori_loop(2 * q, 2 * q + 2, step, 0, unroll=UNROLL_PROJECT)

    def emit(ch, carry):
        wire_ref[ch] = slab_ref[pl.ds(ch, 72, stride=PITCH), :].astype(BF16)
        return carry

    stores = [
        pltpu.make_async_copy(
            wire_ref.at[32 * q : 32 * q + 32], wire_out.at[32 * q : 32 * q + 32], out_sems.at[q]
        )
        for q in range(4)
    ]
    for q in range(4):
        lax.fori_loop(32 * q, 32 * q + 32, emit, 0, unroll=4)
        stores[q].start()
    for copy in stores:
        copy.wait()


def triangle_kernel(wire_ref, perm_ref, out_ref, left_ref, right_ref, sums_ref):
    def unpack(c_pair, carry):
        groups = [(half, yl) for half in range(2) for yl in range(2)]
        source = lambda half, yl, z: wire_ref[(c_pair * 2 + half) * 8 + yl * 4 + z]
        rows = jnp.concatenate(
            [
                jnp.concatenate([source(half, yl, z) for z in range(4)], axis=1)
                for half, yl in groups
            ],
            axis=0,
        )
        swapped = jnp.dot(rows, perm_ref[...], preferred_element_type=F32)
        for n, (half, yl) in enumerate(groups):
            at = lambda k, base: swapped[
                n * 72 + base + kc * 8 : n * 72 + base + kc * 8 + 8, k * 128 : k * 128 + 128
            ]
            for kc in range(3):
                cols = pl.ds((yl * 3 + kc) * 128, 128)
                left = jnp.concatenate(
                    [at(s, 0) for s in range(4)] + [at(0, 48), at(1, 48)], axis=0
                ).astype(BF16)
                right = jnp.concatenate(
                    [at(s, 24) for s in range(4)] + [at(2, 48), at(3, 48)], axis=0
                ).astype(BF16)
                row = pl.multiple_of((c_pair * 2 + half) * 48, 16)
                left_ref[pl.ds(row, 48), cols] = left
                for g3 in range(3):
                    g = half * 3 + g3
                    base = ((c_pair // 4) * 3 + g // 2) * 128 + (c_pair % 4) * 32 + (g % 2) * 16
                    right_ref[pl.ds(pl.multiple_of(base, 16), 16), cols] = right[
                        g3 * 16 : g3 * 16 + 16
                    ]
        return carry

    lax.fori_loop(0, 8, unpack, 0, unroll=UNROLL_UNPACK)
    for n in range(3):
        sums_ref[:, n * 256 : (n + 1) * 256] = lax.dot_general(
            left_ref[...],
            right_ref[n * 256 : (n + 1) * 256, :],
            (((1,), (1,)), ((), ())),
            preferred_element_type=F32,
        )

    def pack(r, carry):
        base = pl.multiple_of(r * 48, 16)
        order = (
            [(s, 0) for s in range(4)],
            [(s, 1) for s in range(4)],
            [(s, 2) for s in range(4)],
            [(4, 0), (5, 0), (4, 1), (5, 1)],
            [(4, 2), (5, 2), (4, 2), (5, 2)],
        )
        for yl in range(2):
            tile = lambda s, jc: sums_ref[
                pl.ds(pl.multiple_of(base + s * 8, 8), 8),
                (yl * 3 + jc) * 128 : (yl * 3 + jc + 1) * 128,
            ]
            parts = [
                jnp.concatenate([tile(*entry[a]) for entry in order], axis=0) for a in range(4)
            ]
            outs = swap_blocks(parts)
            for z in range(4):
                out_ref[r * 8 + yl * 4 + z] = outs[z].astype(BF16)
        return carry

    lax.fori_loop(0, 16, pack, 0, unroll=UNROLL_PACK)


def slab_chunks(base):
    if base < 3:
        return [(s, base) for s in range(4)]
    if base == 3:
        return [(4, 0), (5, 0), (4, 1), (5, 1)]
    return [(4, 2), (5, 2)]


def gate_kernel(pair_ref, gate_w_ref, out_ref):
    gate_w = gate_w_ref[...].T
    same = lax.broadcasted_iota(jnp.int32, (128, 128), 0) == lax.broadcasted_iota(
        jnp.int32, (128, 128), 1
    )
    unit = jnp.where(same, 1.0, 0.0).astype(BF16)

    def step(ii, carry):
        held = [pair_ref[s, ii] for s in range(6)]
        values = jnp.concatenate(held, axis=0).astype(F32)
        normed = layer_norm_rows(values).astype(BF16)
        for base in range(5):
            chunks = slab_chunks(base)
            chunks = chunks + chunks[: 4 - len(chunks)]
            rows = jnp.concatenate(
                [normed[s * 96 + jc * 32 : s * 96 + jc * 32 + 32] for s, jc in chunks], axis=0
            )
            plain = jnp.concatenate(
                [held[s][jc * 32 : jc * 32 + 32] for s, jc in chunks], axis=0
            )
            contract = (((1,), (1,)), ((), ()))
            gate = lax.dot_general(gate_w, rows, contract, preferred_element_type=F32)
            out_ref[base * 8 + ii] = sigmoid(gate).astype(BF16)
            turned = lax.dot_general(unit, plain, contract, preferred_element_type=F32)
            out_ref[40 + base * 8 + ii] = turned.astype(BF16)
        return carry

    lax.fori_loop(0, 8, step, 0)


def first_kernel(
    wire_ref, sides_ref, out_w_ref, attn_w_ref, bias_w_ref, mask_ref,
    send_ref, first_ref, norm_ref, bias_ref,
):
    def add(ch, total):
        return total + wire_ref[ch].astype(F32)

    zero = jnp.zeros((40, 128), F32)
    mean = lax.fori_loop(0, 128, add, zero, unroll=8) * (1.0 / 128)

    def add_square(ch, total):
        center = wire_ref[ch].astype(F32) - mean
        return total + center * center

    spread = lax.fori_loop(0, 128, add_square, zero, unroll=8) * (1.0 / 128)
    scale = lax.rsqrt(spread + 1e-05)

    def write(ch, carry):
        norm_ref[pl.ds(pl.multiple_of(ch * 40, 8), 40), :] = (
            wire_ref[ch].astype(F32) - mean
        ) * scale
        return carry

    lax.fori_loop(0, 128, write, 0, unroll=8)
    lane = lax.broadcasted_iota(jnp.int32, (1, 128), 1)
    query_scale = jnp.where(lane < 32, LOG2E / math.sqrt(32), 1.0)
    bias_w = jnp.broadcast_to(bias_w_ref[...], (16, 128))
    out_w = out_w_ref[...].T

    def step(ii, carry):
        rows = [base * 8 + ii for base in range(5)]
        side = lambda values: jnp.concatenate(values, axis=1)
        tri = side([norm_ref[pl.ds(row, 128, stride=40), :].astype(BF16) for row in rows])
        update = jnp.dot(out_w, tri, preferred_element_type=F32)
        first = side([sides_ref[40 + row].astype(F32) for row in rows]) + (
            side([sides_ref[row].astype(F32) for row in rows]) * update
        )
        center = first - jnp.mean(first, axis=0, keepdims=True)
        spread = jnp.mean(center * center, axis=0, keepdims=True)
        normed = center * lax.rsqrt(spread + 1e-05)
        bias = jnp.dot(bias_w, normed.astype(BF16), preferred_element_type=F32)
        turned = []
        for base, row in enumerate(rows):
            cols = slice(base * 128, base * 128 + 128)
            first_ref[row] = first[:, cols].astype(BF16)
            bias_ref[pl.ds(row, 1), :] = bias[0:1, cols]
            turned.append(normed[:, cols].T)
        turned = jnp.concatenate(turned, axis=0).astype(BF16)
        proj = jnp.dot(turned, attn_w_ref[...], preferred_element_type=F32)
        proj = (proj * query_scale).astype(BF16)
        for base in range(5):
            for n, (s, jc) in enumerate(slab_chunks(base)):
                at = base * 128 + n * 32
                send_ref[ii, s * 96 + jc * 32 : s * 96 + jc * 32 + 32, :] = proj[at : at + 32]
        return carry

    lax.fori_loop(0, 8, step, 0, unroll=UNROLL_FIRST)
    bias = jnp.where(mask_ref[...] > 0, bias_ref[...] * LOG2E, -1e9 * LOG2E)
    bias = jnp.concatenate([bias, jnp.zeros((8, 128), F32)], axis=0).astype(BF16)
    for ii in range(8):
        send_ref[ii, 576:624, :] = bias


def turn_kernel(slab_ref, first_ref):
    def step(ii, carry):
        for base in range(5):
            turned = slab_ref[base * 8 + ii].T
            for n, (s, jc) in enumerate(slab_chunks(base)):
                first_ref[ii, s * 96 + jc * 32 : s * 96 + jc * 32 + 32, :] = turned[
                    n * 32 : n * 32 + 32
                ]
        return carry

    lax.fori_loop(0, 8, step, 0)


def bias_kernel(held_ref, out_ref):
    both = swap_blocks(
        [
            jnp.concatenate(
                [held_ref[yl * 4 + z, 576:624, :].astype(F32)[0:40] for yl in range(2)], axis=0
            )
            for z in range(4)
        ]
    )
    tiles = []
    for yl in range(2):
        parts = [part[yl * 40 : yl * 40 + 40] for part in both]
        tiles.append([p[0:8] for p in parts] + [parts[0][24:32], parts[1][24:32]])
        tiles.append([p[8:16] for p in parts] + [parts[2][24:32], parts[3][24:32]])
        tiles.append([p[16:24] for p in parts] + [parts[0][32:40], parts[1][32:40]])
    whole = jnp.concatenate([jnp.concatenate(t, axis=0) for t in tiles], axis=1).astype(BF16)
    for copy in range(8):
        out_ref[copy] = whole


def split_kernel(held_ref, move_ref, out_ref):
    def step(s, carry):
        rows = jnp.concatenate(
            [held_ref[c, pl.ds(pl.multiple_of(s * 96, 32), 96), :] for c in range(8)], axis=0
        )
        turned = jnp.concatenate(
            [
                held_ref[yl * 4 + z, pl.ds(pl.multiple_of(s * 96 + jc * 32, 32), 32), :]
                for yl in range(2)
                for jc in range(3)
                for z in range(4)
            ],
            axis=0,
        )
        moved = jnp.dot(turned, move_ref[:, 0:256], preferred_element_type=F32).astype(BF16)
        out_ref[s, :, 0:256] = moved
        gate = jnp.dot(rows, move_ref[:, 256:384], preferred_element_type=F32)
        out_ref[s, :, 256:384] = sigmoid(gate).astype(BF16)
        return carry

    lax.fori_loop(0, 6, step, 0)


def attend_half(half, held_ref, keyed_ref, bias_ref, extra_ref, packed_ref):
    for c in range(8):
        extra_ref[c * 48 : c * 48 + 48, :] = bias_ref[c].astype(F32)
    place = lax.broadcasted_iota(jnp.int32, (24, 128), 1) // 32 - 2 * half

    def step(s, carry):
        value = jnp.concatenate([keyed_ref[s, :, 128:256], jnp.ones((768, 128), BF16)], axis=1)
        for t in range(2):
            at = [pl.ds(pl.multiple_of(s * 96 + half * 48, 16), 48)] * 4
            rows = jnp.concatenate([held_ref[t * 4 + c, at[c], :] for c in range(4)], axis=0)
            scores = lax.dot_general(
                rows, keyed_ref[s, :, 0:128], (((1,), (1,)), ((), ())), preferred_element_type=F32
            )
            scores = scores + extra_ref[t * 192 : t * 192 + 192, :]
            top = jnp.max(scores, axis=-1, keepdims=True)
            weights = jnp.exp2(scores - top).astype(BF16)
            summed = jnp.dot(weights, value, preferred_element_type=F32)
            for h in range(4):
                c = t * 4 + h
                part = summed[h * 48 : h * 48 + 48]
                gate = keyed_ref[s, pl.ds(pl.multiple_of(c * 96 + half * 48, 16), 48), 256:384]
                gated = gate.astype(F32) * (part[:, 0:128] / part[:, 128:256])
                packed_ref[pl.ds(pl.multiple_of(c * 144 + s * 24, 8), 24), :] = jnp.where(
                    place == 0, gated[0:24], jnp.where(place == 1, gated[24:48], 0.0)
                )
        return carry

    lax.fori_loop(0, 6, step, 0, unroll=UNROLL_ATTEND)


def attend_mine_kernel(held_ref, keyed_ref, bias_ref, out_ref, extra_ref, packed_ref):
    half = lax.axis_index("core")
    attend_half(half, held_ref, keyed_ref, bias_ref, extra_ref, packed_ref)
    for c in range(8):
        out_ref[c] = packed_ref[c * 144 : (c + 1) * 144, :].astype(BF16)


def attend_other_kernel(held_ref, keyed_ref, bias_ref, mine_ref, out_ref, extra_ref, packed_ref):
    half = 1 - lax.axis_index("core")
    attend_half(half, held_ref, keyed_ref, bias_ref, extra_ref, packed_ref)
    for c in range(8):
        out_ref[c] = (
            packed_ref[c * 144 : (c + 1) * 144, :] + mine_ref[c].astype(F32)
        ).astype(BF16)


def update_kernel(held_ref, first_ref, weight_ref, out_hbm, wide_ref, done_ref, out_sems):
    def store(ii):
        return pltpu.make_async_copy(done_ref.at[:, ii], out_hbm.at[:, ii], out_sems.at[ii])

    wide_ref[...] = jnp.zeros((128, 512), BF16)
    for g in range(4):
        wide_ref[g * 32 : g * 32 + 32, g * 128 : g * 128 + 128] = weight_ref[...]

    def step(ii, carry):
        add = jnp.dot(held_ref[ii], wide_ref[...], preferred_element_type=F32)
        for s in range(6):
            rows = jnp.concatenate(
                [add[s * 24 : s * 24 + 24, g * 128 : (g + 1) * 128] for g in range(4)], axis=0
            )
            first = first_ref[ii, s * 96 : (s + 1) * 96, :].astype(F32)
            done_ref[s, ii] = (first + rows).astype(BF16)
        store(ii).start()
        return carry

    lax.fori_loop(0, 8, step, 0, unroll=UNROLL_UPDATE)
    for ii in range(8):
        store(ii).wait()


def call(kernel, outs, in_specs, out_specs, scratch, limit=LIMIT_OTHER, work=0):
    cost = pl.CostEstimate(flops=work * 10**9, bytes_accessed=work * 10**6, transcendentals=0)
    return pl.pallas_call(
        kernel,
        out_shape=outs,
        in_specs=in_specs,
        out_specs=out_specs,
        scratch_shapes=scratch,
        cost_estimate=cost if work else None,
        compiler_params=pltpu.CompilerParams(vmem_limit_bytes=limit * 1024 * 1024),
    )


def shape(dims, dtype=BF16):
    return jax.ShapeDtypeStruct(dims, dtype)


def settle(values):
    return jnp.maximum(values, jnp.asarray(-3e38, values.dtype))


def exchange(values, axes):
    return lax.all_to_all(values, axes, 0, 0, tiled=True)


def body(
    pair,
    residue_mask,
    left_weight,
    right_weight,
    gate_weight,
    out_weight,
    attn_weight,
    bias_weight,
    attn_out_weight,
):
    pair = pair.reshape(6, 8, 96, 128)
    wire = call(
        project_kernel,
        shape((128, 72, 128)),
        [HBM, pl.BlockSpec(memory_space=pltpu.SMEM), HBM, HBM],
        HBM,
        [
            pltpu.VMEM((6, 8, 96, 128), BF16),
            pltpu.VMEM((72 * PITCH, 128), F32),
            pltpu.VMEM((128, 256), BF16),
            pltpu.VMEM((128, 256), BF16),
            pltpu.VMEM((512, 128), BF16),
            pltpu.VMEM((96, 128), F32),
            pltpu.VMEM((128, 72, 128), BF16),
            pltpu.SemaphoreType.DMA((4,)),
            pltpu.SemaphoreType.DMA((2,)),
            pltpu.SemaphoreType.DMA((4,)),
        ],
        LIMIT_PROJECT,
    )(pair, residue_mask, left_weight, right_weight)
    wire = exchange(wire, ALL)
    sums = call(
        triangle_kernel,
        shape((128, 40, 128)),
        [VMEM, VMEM],
        VMEM,
        [pltpu.VMEM((768, 768), BF16), pltpu.VMEM((768, 768), BF16), pltpu.VMEM((768, 768), F32)],
    )(wire, jnp.asarray(SWAP, BF16))
    sums = exchange(sums, ALL)
    sides = call(gate_kernel, shape((80, 128, 128)), [VMEM] * 2, VMEM, [], work=3)(
        pair, gate_weight
    )
    sides = settle(sides)

    col_mask = lax.dynamic_slice_in_dim(residue_mask, lax.axis_index(COL) * 96, 96).reshape(3, 32)
    chunk = lambda jc: jnp.tile(col_mask[jc], 4)
    split = jnp.concatenate([col_mask[0], col_mask[0], col_mask[1], col_mask[1]])
    mask = jnp.repeat(jnp.stack([chunk(0), chunk(1), chunk(2), split, chunk(2)]), 8, axis=0)
    send, first = call(
        first_kernel,
        (shape((8, 624, 128)), shape((40, 128, 128))),
        [VMEM] * 6,
        (VMEM, VMEM),
        [pltpu.VMEM((128 * 40, 128), F32), pltpu.VMEM((40, 128), F32)],
    )(sums, sides, out_weight, attn_weight, bias_weight[None, :], mask)
    held = exchange(send, COL)
    first, held = lax.optimization_barrier((first, held))
    bias = call(bias_kernel, shape((8, 48, 768)), [VMEM], VMEM, [])(held)
    bias = exchange(bias, ("x", "yh"))
    other = lax.ppermute(bias, "core", [(0, 1), (1, 0)])
    keyed = call(
        split_kernel, shape((6, 768, 384)), [VMEM] * 2, VMEM, [], work=WORK_SCORE
    )(held, jnp.asarray(MOVE, BF16))
    keyed = settle(keyed)
    scratch = [pltpu.VMEM((384, 768), F32), pltpu.VMEM((8 * 144, 128), F32)]
    mine = call(
        attend_mine_kernel, shape((8, 144, 128)), [VMEM] * 3, VMEM, scratch, work=WORK_MINE
    )(held, keyed, bias)
    gated = call(
        attend_other_kernel, shape((8, 144, 128)), [VMEM] * 4, VMEM, scratch, work=2
    )(held, keyed, other, mine)
    first = call(turn_kernel, shape((8, 576, 128)), [VMEM], VMEM, [], work=2)(first)
    first = settle(first)
    gated = exchange(gated, COL)
    updated = call(
        update_kernel,
        shape((6, 8, 96, 128)),
        [VMEM, VMEM, VMEM],
        HBM,
        [
            pltpu.VMEM((128, 512), BF16),
            pltpu.VMEM((6, 8, 96, 128), BF16),
            pltpu.SemaphoreType.DMA((8,)),
        ],
        LIMIT_UPDATE,
    )(gated, first, attn_out_weight)
    return updated.reshape(48, 96, 128)


def solution(mesh):
    parts = Mesh(mesh.devices.reshape(4, 2, 2, 2, 4), ALL)
    spec = P(("x", "yh", "core"), COL, None)
    return jax.shard_map(
        body,
        mesh=parts,
        in_specs=(spec, P(), P(), P(), P(), P(), P(), P(), P()),
        out_specs=spec,
        check_vma=False,
    )
```

```python
import math

import jax
import jax.numpy as jnp
import numpy as np
from jax import lax
from jax.experimental import pallas as pl
from jax.experimental.pallas import tpu as pltpu
from jax.sharding import Mesh
from jax.sharding import PartitionSpec as P

F32 = jnp.float32
BF16 = jnp.bfloat16
LOG2E = math.log2(math.e)
PITCH = 136
UNROLL_PROJECT = 2
WORK_MINE = 30
WORK_LATE = 1
TIE_FIRST = True
TIE_GATE = True
WORK_SCORE = 100
LIMIT_OTHER = 20
LIMIT_PROJECT = 60
LIMIT_TRIANGLE = 20
LIMIT_FIRST = 20
LIMIT_UPDATE = 20
UNROLL_UNPACK = 4
UNROLL_PACK = 2
UNROLL_FIRST = 2
UNROLL_ATTEND = 6
UNROLL_UPDATE = 4
ALL = ("x", "yh", "core", "yl", "z")
COL = ("yl", "z")
VMEM = pl.BlockSpec(memory_space=pltpu.VMEM)
HBM = pl.BlockSpec(memory_space=pltpu.HBM)


def swap_matrix():
    at = np.arange(512)
    target = at % 128 // 32 * 128 + at // 128 * 32 + at % 32
    return (target[:, None] == at[None, :]).astype(np.float32)


def lanes_from(starts):
    row, lane = np.arange(128)[:, None], np.arange(128)[None, :]
    return (row == np.asarray(starts)[lane // 32] + lane % 32).astype(np.float32)


SWAP = swap_matrix()
KEY_MOVE = lanes_from([32, 64, 64, 64])
GATE_MOVE = lanes_from([96, 96, 96, 96])
SETTLE_FIRST = True


def sigmoid(values):
    return 0.5 * jnp.tanh(0.5 * values) + 0.5


def layer_norm_rows(values):
    center = values - jnp.mean(values, axis=-1, keepdims=True)
    spread = jnp.mean(center * center, axis=-1, keepdims=True)
    return center * lax.rsqrt(spread + 1e-05)


def swap_blocks(parts):
    lane = lax.broadcasted_iota(jnp.int32, parts[0].shape, 1)
    odd = jnp.bitwise_and(lane, 32) != 0
    high = lane >= 64
    v0, v1, v2, v3 = parts
    a0 = jnp.where(odd, pltpu.roll(v1, 32, 1), v0)
    a1 = jnp.where(odd, v1, pltpu.roll(v0, 96, 1))
    a2 = jnp.where(odd, pltpu.roll(v3, 32, 1), v2)
    a3 = jnp.where(odd, v3, pltpu.roll(v2, 96, 1))
    return (
        jnp.where(high, pltpu.roll(a2, 64, 1), a0),
        jnp.where(high, pltpu.roll(a3, 64, 1), a1),
        jnp.where(high, a2, pltpu.roll(a0, 64, 1)),
        jnp.where(high, a3, pltpu.roll(a1, 64, 1)),
    )


def project_kernel(
    pair_hbm, mask_ref, left_hbm, right_hbm, wire_out, held_ref, slab_ref,
    left_ref, right_ref, sides_ref, col_ref, wire_ref, sems, w_sems, out_sems,
):
    loads = [
        pltpu.make_async_copy(
            pair_hbm.at[:, 2 * q : 2 * q + 2], held_ref.at[:, 2 * q : 2 * q + 2], sems.at[q]
        )
        for q in range(4)
    ]
    weights = [
        pltpu.make_async_copy(left_hbm, left_ref, w_sems.at[0]),
        pltpu.make_async_copy(right_hbm, right_ref, w_sems.at[1]),
    ]
    for copy in weights + loads:
        copy.start()
    row_base = lax.axis_index(("x", "yh", "core")) * 48
    col_base = lax.axis_index(COL) * 96

    def mask_row(k, carry):
        col_ref[pl.ds(k, 1), :] = jnp.full((1, 128), mask_ref[col_base + k].astype(F32))
        return carry

    lax.fori_loop(0, 96, mask_row, 0, unroll=8)
    for copy in weights:
        copy.wait()
    sides_ref[0:256, :] = left_ref[...].T
    sides_ref[256:512, :] = right_ref[...].T
    lane = lax.broadcasted_iota(jnp.int32, (128, 128), 1)

    def step(ii, carry):
        values = jnp.concatenate([held_ref[s, ii] for s in range(6)], axis=0).astype(F32)
        normed = layer_norm_rows(values)
        kept = [
            (
                normed[s * 96 : s * 96 + 96]
                * (col_ref[...] * mask_ref[row_base + s * 8 + ii].astype(F32))
            ).astype(BF16)
            for s in range(6)
        ]
        piece = lambda s, kc: kept[s][kc * 32 : kc * 32 + 32]
        store = lambda row: pl.ds(pl.multiple_of(row * PITCH, 8), 128)
        blocks = [(kc, s) for kc in range(3) for s in range(4)]
        blocks += [(kc, s) for kc in range(3) for s in (4, 5, 4, 5)]
        rows = jnp.concatenate([piece(s, kc) for kc, s in blocks], axis=0)
        for n in range(6):
            if n % 2 == 0:
                pair_of = lax.dot_general(
                    sides_ref[...],
                    rows[n * 128 : n * 128 + 256],
                    (((1,), (1,)), ((), ())),
                    preferred_element_type=F32,
                )
            proj = pair_of[:, n % 2 * 128 : n % 2 * 128 + 128]
            if n < 3:
                slab_ref[store(n * 8 + ii), :] = sigmoid(proj[128:256]) * proj[0:128]
                slab_ref[store(24 + n * 8 + ii), :] = sigmoid(proj[384:512]) * proj[256:384]
            else:
                value = jnp.where(lane < 64, proj[0:128], proj[256:384])
                gating = jnp.where(lane < 64, proj[128:256], proj[384:512])
                slab_ref[store(24 + n * 8 + ii), :] = sigmoid(gating) * value
        return carry

    for q in range(4):
        loads[q].wait()
        lax.fori_loop(2 * q, 2 * q + 2, step, 0, unroll=UNROLL_PROJECT)

    def emit(ch, carry):
        wire_ref[ch] = slab_ref[pl.ds(ch, 72, stride=PITCH), :].astype(BF16)
        return carry

    stores = [
        pltpu.make_async_copy(
            wire_ref.at[32 * q : 32 * q + 32], wire_out.at[32 * q : 32 * q + 32], out_sems.at[q]
        )
        for q in range(4)
    ]
    for q in range(4):
        lax.fori_loop(32 * q, 32 * q + 32, emit, 0, unroll=4)
        stores[q].start()
    for copy in stores:
        copy.wait()


def triangle_kernel(wire_ref, perm_ref, out_ref, left_ref, right_ref, sums_ref):
    def unpack(c_pair, carry):
        groups = [(half, yl) for half in range(2) for yl in range(2)]
        source = lambda half, yl, z: wire_ref[(c_pair * 2 + half) * 8 + yl * 4 + z]
        rows = jnp.concatenate(
            [
                jnp.concatenate([source(half, yl, z) for z in range(4)], axis=1)
                for half, yl in groups
            ],
            axis=0,
        )
        swapped = jnp.dot(rows, perm_ref[...], preferred_element_type=F32)
        for n, (half, yl) in enumerate(groups):
            at = lambda k, base: swapped[
                n * 72 + base + kc * 8 : n * 72 + base + kc * 8 + 8, k * 128 : k * 128 + 128
            ]
            for kc in range(3):
                cols = pl.ds((yl * 3 + kc) * 128, 128)
                left = jnp.concatenate(
                    [at(s, 0) for s in range(4)] + [at(0, 48), at(1, 48)], axis=0
                ).astype(BF16)
                right = jnp.concatenate(
                    [at(s, 24) for s in range(4)] + [at(2, 48), at(3, 48)], axis=0
                ).astype(BF16)
                row = pl.multiple_of((c_pair * 2 + half) * 48, 16)
                left_ref[pl.ds(row, 48), cols] = left
                for g3 in range(3):
                    g = half * 3 + g3
                    base = ((c_pair // 4) * 3 + g // 2) * 128 + (c_pair % 4) * 32 + (g % 2) * 16
                    right_ref[pl.ds(pl.multiple_of(base, 16), 16), cols] = right[
                        g3 * 16 : g3 * 16 + 16
                    ]
        return carry

    lax.fori_loop(0, 8, unpack, 0, unroll=UNROLL_UNPACK)
    for n in range(3):
        sums_ref[:, n * 256 : (n + 1) * 256] = lax.dot_general(
            left_ref[...],
            right_ref[n * 256 : (n + 1) * 256, :],
            (((1,), (1,)), ((), ())),
            preferred_element_type=F32,
        )

    def pack(r, carry):
        base = pl.multiple_of(r * 48, 16)
        order = (
            [(s, 0) for s in range(4)],
            [(s, 1) for s in range(4)],
            [(s, 2) for s in range(4)],
            [(4, 0), (5, 0), (4, 1), (5, 1)],
            [(4, 2), (5, 2), (4, 2), (5, 2)],
        )
        for yl in range(2):
            tile = lambda s, jc: sums_ref[
                pl.ds(pl.multiple_of(base + s * 8, 8), 8),
                (yl * 3 + jc) * 128 : (yl * 3 + jc + 1) * 128,
            ]
            parts = [
                jnp.concatenate([tile(*entry[a]) for entry in order], axis=0) for a in range(4)
            ]
            outs = swap_blocks(parts)
            for z in range(4):
                out_ref[r * 8 + yl * 4 + z] = outs[z].astype(BF16)
        return carry

    lax.fori_loop(0, 16, pack, 0, unroll=UNROLL_PACK)


def slab_chunks(base):
    if base < 3:
        return [(s, base) for s in range(4)]
    if base == 3:
        return [(4, 0), (5, 0), (4, 1), (5, 1)]
    return [(4, 2), (5, 2)]


def gate_kernel(pair_ref, gate_w_ref, out_ref):
    gate_w = gate_w_ref[...].T

    def step(ii, carry):
        held = [pair_ref[s, ii] for s in range(6)]
        values = jnp.concatenate(held, axis=0).astype(F32)
        normed = layer_norm_rows(values).astype(BF16)
        for base in range(5):
            chunks = slab_chunks(base)
            chunks = chunks + chunks[: 4 - len(chunks)]
            rows = jnp.concatenate(
                [normed[s * 96 + jc * 32 : s * 96 + jc * 32 + 32] for s, jc in chunks], axis=0
            )
            gate = lax.dot_general(
                gate_w, rows, (((1,), (1,)), ((), ())), preferred_element_type=F32
            )
            out_ref[base * 8 + ii] = sigmoid(gate).astype(BF16)
        return carry

    lax.fori_loop(0, 8, step, 0)


def first_kernel(
    wire_ref, pair_ref, gate_ref, out_w_ref, attn_w_ref, bias_w_ref, mask_ref,
    send_ref, first_ref, norm_ref, bias_ref,
):
    def add(ch, total):
        return total + wire_ref[ch].astype(F32)

    zero = jnp.zeros((40, 128), F32)
    mean = lax.fori_loop(0, 128, add, zero, unroll=8) * (1.0 / 128)

    def add_square(ch, total):
        center = wire_ref[ch].astype(F32) - mean
        return total + center * center

    spread = lax.fori_loop(0, 128, add_square, zero, unroll=8) * (1.0 / 128)
    scale = lax.rsqrt(spread + 1e-05)

    def write(ch, carry):
        norm_ref[pl.ds(pl.multiple_of(ch * 40, 8), 40), :] = (
            wire_ref[ch].astype(F32) - mean
        ) * scale
        return carry

    lax.fori_loop(0, 128, write, 0, unroll=8)
    lane = lax.broadcasted_iota(jnp.int32, (1, 128), 1)
    query_scale = jnp.where(lane < 32, LOG2E / math.sqrt(32), 1.0)
    bias_w = jnp.broadcast_to(bias_w_ref[...], (16, 128))
    out_w = out_w_ref[...].T
    same = lax.broadcasted_iota(jnp.int32, (128, 128), 0) == lax.broadcasted_iota(
        jnp.int32, (128, 128), 1
    )
    unit = jnp.where(same, 1.0, 0.0).astype(BF16)

    def step(ii, carry):
        rows = [base * 8 + ii for base in range(5)]
        side = lambda values: jnp.concatenate(values, axis=1)
        tri = side([norm_ref[pl.ds(row, 128, stride=40), :].astype(BF16) for row in rows])
        update = jnp.dot(out_w, tri, preferred_element_type=F32)
        chunks = [chunk for base in range(5) for chunk in (slab_chunks(base) * 2)[:4]]
        plain = jnp.concatenate(
            [pair_ref[s, ii, jc * 32 : jc * 32 + 32, :] for s, jc in chunks], axis=0
        )
        pair = lax.dot_general(
            unit, plain, (((1,), (1,)), ((), ())), preferred_element_type=F32
        )
        first = pair + side([gate_ref[row].astype(F32) for row in rows]) * update
        center = first - jnp.mean(first, axis=0, keepdims=True)
        spread = jnp.mean(center * center, axis=0, keepdims=True)
        normed = center * lax.rsqrt(spread + 1e-05)
        bias = jnp.dot(bias_w, normed.astype(BF16), preferred_element_type=F32)
        turned = []
        for base, row in enumerate(rows):
            cols = slice(base * 128, base * 128 + 128)
            first_ref[row] = first[:, cols].astype(BF16)
            bias_ref[pl.ds(row, 1), :] = bias[0:1, cols]
            turned.append(normed[:, cols].T)
        turned = jnp.concatenate(turned, axis=0).astype(BF16)
        proj = jnp.dot(turned, attn_w_ref[...], preferred_element_type=F32)
        proj = (proj * query_scale).astype(BF16)
        for base in range(5):
            for n, (s, jc) in enumerate(slab_chunks(base)):
                at = base * 128 + n * 32
                send_ref[ii, s * 96 + jc * 32 : s * 96 + jc * 32 + 32, :] = proj[at : at + 32]
        return carry

    lax.fori_loop(0, 8, step, 0, unroll=UNROLL_FIRST)
    bias = jnp.where(mask_ref[...] > 0, bias_ref[...] * LOG2E, -1e9 * LOG2E)
    bias = jnp.concatenate([bias, jnp.zeros((8, 128), F32)], axis=0).astype(BF16)
    for ii in range(8):
        send_ref[ii, 576:624, :] = bias


def turn_kernel(slab_ref, attn_w_ref, move_ref, out_ref):
    gate_w = jnp.dot(attn_w_ref[...], move_ref[...], preferred_element_type=F32).astype(BF16)
    lane = lax.broadcasted_iota(jnp.int32, (24, 128), 1)

    def step(ii, carry):
        first = jnp.concatenate(
            [slab_ref[base * 8 + ii].astype(F32) for base in range(5)], axis=1
        )
        center = first - jnp.mean(first, axis=0, keepdims=True)
        spread = jnp.mean(center * center, axis=0, keepdims=True)
        normed = center * lax.rsqrt(spread + 1e-05)
        turned = jnp.concatenate(
            [normed[:, base * 128 : base * 128 + 128].T for base in range(5)], axis=0
        )
        gate = jnp.dot(turned.astype(BF16), gate_w, preferred_element_type=F32)
        place = {}
        for base in range(5):
            plain = first[:, base * 128 : base * 128 + 128].T.astype(BF16)
            for n, (s, jc) in enumerate(slab_chunks(base)):
                out_ref[ii, s * 96 + jc * 32 : s * 96 + jc * 32 + 32, :] = plain[
                    n * 32 : n * 32 + 32
                ]
                place[s, jc] = gate[base * 128 + n * 32 : base * 128 + n * 32 + 32]
        packed = []
        for s in range(6):
            whole = sigmoid(jnp.concatenate([place[s, jc] for jc in range(3)], axis=0))
            g = [whole[q * 24 : q * 24 + 24] for q in range(4)]
            low = jnp.where(lane < 32, g[0], g[1])
            high = jnp.where(lane < 96, g[2], g[3])
            packed.append(jnp.where(lane < 64, low, high))
        out_ref[ii, 576:720, :] = jnp.concatenate(packed, axis=0).astype(BF16)
        return carry

    lax.fori_loop(0, 8, step, 0)


def bias_kernel(held_ref, out_ref):
    both = swap_blocks(
        [
            jnp.concatenate(
                [held_ref[yl * 4 + z, 576:624, :].astype(F32)[0:40] for yl in range(2)], axis=0
            )
            for z in range(4)
        ]
    )
    tiles = []
    for yl in range(2):
        parts = [part[yl * 40 : yl * 40 + 40] for part in both]
        tiles.append([p[0:8] for p in parts] + [parts[0][24:32], parts[1][24:32]])
        tiles.append([p[8:16] for p in parts] + [parts[2][24:32], parts[3][24:32]])
        tiles.append([p[16:24] for p in parts] + [parts[0][32:40], parts[1][32:40]])
    whole = jnp.concatenate([jnp.concatenate(t, axis=0) for t in tiles], axis=1).astype(BF16)
    for copy in range(8):
        out_ref[copy] = whole


def split_kernel(held_ref, move_ref, out_ref):
    def step(s, carry):
        turned = jnp.concatenate(
            [
                held_ref[yl * 4 + z, pl.ds(pl.multiple_of(s * 96 + jc * 32, 32), 32), :]
                for yl in range(2)
                for jc in range(3)
                for z in range(4)
            ],
            axis=0,
        )
        out_ref[s] = jnp.dot(turned, move_ref[...], preferred_element_type=F32).astype(BF16)
        return carry

    lax.fori_loop(0, 6, step, 0)


def attend_half(half, held_ref, keyed_ref, bias_ref, extra_ref, packed_ref):
    for c in range(8):
        extra_ref[c * 48 : c * 48 + 48, :] = bias_ref[c].astype(F32)
    wide = lax.broadcasted_iota(jnp.int32, (192, 128), 1)
    lane = lax.broadcasted_iota(jnp.int32, (24, 128), 1)

    def step(s, carry):
        value = jnp.concatenate([keyed_ref[s], jnp.ones((768, 128), BF16)], axis=1)
        at = pl.ds(pl.multiple_of(s * 96 + half * 48, 16), 48)
        for t in range(2):
            rows = jnp.concatenate([held_ref[t * 4 + c, at, :] for c in range(4)], axis=0)
            query = jnp.where(wide < 32, rows, jnp.zeros_like(rows))
            scores = lax.dot_general(
                query, keyed_ref[s], (((1,), (1,)), ((), ())), preferred_element_type=F32
            )
            scores = scores + extra_ref[t * 192 : t * 192 + 192, :]
            top = jnp.max(scores, axis=-1, keepdims=True)
            weights = jnp.exp2(scores - top).astype(BF16)
            summed = jnp.dot(weights, value, preferred_element_type=F32)
            result = summed[:, 0:128] / summed[:, 128:256]
            for h in range(4):
                packed_ref[pl.ds(pl.multiple_of((t * 4 + h) * 144 + s * 24, 8), 24), :] = jnp.where(
                    lane < 96, result[h * 48 : h * 48 + 24], result[h * 48 + 24 : h * 48 + 48]
                )
        return carry

    lax.fori_loop(0, 6, step, 0, unroll=UNROLL_ATTEND)


def attend_mine_kernel(held_ref, keyed_ref, bias_ref, out_ref, extra_ref, packed_ref):
    half = lax.axis_index("core")
    attend_half(half, held_ref, keyed_ref, bias_ref, extra_ref, packed_ref)
    for c in range(8):
        out_ref[c] = packed_ref[c * 144 : (c + 1) * 144, :].astype(BF16)


def attend_other_kernel(held_ref, keyed_ref, bias_ref, mine_ref, out_ref, extra_ref, packed_ref):
    half = 1 - lax.axis_index("core")
    attend_half(half, held_ref, keyed_ref, bias_ref, extra_ref, packed_ref)
    lane = lax.broadcasted_iota(jnp.int32, (144, 128), 1)
    for c in range(8):
        mine, other = mine_ref[c].astype(F32), packed_ref[c * 144 : (c + 1) * 144, :]
        low = jnp.where(half == 0, other, mine)
        high = jnp.where(half == 0, mine, other)
        out_ref[c] = jnp.where(lane < 64, pltpu.roll(low, 64, 1), high).astype(BF16)


def update_kernel(held_ref, first_ref, weight_ref, out_hbm, wide_ref, done_ref, out_sems):
    def store(ii):
        return pltpu.make_async_copy(done_ref.at[:, ii], out_hbm.at[:, ii], out_sems.at[ii])

    wide_ref[...] = jnp.zeros((128, 512), BF16)
    for g in range(4):
        wide_ref[g * 32 : g * 32 + 32, g * 128 : g * 128 + 128] = weight_ref[...]

    def step(ii, carry):
        gated = held_ref[ii].astype(F32) * first_ref[ii, 576:720, :].astype(F32)
        add = jnp.dot(gated.astype(BF16), wide_ref[...], preferred_element_type=F32)
        for s in range(6):
            rows = jnp.concatenate(
                [add[s * 24 : s * 24 + 24, g * 128 : (g + 1) * 128] for g in range(4)], axis=0
            )
            first = first_ref[ii, s * 96 : (s + 1) * 96, :].astype(F32)
            done_ref[s, ii] = (first + rows).astype(BF16)
        store(ii).start()
        return carry

    lax.fori_loop(0, 8, step, 0, unroll=UNROLL_UPDATE)
    for ii in range(8):
        store(ii).wait()


def call(kernel, outs, in_specs, out_specs, scratch, limit=LIMIT_OTHER, work=0):
    cost = pl.CostEstimate(flops=work * 10**9, bytes_accessed=work * 10**6, transcendentals=0)
    return pl.pallas_call(
        kernel,
        out_shape=outs,
        in_specs=in_specs,
        out_specs=out_specs,
        scratch_shapes=scratch,
        cost_estimate=cost if work else None,
        compiler_params=pltpu.CompilerParams(vmem_limit_bytes=limit * 1024 * 1024),
    )


def shape(dims, dtype=BF16):
    return jax.ShapeDtypeStruct(dims, dtype)


def settle(values):
    return jnp.maximum(values, jnp.asarray(-3e38, values.dtype))


def exchange(values, axes):
    return lax.all_to_all(values, axes, 0, 0, tiled=True)


def body(
    pair,
    residue_mask,
    left_weight,
    right_weight,
    gate_weight,
    out_weight,
    attn_weight,
    bias_weight,
    attn_out_weight,
):
    pair = pair.reshape(6, 8, 96, 128)
    wire = call(
        project_kernel,
        shape((128, 72, 128)),
        [HBM, pl.BlockSpec(memory_space=pltpu.SMEM), HBM, HBM],
        HBM,
        [
            pltpu.VMEM((6, 8, 96, 128), BF16),
            pltpu.VMEM((72 * PITCH, 128), F32),
            pltpu.VMEM((128, 256), BF16),
            pltpu.VMEM((128, 256), BF16),
            pltpu.VMEM((512, 128), BF16),
            pltpu.VMEM((96, 128), F32),
            pltpu.VMEM((128, 72, 128), BF16),
            pltpu.SemaphoreType.DMA((4,)),
            pltpu.SemaphoreType.DMA((2,)),
            pltpu.SemaphoreType.DMA((4,)),
        ],
        LIMIT_PROJECT,
    )(pair, residue_mask, left_weight, right_weight)
    wire = exchange(wire, ALL)
    gate = call(gate_kernel, shape((40, 128, 128)), [VMEM] * 2, VMEM, [], work=3)(
        pair, gate_weight
    )

    col_mask = lax.dynamic_slice_in_dim(residue_mask, lax.axis_index(COL) * 96, 96).reshape(3, 32)
    chunk = lambda jc: jnp.tile(col_mask[jc], 4)
    split = jnp.concatenate([col_mask[0], col_mask[0], col_mask[1], col_mask[1]])
    mask = jnp.repeat(jnp.stack([chunk(0), chunk(1), chunk(2), split, chunk(2)]), 8, axis=0)
    if TIE_GATE:
        gate, mask, wire = lax.optimization_barrier((gate, mask, wire))
    sums = call(
        triangle_kernel,
        shape((128, 40, 128)),
        [VMEM, VMEM],
        VMEM,
        [pltpu.VMEM((768, 768), BF16), pltpu.VMEM((768, 768), BF16), pltpu.VMEM((768, 768), F32)],
    )(wire, jnp.asarray(SWAP, BF16))
    sums = exchange(sums, ALL)
    send, first = call(
        first_kernel,
        (shape((8, 624, 128)), shape((40, 128, 128))),
        [VMEM] * 7,
        (VMEM, VMEM),
        [pltpu.VMEM((128 * 40, 128), F32), pltpu.VMEM((40, 128), F32)],
    )(sums, pair, gate, out_weight, attn_weight, bias_weight[None, :], mask)
    held = exchange(send, COL)
    first, held = lax.optimization_barrier((first, held))
    bias = call(bias_kernel, shape((8, 48, 768)), [VMEM], VMEM, [])(held)
    bias = exchange(bias, ("x", "yh"))
    first = call(turn_kernel, shape((8, 720, 128)), [VMEM] * 3, VMEM, [], work=WORK_LATE)(
        first, attn_weight, jnp.asarray(GATE_MOVE, BF16)
    )
    if SETTLE_FIRST:
        first = settle(first)
    if TIE_FIRST:
        first, bias = lax.optimization_barrier((first, bias))
    other = lax.ppermute(bias, "core", [(0, 1), (1, 0)])
    keyed = call(
        split_kernel, shape((6, 768, 128)), [VMEM] * 2, VMEM, [], work=WORK_SCORE
    )(held, jnp.asarray(KEY_MOVE, BF16))
    scratch = [pltpu.VMEM((384, 768), F32), pltpu.VMEM((8 * 144, 128), F32)]
    mine = call(
        attend_mine_kernel, shape((8, 144, 128)), [VMEM] * 3, VMEM, scratch, work=WORK_MINE
    )(held, keyed, bias)
    gated = call(
        attend_other_kernel, shape((8, 144, 128)), [VMEM] * 4, VMEM, scratch, work=2
    )(held, keyed, other, mine)
    gated = exchange(gated, COL)
    updated = call(
        update_kernel,
        shape((6, 8, 96, 128)),
        [VMEM, VMEM, VMEM],
        HBM,
        [
            pltpu.VMEM((128, 512), BF16),
            pltpu.VMEM((6, 8, 96, 128), BF16),
            pltpu.SemaphoreType.DMA((8,)),
        ],
        LIMIT_UPDATE,
    )(gated, first, attn_out_weight)
    return updated.reshape(48, 96, 128)


def solution(mesh):
    parts = Mesh(mesh.devices.reshape(4, 2, 2, 2, 4), ALL)
    spec = P(("x", "yh", "core"), COL, None)
    return jax.shard_map(
        body,
        mesh=parts,
        in_specs=(spec, P(), P(), P(), P(), P(), P(), P(), P()),
        out_specs=spec,
        check_vma=False,
    )
```

```python
import math

import jax
import jax.numpy as jnp
import numpy as np
from jax import lax
from jax.experimental import pallas as pl
from jax.experimental.pallas import tpu as pltpu
from jax.sharding import Mesh
from jax.sharding import PartitionSpec as P

F32 = jnp.float32
BF16 = jnp.bfloat16
LOG2E = math.log2(math.e)
PITCH = 136
UNROLL_PROJECT = 2
WORK_MINE = 30
WORK_LATE = 1
WORK_SCORE = 100
LIMIT_OTHER = 20
LIMIT_PROJECT = 60
LIMIT_TRIANGLE = 20
LIMIT_FIRST = 20
LIMIT_UPDATE = 20
UNROLL_UNPACK = 8
UNROLL_PACK = 2
UNROLL_FIRST = 8
UNROLL_ATTEND = 6
PARTS = 2
UNROLL_UPDATE = 8
ALL = ("x", "yh", "core", "yl", "z")
COL = ("yl", "z")
VMEM = pl.BlockSpec(memory_space=pltpu.VMEM)
HBM = pl.BlockSpec(memory_space=pltpu.HBM)


def lanes_from(starts):
    row, lane = np.arange(128)[:, None], np.arange(128)[None, :]
    return (row == np.asarray(starts)[lane // 32] + lane % 32).astype(np.float32)


KEY_MOVE = lanes_from([32, 64, 64, 64])
GATE_MOVE = lanes_from([96, 96, 96, 96])


def sigmoid(values):
    return 0.5 * jnp.tanh(0.5 * values) + 0.5


def layer_norm_rows(values):
    center = values - jnp.mean(values, axis=-1, keepdims=True)
    spread = jnp.mean(center * center, axis=-1, keepdims=True)
    return center * lax.rsqrt(spread + 1e-05)


def swap_blocks(parts):
    lane = lax.broadcasted_iota(jnp.int32, parts[0].shape, 1)
    odd = jnp.bitwise_and(lane, 32) != 0
    high = lane >= 64
    v0, v1, v2, v3 = parts
    a0 = jnp.where(odd, pltpu.roll(v1, 32, 1), v0)
    a1 = jnp.where(odd, v1, pltpu.roll(v0, 96, 1))
    a2 = jnp.where(odd, pltpu.roll(v3, 32, 1), v2)
    a3 = jnp.where(odd, v3, pltpu.roll(v2, 96, 1))
    return (
        jnp.where(high, pltpu.roll(a2, 64, 1), a0),
        jnp.where(high, pltpu.roll(a3, 64, 1), a1),
        jnp.where(high, a2, pltpu.roll(a0, 64, 1)),
        jnp.where(high, a3, pltpu.roll(a1, 64, 1)),
    )


def project_kernel(
    pair_hbm, mask_ref, left_hbm, right_hbm, wire_out, held_ref, slab_ref,
    left_ref, right_ref, sides_ref, col_ref, wire_ref, sems, w_sems, out_sems,
):
    loads = [
        pltpu.make_async_copy(
            pair_hbm.at[:, 2 * q : 2 * q + 2], held_ref.at[:, 2 * q : 2 * q + 2], sems.at[q]
        )
        for q in range(4)
    ]
    weights = [
        pltpu.make_async_copy(left_hbm, left_ref, w_sems.at[0]),
        pltpu.make_async_copy(right_hbm, right_ref, w_sems.at[1]),
    ]
    for copy in weights + loads:
        copy.start()
    row_base = lax.axis_index(("x", "yh", "core")) * 48
    col_base = lax.axis_index(COL) * 96

    def mask_row(k, carry):
        col_ref[pl.ds(k, 1), :] = jnp.full((1, 128), mask_ref[col_base + k].astype(F32))
        return carry

    lax.fori_loop(0, 96, mask_row, 0, unroll=8)
    for copy in weights:
        copy.wait()
    sides_ref[0:256, :] = left_ref[...].T
    sides_ref[256:512, :] = right_ref[...].T
    lane = lax.broadcasted_iota(jnp.int32, (128, 128), 1)

    def step(ii, carry):
        values = jnp.concatenate([held_ref[s, ii] for s in range(6)], axis=0).astype(F32)
        normed = layer_norm_rows(values)
        kept = [
            (
                normed[s * 96 : s * 96 + 96]
                * (col_ref[...] * mask_ref[row_base + s * 8 + ii].astype(F32))
            ).astype(BF16)
            for s in range(6)
        ]
        piece = lambda s, kc: kept[s][kc * 32 : kc * 32 + 32]
        store = lambda row: pl.ds(pl.multiple_of(row * PITCH, 8), 128)
        blocks = [(kc, s) for kc in range(3) for s in range(4)]
        blocks += [(kc, s) for kc in range(3) for s in (4, 5, 4, 5)]
        rows = jnp.concatenate([piece(s, kc) for kc, s in blocks], axis=0)
        for n in range(6):
            if n % 2 == 0:
                pair_of = lax.dot_general(
                    sides_ref[...],
                    rows[n * 128 : n * 128 + 256],
                    (((1,), (1,)), ((), ())),
                    preferred_element_type=F32,
                )
            proj = pair_of[:, n % 2 * 128 : n % 2 * 128 + 128]
            if n < 3:
                slab_ref[store(n * 8 + ii), :] = sigmoid(proj[128:256]) * proj[0:128]
                slab_ref[store(24 + n * 8 + ii), :] = sigmoid(proj[384:512]) * proj[256:384]
            else:
                value = jnp.where(lane < 64, proj[0:128], proj[256:384])
                gating = jnp.where(lane < 64, proj[128:256], proj[384:512])
                slab_ref[store(24 + n * 8 + ii), :] = sigmoid(gating) * value
        return carry

    for q in range(4):
        loads[q].wait()
        lax.fori_loop(2 * q, 2 * q + 2, step, 0, unroll=UNROLL_PROJECT)

    def emit(ch, carry):
        wire_ref[ch] = slab_ref[pl.ds(ch, 72, stride=PITCH), :].astype(BF16)
        return carry

    stores = [
        pltpu.make_async_copy(
            wire_ref.at[32 * q : 32 * q + 32], wire_out.at[32 * q : 32 * q + 32], out_sems.at[q]
        )
        for q in range(4)
    ]
    for q in range(4):
        lax.fori_loop(32 * q, 32 * q + 32, emit, 0, unroll=4)
        stores[q].start()
    for copy in stores:
        copy.wait()


def triangle_kernel(wire_ref, out_ref, left_ref, right_ref, sums_ref, perm_ref):
    row = lax.broadcasted_iota(jnp.int32, (128, 128), 0)
    col = lax.broadcasted_iota(jnp.int32, (128, 128), 1)
    same = jnp.bitwise_and(row, 31) == jnp.bitwise_and(col, 31)
    for z in range(4):
        for b in range(4):
            hit = same & (row >= b * 32) & (row < b * 32 + 32) & (col >= z * 32) & (col < z * 32 + 32)
            perm_ref[z * 128 : z * 128 + 128, b * 128 : b * 128 + 128] = jnp.where(
                hit, 1.0, 0.0
            ).astype(BF16)

    def unpack(c_pair, carry):
        groups = [(half, yl) for half in range(2) for yl in range(2)]
        source = lambda half, yl, z: wire_ref[(c_pair * 2 + half) * 8 + yl * 4 + z]
        rows = jnp.concatenate(
            [
                jnp.concatenate([source(half, yl, z) for z in range(4)], axis=1)
                for half, yl in groups
            ],
            axis=0,
        )
        swapped = jnp.dot(rows, perm_ref[...], preferred_element_type=F32)
        for n, (half, yl) in enumerate(groups):
            at = lambda k, base: swapped[
                n * 72 + base + kc * 8 : n * 72 + base + kc * 8 + 8, k * 128 : k * 128 + 128
            ]
            for kc in range(3):
                cols = pl.ds((yl * 3 + kc) * 128, 128)
                left = jnp.concatenate(
                    [at(s, 0) for s in range(4)] + [at(0, 48), at(1, 48)], axis=0
                ).astype(BF16)
                right = jnp.concatenate(
                    [at(s, 24) for s in range(4)] + [at(2, 48), at(3, 48)], axis=0
                ).astype(BF16)
                row = pl.multiple_of((c_pair * 2 + half) * 48, 16)
                left_ref[pl.ds(row, 48), cols] = left
                for g3 in range(3):
                    g = half * 3 + g3
                    base = ((c_pair // 4) * 3 + g // 2) * 128 + (c_pair % 4) * 32 + (g % 2) * 16
                    right_ref[pl.ds(pl.multiple_of(base, 16), 16), cols] = right[
                        g3 * 16 : g3 * 16 + 16
                    ]
        return carry

    lax.fori_loop(0, 8, unpack, 0, unroll=UNROLL_UNPACK)
    for n in range(3):
        sums_ref[:, n * 256 : (n + 1) * 256] = lax.dot_general(
            left_ref[...],
            right_ref[n * 256 : (n + 1) * 256, :],
            (((1,), (1,)), ((), ())),
            preferred_element_type=F32,
        )

    def pack(r, carry):
        base = pl.multiple_of(r * 48, 16)
        order = (
            [(s, 0) for s in range(4)],
            [(s, 1) for s in range(4)],
            [(s, 2) for s in range(4)],
            [(4, 0), (5, 0), (4, 1), (5, 1)],
            [(4, 2), (5, 2), (4, 2), (5, 2)],
        )
        for yl in range(2):
            tile = lambda s, jc: sums_ref[
                pl.ds(pl.multiple_of(base + s * 8, 8), 8),
                (yl * 3 + jc) * 128 : (yl * 3 + jc + 1) * 128,
            ]
            parts = [
                jnp.concatenate([tile(*entry[a]) for entry in order], axis=0) for a in range(4)
            ]
            outs = swap_blocks(parts)
            for z in range(4):
                out_ref[r * 8 + yl * 4 + z] = outs[z].astype(BF16)
        return carry

    lax.fori_loop(0, 16, pack, 0, unroll=UNROLL_PACK)


def slab_chunks(base):
    if base < 3:
        return [(s, base) for s in range(4)]
    if base == 3:
        return [(4, 0), (5, 0), (4, 1), (5, 1)]
    return [(4, 2), (5, 2)]


def gate_kernel(pair_ref, gate_w_ref, out_ref):
    gate_w = gate_w_ref[...].T

    def step(ii, carry):
        held = [pair_ref[s, ii] for s in range(6)]
        values = jnp.concatenate(held, axis=0).astype(F32)
        normed = layer_norm_rows(values).astype(BF16)
        for base in range(5):
            chunks = slab_chunks(base)
            chunks = chunks + chunks[: 4 - len(chunks)]
            rows = jnp.concatenate(
                [normed[s * 96 + jc * 32 : s * 96 + jc * 32 + 32] for s, jc in chunks], axis=0
            )
            gate = lax.dot_general(
                gate_w, rows, (((1,), (1,)), ((), ())), preferred_element_type=F32
            )
            out_ref[base * 8 + ii] = sigmoid(gate).astype(BF16)
        return carry

    lax.fori_loop(0, 8, step, 0)


def first_kernel(
    wire_ref, pair_ref, gate_ref, out_w_ref, attn_w_ref, bias_w_ref, mask_ref,
    send_ref, first_ref, norm_ref, bias_ref,
):
    def add(ch, total):
        return total + wire_ref[ch].astype(F32)

    zero = jnp.zeros((40, 128), F32)
    mean = lax.fori_loop(0, 128, add, zero, unroll=8) * (1.0 / 128)

    def add_square(ch, total):
        center = wire_ref[ch].astype(F32) - mean
        return total + center * center

    spread = lax.fori_loop(0, 128, add_square, zero, unroll=8) * (1.0 / 128)
    scale = lax.rsqrt(spread + 1e-05)

    def write(ch, carry):
        norm_ref[pl.ds(pl.multiple_of(ch * 40, 8), 40), :] = (
            wire_ref[ch].astype(F32) - mean
        ) * scale
        return carry

    lax.fori_loop(0, 128, write, 0, unroll=8)
    lane = lax.broadcasted_iota(jnp.int32, (1, 128), 1)
    query_scale = jnp.where(lane < 32, LOG2E / math.sqrt(32), 1.0)
    bias_w = jnp.broadcast_to(bias_w_ref[...], (16, 128))
    out_w = out_w_ref[...].T
    same = lax.broadcasted_iota(jnp.int32, (128, 128), 0) == lax.broadcasted_iota(
        jnp.int32, (128, 128), 1
    )
    unit = jnp.where(same, 1.0, 0.0).astype(BF16)

    def step(ii, carry):
        rows = [base * 8 + ii for base in range(5)]
        side = lambda values: jnp.concatenate(values, axis=1)
        tri = side([norm_ref[pl.ds(row, 128, stride=40), :].astype(BF16) for row in rows])
        update = jnp.dot(out_w, tri, preferred_element_type=F32)
        chunks = [chunk for base in range(5) for chunk in (slab_chunks(base) * 2)[:4]]
        plain = jnp.concatenate(
            [pair_ref[s, ii, jc * 32 : jc * 32 + 32, :] for s, jc in chunks], axis=0
        )
        pair = lax.dot_general(
            unit, plain, (((1,), (1,)), ((), ())), preferred_element_type=F32
        )
        first = pair + side([gate_ref[row].astype(F32) for row in rows]) * update
        center = first - jnp.mean(first, axis=0, keepdims=True)
        spread = jnp.mean(center * center, axis=0, keepdims=True)
        normed = center * lax.rsqrt(spread + 1e-05)
        bias = jnp.dot(bias_w, normed.astype(BF16), preferred_element_type=F32)
        turned = []
        for base, row in enumerate(rows):
            cols = slice(base * 128, base * 128 + 128)
            first_ref[row] = first[:, cols].astype(BF16)
            bias_ref[pl.ds(row, 1), :] = bias[0:1, cols]
            turned.append(normed[:, cols].T)
        turned = jnp.concatenate(turned, axis=0).astype(BF16)
        proj = jnp.dot(turned, attn_w_ref[...], preferred_element_type=F32)
        proj = (proj * query_scale).astype(BF16)
        for base in range(5):
            for n, (s, jc) in enumerate(slab_chunks(base)):
                at = base * 128 + n * 32
                send_ref[ii, s * 96 + jc * 32 : s * 96 + jc * 32 + 32, :] = proj[at : at + 32]
        return carry

    lax.fori_loop(0, 8, step, 0, unroll=UNROLL_FIRST)
    bias = jnp.where(mask_ref[...] > 0, bias_ref[...] * LOG2E, -1e9 * LOG2E)
    bias = jnp.concatenate([bias, jnp.zeros((8, 128), F32)], axis=0)
    wide = lax.broadcasted_iota(jnp.int32, (48, 128), 1)
    for g in range(4):
        rows = slice(g * 48, g * 48 + 48)
        part = bias if g == 3 else pltpu.roll(bias, 96 - 32 * g, 1)
        for ii in range(8):
            held = send_ref[ii, rows, :].astype(F32)
            send_ref[ii, rows, :] = jnp.where(wide < 96, held, part).astype(BF16)


def turn_kernel(slab_ref, attn_w_ref, move_ref, out_ref):
    gate_w = jnp.dot(attn_w_ref[...], move_ref[...], preferred_element_type=F32).astype(BF16)
    lane = lax.broadcasted_iota(jnp.int32, (24, 128), 1)

    def step(ii, carry):
        first = jnp.concatenate(
            [slab_ref[base * 8 + ii].astype(F32) for base in range(5)], axis=1
        )
        center = first - jnp.mean(first, axis=0, keepdims=True)
        spread = jnp.mean(center * center, axis=0, keepdims=True)
        normed = center * lax.rsqrt(spread + 1e-05)
        turned = jnp.concatenate(
            [normed[:, base * 128 : base * 128 + 128].T for base in range(5)], axis=0
        )
        gate = jnp.dot(turned.astype(BF16), gate_w, preferred_element_type=F32)
        place = {}
        for base in range(5):
            plain = first[:, base * 128 : base * 128 + 128].T.astype(BF16)
            for n, (s, jc) in enumerate(slab_chunks(base)):
                out_ref[ii, s * 96 + jc * 32 : s * 96 + jc * 32 + 32, :] = plain[
                    n * 32 : n * 32 + 32
                ]
                place[s, jc] = gate[base * 128 + n * 32 : base * 128 + n * 32 + 32]
        packed = []
        for s in range(6):
            whole = sigmoid(jnp.concatenate([place[s, jc] for jc in range(3)], axis=0))
            g = [whole[q * 24 : q * 24 + 24] for q in range(4)]
            low = jnp.where(lane < 32, g[0], g[1])
            high = jnp.where(lane < 96, g[2], g[3])
            packed.append(jnp.where(lane < 64, low, high))
        out_ref[ii, 576:720, :] = jnp.concatenate(packed, axis=0).astype(BF16)
        return carry

    lax.fori_loop(0, 8, step, 0)


def bias_kernel(held_ref, out_ref):
    wide = lax.broadcasted_iota(jnp.int32, (48, 128), 1)

    def slabs(block):
        g = [held_ref[block, q * 48 : q * 48 + 48, :].astype(F32) for q in range(4)]
        g = [pltpu.roll(g[q], 32 * q + 32, 1) for q in range(3)] + [g[3]]
        low = jnp.where(wide < 32, g[0], g[1])
        return jnp.where(wide < 64, low, jnp.where(wide < 96, g[2], g[3]))[0:40]

    both = swap_blocks(
        [jnp.concatenate([slabs(yl * 4 + z) for yl in range(2)], axis=0) for z in range(4)]
    )
    tiles = []
    for yl in range(2):
        parts = [part[yl * 40 : yl * 40 + 40] for part in both]
        tiles.append([p[0:8] for p in parts] + [parts[0][24:32], parts[1][24:32]])
        tiles.append([p[8:16] for p in parts] + [parts[2][24:32], parts[3][24:32]])
        tiles.append([p[16:24] for p in parts] + [parts[0][32:40], parts[1][32:40]])
    whole = jnp.concatenate([jnp.concatenate(t, axis=0) for t in tiles], axis=1).astype(BF16)
    for copy in range(8):
        out_ref[copy] = whole


def split_kernel(held_ref, move_ref, out_ref):
    def step(s, carry):
        turned = jnp.concatenate(
            [
                held_ref[yl * 4 + z, pl.ds(pl.multiple_of(s * 96 + jc * 32, 32), 32), :]
                for yl in range(2)
                for jc in range(3)
                for z in range(4)
            ],
            axis=0,
        )
        out_ref[s] = jnp.dot(turned, move_ref[...], preferred_element_type=F32).astype(BF16)
        return carry

    lax.fori_loop(0, 6, step, 0)


def attend_half(half, held_ref, keyed_ref, bias_ref, extra_ref, packed_ref):
    for c in range(8):
        extra_ref[c * 48 : c * 48 + 48, :] = bias_ref[c].astype(F32)
    blocks = 8 // PARTS
    size = blocks * 48
    wide = lax.broadcasted_iota(jnp.int32, (size, 128), 1)
    lane = lax.broadcasted_iota(jnp.int32, (24, 128), 1)

    def step(s, carry):
        value = jnp.concatenate([keyed_ref[s], jnp.ones((768, 128), BF16)], axis=1)
        at = pl.ds(pl.multiple_of(s * 96 + half * 48, 16), 48)
        for t in range(PARTS):
            rows = jnp.concatenate(
                [held_ref[t * blocks + c, at, :] for c in range(blocks)], axis=0
            )
            query = jnp.where(wide < 32, rows, jnp.zeros_like(rows))
            scores = lax.dot_general(
                query, keyed_ref[s], (((1,), (1,)), ((), ())), preferred_element_type=F32
            )
            scores = scores + extra_ref[t * size : (t + 1) * size, :]
            top = jnp.max(scores, axis=-1, keepdims=True)
            weights = jnp.exp2(scores - top).astype(BF16)
            summed = jnp.dot(weights, value, preferred_element_type=F32)
            result = summed[:, 0:128] / summed[:, 128:256]
            for h in range(blocks):
                row = pl.multiple_of((t * blocks + h) * 144 + s * 24, 8)
                packed_ref[pl.ds(row, 24), :] = jnp.where(
                    lane < 96, result[h * 48 : h * 48 + 24], result[h * 48 + 24 : h * 48 + 48]
                )
        return carry

    lax.fori_loop(0, 6, step, 0, unroll=UNROLL_ATTEND)


def attend_mine_kernel(held_ref, keyed_ref, bias_ref, out_ref, extra_ref, packed_ref):
    half = lax.axis_index("core")
    attend_half(half, held_ref, keyed_ref, bias_ref, extra_ref, packed_ref)
    for c in range(8):
        out_ref[c] = packed_ref[c * 144 : (c + 1) * 144, :].astype(BF16)


def attend_other_kernel(held_ref, keyed_ref, bias_ref, mine_ref, out_ref, extra_ref, packed_ref):
    half = 1 - lax.axis_index("core")
    attend_half(half, held_ref, keyed_ref, bias_ref, extra_ref, packed_ref)
    lane = lax.broadcasted_iota(jnp.int32, (144, 128), 1)
    for c in range(8):
        mine, other = mine_ref[c].astype(F32), packed_ref[c * 144 : (c + 1) * 144, :]
        low = jnp.where(half == 0, other, mine)
        high = jnp.where(half == 0, mine, other)
        out_ref[c] = jnp.where(lane < 64, pltpu.roll(low, 64, 1), high).astype(BF16)


def update_kernel(held_ref, first_ref, weight_ref, out_hbm, wide_ref, done_ref, out_sems):
    def store(ii):
        return pltpu.make_async_copy(done_ref.at[:, ii], out_hbm.at[:, ii], out_sems.at[ii])

    wide_ref[...] = jnp.zeros((128, 512), BF16)
    for g in range(4):
        wide_ref[g * 32 : g * 32 + 32, g * 128 : g * 128 + 128] = weight_ref[...]

    def step(ii, carry):
        gated = held_ref[ii].astype(F32) * first_ref[ii, 576:720, :].astype(F32)
        add = jnp.dot(gated.astype(BF16), wide_ref[...], preferred_element_type=F32)
        for s in range(6):
            rows = jnp.concatenate(
                [add[s * 24 : s * 24 + 24, g * 128 : (g + 1) * 128] for g in range(4)], axis=0
            )
            first = first_ref[ii, s * 96 : (s + 1) * 96, :].astype(F32)
            done_ref[s, ii] = (first + rows).astype(BF16)
        store(ii).start()
        return carry

    lax.fori_loop(0, 8, step, 0, unroll=UNROLL_UPDATE)
    for ii in range(8):
        store(ii).wait()


def call(kernel, outs, in_specs, out_specs, scratch, limit=LIMIT_OTHER, work=0):
    cost = pl.CostEstimate(flops=work * 10**9, bytes_accessed=work * 10**6, transcendentals=0)
    return pl.pallas_call(
        kernel,
        out_shape=outs,
        in_specs=in_specs,
        out_specs=out_specs,
        scratch_shapes=scratch,
        cost_estimate=cost if work else None,
        compiler_params=pltpu.CompilerParams(vmem_limit_bytes=limit * 1024 * 1024),
    )


def shape(dims, dtype=BF16):
    return jax.ShapeDtypeStruct(dims, dtype)


def exchange(values, axes):
    return lax.all_to_all(values, axes, 0, 0, tiled=True)


def body(
    pair,
    residue_mask,
    left_weight,
    right_weight,
    gate_weight,
    out_weight,
    attn_weight,
    bias_weight,
    attn_out_weight,
):
    pair = pair.reshape(6, 8, 96, 128)
    wire = call(
        project_kernel,
        shape((128, 72, 128)),
        [HBM, pl.BlockSpec(memory_space=pltpu.SMEM), HBM, HBM],
        HBM,
        [
            pltpu.VMEM((6, 8, 96, 128), BF16),
            pltpu.VMEM((72 * PITCH, 128), F32),
            pltpu.VMEM((128, 256), BF16),
            pltpu.VMEM((128, 256), BF16),
            pltpu.VMEM((512, 128), BF16),
            pltpu.VMEM((96, 128), F32),
            pltpu.VMEM((128, 72, 128), BF16),
            pltpu.SemaphoreType.DMA((4,)),
            pltpu.SemaphoreType.DMA((2,)),
            pltpu.SemaphoreType.DMA((4,)),
        ],
        LIMIT_PROJECT,
    )(pair, residue_mask, left_weight, right_weight)
    wire = exchange(wire, ALL)
    gate = call(gate_kernel, shape((40, 128, 128)), [VMEM] * 2, VMEM, [], work=3)(
        pair, gate_weight
    )

    col_mask = lax.dynamic_slice_in_dim(residue_mask, lax.axis_index(COL) * 96, 96).reshape(3, 32)
    chunk = lambda jc: jnp.tile(col_mask[jc], 4)
    split = jnp.concatenate([col_mask[0], col_mask[0], col_mask[1], col_mask[1]])
    mask = jnp.repeat(jnp.stack([chunk(0), chunk(1), chunk(2), split, chunk(2)]), 8, axis=0)
    gate, mask, wire = lax.optimization_barrier((gate, mask, wire))
    sums = call(
        triangle_kernel,
        shape((128, 40, 128)),
        [VMEM],
        VMEM,
        [
            pltpu.VMEM((768, 768), BF16),
            pltpu.VMEM((768, 768), BF16),
            pltpu.VMEM((768, 768), F32),
            pltpu.VMEM((512, 512), BF16),
        ],
    )(wire)
    sums = exchange(sums, ALL)
    send, first = call(
        first_kernel,
        (shape((8, 576, 128)), shape((40, 128, 128))),
        [VMEM] * 7,
        (VMEM, VMEM),
        [pltpu.VMEM((128 * 40, 128), F32), pltpu.VMEM((40, 128), F32)],
    )(sums, pair, gate, out_weight, attn_weight, bias_weight[None, :], mask)
    held = exchange(send, COL)
    first, held = lax.optimization_barrier((first, held))
    bias = call(bias_kernel, shape((8, 48, 768)), [VMEM], VMEM, [])(held)
    bias = exchange(bias, ("x", "yh"))
    first = call(turn_kernel, shape((8, 720, 128)), [VMEM] * 3, VMEM, [], work=WORK_LATE)(
        first, attn_weight, jnp.asarray(GATE_MOVE, BF16)
    )
    first, bias = lax.optimization_barrier((first, bias))
    other = lax.ppermute(bias, "core", [(0, 1), (1, 0)])
    keyed = call(
        split_kernel, shape((6, 768, 128)), [VMEM] * 2, VMEM, [], work=WORK_SCORE
    )(held, jnp.asarray(KEY_MOVE, BF16))
    scratch = [pltpu.VMEM((384, 768), F32), pltpu.VMEM((8 * 144, 128), F32)]
    mine = call(
        attend_mine_kernel, shape((8, 144, 128)), [VMEM] * 3, VMEM, scratch, work=WORK_MINE
    )(held, keyed, bias)
    gated = call(
        attend_other_kernel, shape((8, 144, 128)), [VMEM] * 4, VMEM, scratch, work=2
    )(held, keyed, other, mine)
    gated = exchange(gated, COL)
    updated = call(
        update_kernel,
        shape((6, 8, 96, 128)),
        [VMEM, VMEM, VMEM],
        HBM,
        [
            pltpu.VMEM((128, 512), BF16),
            pltpu.VMEM((6, 8, 96, 128), BF16),
            pltpu.SemaphoreType.DMA((8,)),
        ],
        LIMIT_UPDATE,
    )(gated, first, attn_out_weight)
    return updated.reshape(48, 96, 128)


def solution(mesh):
    parts = Mesh(mesh.devices.reshape(4, 2, 2, 2, 4), ALL)
    spec = P(("x", "yh", "core"), COL, None)
    return jax.shard_map(
        body,
        mesh=parts,
        in_specs=(spec, P(), P(), P(), P(), P(), P(), P(), P()),
        out_specs=spec,
        check_vma=False,
    )
```

```python
import math

import jax
import jax.numpy as jnp
import numpy as np
from jax import lax
from jax.experimental import pallas as pl
from jax.experimental.pallas import tpu as pltpu
from jax.sharding import Mesh
from jax.sharding import PartitionSpec as P

F32 = jnp.float32
BF16 = jnp.bfloat16
LOG2E = math.log2(math.e)
PITCH = 136
UNROLL_PROJECT = 8
UNROLL_EMIT = 8
LOADS = 1
STORES = 8
WORK_MINE = 30
WORK_LATE = 1
WORK_SCORE = 100
LIMIT_OTHER = 20
LIMIT_PROJECT = 60
LIMIT_TRIANGLE = 20
LIMIT_FIRST = 20
LIMIT_UPDATE = 20
UNROLL_UNPACK = 8
UNROLL_PACK = 2
UNROLL_FIRST = 8
UNROLL_ATTEND = 6
PARTS = 2
UNROLL_UPDATE = 8
ALL = ("x", "yh", "core", "yl", "z")
COL = ("yl", "z")
VMEM = pl.BlockSpec(memory_space=pltpu.VMEM)
HBM = pl.BlockSpec(memory_space=pltpu.HBM)


def lanes_from(starts):
    row, lane = np.arange(128)[:, None], np.arange(128)[None, :]
    return (row == np.asarray(starts)[lane // 32] + lane % 32).astype(np.float32)


KEY_MOVE = lanes_from([32, 64, 64, 64])
GATE_MOVE = lanes_from([96, 96, 96, 96])


def sigmoid(values):
    return 0.5 * jnp.tanh(0.5 * values) + 0.5


def layer_norm_rows(values):
    center = values - jnp.mean(values, axis=-1, keepdims=True)
    spread = jnp.mean(center * center, axis=-1, keepdims=True)
    return center * lax.rsqrt(spread + 1e-05)


def swap_blocks(parts):
    lane = lax.broadcasted_iota(jnp.int32, parts[0].shape, 1)
    odd = jnp.bitwise_and(lane, 32) != 0
    high = lane >= 64
    v0, v1, v2, v3 = parts
    a0 = jnp.where(odd, pltpu.roll(v1, 32, 1), v0)
    a1 = jnp.where(odd, v1, pltpu.roll(v0, 96, 1))
    a2 = jnp.where(odd, pltpu.roll(v3, 32, 1), v2)
    a3 = jnp.where(odd, v3, pltpu.roll(v2, 96, 1))
    return (
        jnp.where(high, pltpu.roll(a2, 64, 1), a0),
        jnp.where(high, pltpu.roll(a3, 64, 1), a1),
        jnp.where(high, a2, pltpu.roll(a0, 64, 1)),
        jnp.where(high, a3, pltpu.roll(a1, 64, 1)),
    )


def project_kernel(
    pair_hbm, mask_ref, left_hbm, right_hbm, wire_out, held_ref, slab_ref,
    left_ref, right_ref, sides_ref, col_ref, wire_ref, sems, w_sems, out_sems,
):
    step_rows, step_channels = 8 // LOADS, 128 // STORES
    loads = []
    for q in range(LOADS):
        part = slice(step_rows * q, step_rows * q + step_rows)
        loads.append(
            pltpu.make_async_copy(pair_hbm.at[:, part], held_ref.at[:, part], sems.at[q])
        )
    weights = [
        pltpu.make_async_copy(left_hbm, left_ref, w_sems.at[0]),
        pltpu.make_async_copy(right_hbm, right_ref, w_sems.at[1]),
    ]
    for copy in weights + loads:
        copy.start()
    row_base = lax.axis_index(("x", "yh", "core")) * 48
    col_base = lax.axis_index(COL) * 96

    def mask_row(k, carry):
        col_ref[pl.ds(k, 1), :] = jnp.full((1, 128), mask_ref[col_base + k].astype(F32))
        return carry

    lax.fori_loop(0, 96, mask_row, 0, unroll=8)
    for copy in weights:
        copy.wait()
    sides_ref[0:256, :] = left_ref[...].T
    sides_ref[256:512, :] = right_ref[...].T
    lane = lax.broadcasted_iota(jnp.int32, (128, 128), 1)

    def step(ii, carry):
        values = jnp.concatenate([held_ref[s, ii] for s in range(6)], axis=0).astype(F32)
        normed = layer_norm_rows(values)
        kept = [
            (
                normed[s * 96 : s * 96 + 96]
                * (col_ref[...] * mask_ref[row_base + s * 8 + ii].astype(F32))
            ).astype(BF16)
            for s in range(6)
        ]
        piece = lambda s, kc: kept[s][kc * 32 : kc * 32 + 32]
        store = lambda row: pl.ds(pl.multiple_of(row * PITCH, 8), 128)
        blocks = [(kc, s) for kc in range(3) for s in range(4)]
        blocks += [(kc, s) for kc in range(3) for s in (4, 5, 4, 5)]
        rows = jnp.concatenate([piece(s, kc) for kc, s in blocks], axis=0)
        for n in range(6):
            if n % 2 == 0:
                pair_of = lax.dot_general(
                    sides_ref[...],
                    rows[n * 128 : n * 128 + 256],
                    (((1,), (1,)), ((), ())),
                    preferred_element_type=F32,
                )
            proj = pair_of[:, n % 2 * 128 : n % 2 * 128 + 128]
            if n < 3:
                slab_ref[store(n * 8 + ii), :] = sigmoid(proj[128:256]) * proj[0:128]
                slab_ref[store(24 + n * 8 + ii), :] = sigmoid(proj[384:512]) * proj[256:384]
            else:
                value = jnp.where(lane < 64, proj[0:128], proj[256:384])
                gating = jnp.where(lane < 64, proj[128:256], proj[384:512])
                slab_ref[store(24 + n * 8 + ii), :] = sigmoid(gating) * value
        return carry

    for q in range(LOADS):
        loads[q].wait()
        lax.fori_loop(
            step_rows * q, step_rows * q + step_rows, step, 0, unroll=UNROLL_PROJECT
        )

    def emit(ch, carry):
        wire_ref[ch] = slab_ref[pl.ds(ch, 72, stride=PITCH), :].astype(BF16)
        return carry

    stores = []
    for q in range(STORES):
        part = slice(step_channels * q, step_channels * q + step_channels)
        stores.append(
            pltpu.make_async_copy(wire_ref.at[part], wire_out.at[part], out_sems.at[q])
        )
    for q in range(STORES):
        lax.fori_loop(
            step_channels * q, step_channels * q + step_channels, emit, 0, unroll=UNROLL_EMIT
        )
        stores[q].start()
    for copy in stores:
        copy.wait()


def triangle_kernel(wire_ref, out_ref, left_ref, right_ref, sums_ref, perm_ref):
    row = lax.broadcasted_iota(jnp.int32, (128, 128), 0)
    col = lax.broadcasted_iota(jnp.int32, (128, 128), 1)
    same = jnp.bitwise_and(row, 31) == jnp.bitwise_and(col, 31)
    for z in range(4):
        for b in range(4):
            hit = same & (row >= b * 32) & (row < b * 32 + 32) & (col >= z * 32) & (col < z * 32 + 32)
            perm_ref[z * 128 : z * 128 + 128, b * 128 : b * 128 + 128] = jnp.where(
                hit, 1.0, 0.0
            ).astype(BF16)

    def unpack(c_pair, carry):
        groups = [(half, yl) for half in range(2) for yl in range(2)]
        source = lambda half, yl, z: wire_ref[(c_pair * 2 + half) * 8 + yl * 4 + z]
        rows = jnp.concatenate(
            [
                jnp.concatenate([source(half, yl, z) for z in range(4)], axis=1)
                for half, yl in groups
            ],
            axis=0,
        )
        swapped = jnp.dot(rows, perm_ref[...], preferred_element_type=F32)
        for n, (half, yl) in enumerate(groups):
            at = lambda k, base: swapped[
                n * 72 + base + kc * 8 : n * 72 + base + kc * 8 + 8, k * 128 : k * 128 + 128
            ]
            for kc in range(3):
                cols = pl.ds((yl * 3 + kc) * 128, 128)
                left = jnp.concatenate(
                    [at(s, 0) for s in range(4)] + [at(0, 48), at(1, 48)], axis=0
                ).astype(BF16)
                right = jnp.concatenate(
                    [at(s, 24) for s in range(4)] + [at(2, 48), at(3, 48)], axis=0
                ).astype(BF16)
                row = pl.multiple_of((c_pair * 2 + half) * 48, 16)
                left_ref[pl.ds(row, 48), cols] = left
                for g3 in range(3):
                    g = half * 3 + g3
                    base = ((c_pair // 4) * 3 + g // 2) * 128 + (c_pair % 4) * 32 + (g % 2) * 16
                    right_ref[pl.ds(pl.multiple_of(base, 16), 16), cols] = right[
                        g3 * 16 : g3 * 16 + 16
                    ]
        return carry

    lax.fori_loop(0, 8, unpack, 0, unroll=UNROLL_UNPACK)
    for n in range(3):
        sums_ref[:, n * 256 : (n + 1) * 256] = lax.dot_general(
            left_ref[...],
            right_ref[n * 256 : (n + 1) * 256, :],
            (((1,), (1,)), ((), ())),
            preferred_element_type=F32,
        )

    def pack(r, carry):
        base = pl.multiple_of(r * 48, 16)
        order = (
            [(s, 0) for s in range(4)],
            [(s, 1) for s in range(4)],
            [(s, 2) for s in range(4)],
            [(4, 0), (5, 0), (4, 1), (5, 1)],
            [(4, 2), (5, 2), (4, 2), (5, 2)],
        )
        for yl in range(2):
            tile = lambda s, jc: sums_ref[
                pl.ds(pl.multiple_of(base + s * 8, 8), 8),
                (yl * 3 + jc) * 128 : (yl * 3 + jc + 1) * 128,
            ]
            parts = [
                jnp.concatenate([tile(*entry[a]) for entry in order], axis=0) for a in range(4)
            ]
            outs = swap_blocks(parts)
            for z in range(4):
                out_ref[r * 8 + yl * 4 + z] = outs[z].astype(BF16)
        return carry

    lax.fori_loop(0, 16, pack, 0, unroll=UNROLL_PACK)


def slab_chunks(base):
    if base < 3:
        return [(s, base) for s in range(4)]
    if base == 3:
        return [(4, 0), (5, 0), (4, 1), (5, 1)]
    return [(4, 2), (5, 2)]


def gate_kernel(pair_ref, gate_w_ref, out_ref):
    gate_w = gate_w_ref[...].T

    def step(ii, carry):
        held = [pair_ref[s, ii] for s in range(6)]
        values = jnp.concatenate(held, axis=0).astype(F32)
        normed = layer_norm_rows(values).astype(BF16)
        for base in range(5):
            chunks = slab_chunks(base)
            chunks = chunks + chunks[: 4 - len(chunks)]
            rows = jnp.concatenate(
                [normed[s * 96 + jc * 32 : s * 96 + jc * 32 + 32] for s, jc in chunks], axis=0
            )
            gate = lax.dot_general(
                gate_w, rows, (((1,), (1,)), ((), ())), preferred_element_type=F32
            )
            out_ref[base * 8 + ii] = sigmoid(gate).astype(BF16)
        return carry

    lax.fori_loop(0, 8, step, 0)


def first_kernel(
    wire_ref, pair_ref, gate_ref, out_w_ref, attn_w_ref, bias_w_ref, mask_ref,
    send_ref, first_ref, norm_ref, bias_ref,
):
    def add(ch, total):
        return total + wire_ref[ch].astype(F32)

    zero = jnp.zeros((40, 128), F32)
    mean = lax.fori_loop(0, 128, add, zero, unroll=8) * (1.0 / 128)

    def add_square(ch, total):
        center = wire_ref[ch].astype(F32) - mean
        return total + center * center

    spread = lax.fori_loop(0, 128, add_square, zero, unroll=8) * (1.0 / 128)
    scale = lax.rsqrt(spread + 1e-05)

    def write(ch, carry):
        norm_ref[pl.ds(pl.multiple_of(ch * 40, 8), 40), :] = (
            wire_ref[ch].astype(F32) - mean
        ) * scale
        return carry

    lax.fori_loop(0, 128, write, 0, unroll=8)
    lane = lax.broadcasted_iota(jnp.int32, (1, 128), 1)
    query_scale = jnp.where(lane < 32, LOG2E / math.sqrt(32), 1.0)
    bias_w = jnp.broadcast_to(bias_w_ref[...], (16, 128))
    out_w = out_w_ref[...].T
    same = lax.broadcasted_iota(jnp.int32, (128, 128), 0) == lax.broadcasted_iota(
        jnp.int32, (128, 128), 1
    )
    unit = jnp.where(same, 1.0, 0.0).astype(BF16)

    def step(ii, carry):
        rows = [base * 8 + ii for base in range(5)]
        side = lambda values: jnp.concatenate(values, axis=1)
        tri = side([norm_ref[pl.ds(row, 128, stride=40), :].astype(BF16) for row in rows])
        update = jnp.dot(out_w, tri, preferred_element_type=F32)
        chunks = [chunk for base in range(5) for chunk in (slab_chunks(base) * 2)[:4]]
        plain = jnp.concatenate(
            [pair_ref[s, ii, jc * 32 : jc * 32 + 32, :] for s, jc in chunks], axis=0
        )
        pair = lax.dot_general(
            unit, plain, (((1,), (1,)), ((), ())), preferred_element_type=F32
        )
        first = pair + side([gate_ref[row].astype(F32) for row in rows]) * update
        center = first - jnp.mean(first, axis=0, keepdims=True)
        spread = jnp.mean(center * center, axis=0, keepdims=True)
        normed = center * lax.rsqrt(spread + 1e-05)
        bias = jnp.dot(bias_w, normed.astype(BF16), preferred_element_type=F32)
        turned = []
        for base, row in enumerate(rows):
            cols = slice(base * 128, base * 128 + 128)
            first_ref[row] = first[:, cols].astype(BF16)
            bias_ref[pl.ds(row, 1), :] = bias[0:1, cols]
            turned.append(normed[:, cols].T)
        turned = jnp.concatenate(turned, axis=0).astype(BF16)
        proj = jnp.dot(turned, attn_w_ref[...], preferred_element_type=F32)
        proj = (proj * query_scale).astype(BF16)
        for base in range(5):
            for n, (s, jc) in enumerate(slab_chunks(base)):
                at = base * 128 + n * 32
                send_ref[ii, s * 96 + jc * 32 : s * 96 + jc * 32 + 32, :] = proj[at : at + 32]
        return carry

    lax.fori_loop(0, 8, step, 0, unroll=UNROLL_FIRST)
    bias = jnp.where(mask_ref[...] > 0, bias_ref[...] * LOG2E, -1e9 * LOG2E)
    bias = jnp.concatenate([bias, jnp.zeros((8, 128), F32)], axis=0)
    wide = lax.broadcasted_iota(jnp.int32, (48, 128), 1)
    for g in range(4):
        rows = slice(g * 48, g * 48 + 48)
        part = bias if g == 3 else pltpu.roll(bias, 96 - 32 * g, 1)
        for ii in range(8):
            held = send_ref[ii, rows, :].astype(F32)
            send_ref[ii, rows, :] = jnp.where(wide < 96, held, part).astype(BF16)


def turn_kernel(slab_ref, attn_w_ref, move_ref, out_ref):
    gate_w = jnp.dot(attn_w_ref[...], move_ref[...], preferred_element_type=F32).astype(BF16)
    lane = lax.broadcasted_iota(jnp.int32, (24, 128), 1)

    def step(ii, carry):
        first = jnp.concatenate(
            [slab_ref[base * 8 + ii].astype(F32) for base in range(5)], axis=1
        )
        center = first - jnp.mean(first, axis=0, keepdims=True)
        spread = jnp.mean(center * center, axis=0, keepdims=True)
        normed = center * lax.rsqrt(spread + 1e-05)
        turned = jnp.concatenate(
            [normed[:, base * 128 : base * 128 + 128].T for base in range(5)], axis=0
        )
        gate = jnp.dot(turned.astype(BF16), gate_w, preferred_element_type=F32)
        place = {}
        for base in range(5):
            plain = first[:, base * 128 : base * 128 + 128].T.astype(BF16)
            for n, (s, jc) in enumerate(slab_chunks(base)):
                out_ref[ii, s * 96 + jc * 32 : s * 96 + jc * 32 + 32, :] = plain[
                    n * 32 : n * 32 + 32
                ]
                place[s, jc] = gate[base * 128 + n * 32 : base * 128 + n * 32 + 32]
        packed = []
        for s in range(6):
            whole = sigmoid(jnp.concatenate([place[s, jc] for jc in range(3)], axis=0))
            g = [whole[q * 24 : q * 24 + 24] for q in range(4)]
            low = jnp.where(lane < 32, g[0], g[1])
            high = jnp.where(lane < 96, g[2], g[3])
            packed.append(jnp.where(lane < 64, low, high))
        out_ref[ii, 576:720, :] = jnp.concatenate(packed, axis=0).astype(BF16)
        return carry

    lax.fori_loop(0, 8, step, 0)


def bias_kernel(held_ref, out_ref):
    wide = lax.broadcasted_iota(jnp.int32, (48, 128), 1)

    def slabs(block):
        g = [held_ref[block, q * 48 : q * 48 + 48, :].astype(F32) for q in range(4)]
        g = [pltpu.roll(g[q], 32 * q + 32, 1) for q in range(3)] + [g[3]]
        low = jnp.where(wide < 32, g[0], g[1])
        return jnp.where(wide < 64, low, jnp.where(wide < 96, g[2], g[3]))[0:40]

    both = swap_blocks(
        [jnp.concatenate([slabs(yl * 4 + z) for yl in range(2)], axis=0) for z in range(4)]
    )
    tiles = []
    for yl in range(2):
        parts = [part[yl * 40 : yl * 40 + 40] for part in both]
        tiles.append([p[0:8] for p in parts] + [parts[0][24:32], parts[1][24:32]])
        tiles.append([p[8:16] for p in parts] + [parts[2][24:32], parts[3][24:32]])
        tiles.append([p[16:24] for p in parts] + [parts[0][32:40], parts[1][32:40]])
    whole = jnp.concatenate([jnp.concatenate(t, axis=0) for t in tiles], axis=1).astype(BF16)
    for copy in range(8):
        out_ref[copy] = whole


def split_kernel(held_ref, move_ref, out_ref):
    def step(s, carry):
        turned = jnp.concatenate(
            [
                held_ref[yl * 4 + z, pl.ds(pl.multiple_of(s * 96 + jc * 32, 32), 32), :]
                for yl in range(2)
                for jc in range(3)
                for z in range(4)
            ],
            axis=0,
        )
        out_ref[s] = jnp.dot(turned, move_ref[...], preferred_element_type=F32).astype(BF16)
        return carry

    lax.fori_loop(0, 6, step, 0)


def attend_half(half, held_ref, keyed_ref, bias_ref, extra_ref, packed_ref):
    for c in range(8):
        extra_ref[c * 48 : c * 48 + 48, :] = bias_ref[c].astype(F32)
    blocks = 8 // PARTS
    size = blocks * 48
    wide = lax.broadcasted_iota(jnp.int32, (size, 128), 1)
    lane = lax.broadcasted_iota(jnp.int32, (24, 128), 1)

    def step(s, carry):
        value = jnp.concatenate([keyed_ref[s], jnp.ones((768, 128), BF16)], axis=1)
        at = pl.ds(pl.multiple_of(s * 96 + half * 48, 16), 48)
        for t in range(PARTS):
            rows = jnp.concatenate(
                [held_ref[t * blocks + c, at, :] for c in range(blocks)], axis=0
            )
            query = jnp.where(wide < 32, rows, jnp.zeros_like(rows))
            scores = lax.dot_general(
                query, keyed_ref[s], (((1,), (1,)), ((), ())), preferred_element_type=F32
            )
            scores = scores + extra_ref[t * size : (t + 1) * size, :]
            top = jnp.max(scores, axis=-1, keepdims=True)
            weights = jnp.exp2(scores - top).astype(BF16)
            summed = jnp.dot(weights, value, preferred_element_type=F32)
            result = summed[:, 0:128] / summed[:, 128:256]
            for h in range(blocks):
                row = pl.multiple_of((t * blocks + h) * 144 + s * 24, 8)
                packed_ref[pl.ds(row, 24), :] = jnp.where(
                    lane < 96, result[h * 48 : h * 48 + 24], result[h * 48 + 24 : h * 48 + 48]
                )
        return carry

    lax.fori_loop(0, 6, step, 0, unroll=UNROLL_ATTEND)


def attend_mine_kernel(held_ref, keyed_ref, bias_ref, out_ref, extra_ref, packed_ref):
    half = lax.axis_index("core")
    attend_half(half, held_ref, keyed_ref, bias_ref, extra_ref, packed_ref)
    for c in range(8):
        out_ref[c] = packed_ref[c * 144 : (c + 1) * 144, :].astype(BF16)


def attend_other_kernel(held_ref, keyed_ref, bias_ref, mine_ref, out_ref, extra_ref, packed_ref):
    half = 1 - lax.axis_index("core")
    attend_half(half, held_ref, keyed_ref, bias_ref, extra_ref, packed_ref)
    lane = lax.broadcasted_iota(jnp.int32, (144, 128), 1)
    for c in range(8):
        mine, other = mine_ref[c].astype(F32), packed_ref[c * 144 : (c + 1) * 144, :]
        low = jnp.where(half == 0, other, mine)
        high = jnp.where(half == 0, mine, other)
        out_ref[c] = jnp.where(lane < 64, pltpu.roll(low, 64, 1), high).astype(BF16)


def update_kernel(held_ref, first_ref, weight_ref, out_hbm, wide_ref, done_ref, out_sems):
    def store(ii):
        return pltpu.make_async_copy(done_ref.at[:, ii], out_hbm.at[:, ii], out_sems.at[ii])

    wide_ref[...] = jnp.zeros((128, 512), BF16)
    for g in range(4):
        wide_ref[g * 32 : g * 32 + 32, g * 128 : g * 128 + 128] = weight_ref[...]

    def step(ii, carry):
        gated = held_ref[ii].astype(F32) * first_ref[ii, 576:720, :].astype(F32)
        add = jnp.dot(gated.astype(BF16), wide_ref[...], preferred_element_type=F32)
        for s in range(6):
            rows = jnp.concatenate(
                [add[s * 24 : s * 24 + 24, g * 128 : (g + 1) * 128] for g in range(4)], axis=0
            )
            first = first_ref[ii, s * 96 : (s + 1) * 96, :].astype(F32)
            done_ref[s, ii] = (first + rows).astype(BF16)
        store(ii).start()
        return carry

    lax.fori_loop(0, 8, step, 0, unroll=UNROLL_UPDATE)
    for ii in range(8):
        store(ii).wait()


def call(kernel, outs, in_specs, out_specs, scratch, limit=LIMIT_OTHER, work=0):
    cost = pl.CostEstimate(flops=work * 10**9, bytes_accessed=work * 10**6, transcendentals=0)
    return pl.pallas_call(
        kernel,
        out_shape=outs,
        in_specs=in_specs,
        out_specs=out_specs,
        scratch_shapes=scratch,
        cost_estimate=cost if work else None,
        compiler_params=pltpu.CompilerParams(vmem_limit_bytes=limit * 1024 * 1024),
    )


def shape(dims, dtype=BF16):
    return jax.ShapeDtypeStruct(dims, dtype)


def exchange(values, axes):
    return lax.all_to_all(values, axes, 0, 0, tiled=True)


def body(
    pair,
    residue_mask,
    left_weight,
    right_weight,
    gate_weight,
    out_weight,
    attn_weight,
    bias_weight,
    attn_out_weight,
):
    pair = pair.reshape(6, 8, 96, 128)
    wire = call(
        project_kernel,
        shape((128, 72, 128)),
        [HBM, pl.BlockSpec(memory_space=pltpu.SMEM), HBM, HBM],
        HBM,
        [
            pltpu.VMEM((6, 8, 96, 128), BF16),
            pltpu.VMEM((72 * PITCH, 128), F32),
            pltpu.VMEM((128, 256), BF16),
            pltpu.VMEM((128, 256), BF16),
            pltpu.VMEM((512, 128), BF16),
            pltpu.VMEM((96, 128), F32),
            pltpu.VMEM((128, 72, 128), BF16),
            pltpu.SemaphoreType.DMA((LOADS,)),
            pltpu.SemaphoreType.DMA((2,)),
            pltpu.SemaphoreType.DMA((STORES,)),
        ],
        LIMIT_PROJECT,
    )(pair, residue_mask, left_weight, right_weight)
    wire = exchange(wire, ALL)
    gate = call(gate_kernel, shape((40, 128, 128)), [VMEM] * 2, VMEM, [], work=3)(
        pair, gate_weight
    )

    col_mask = lax.dynamic_slice_in_dim(residue_mask, lax.axis_index(COL) * 96, 96).reshape(3, 32)
    chunk = lambda jc: jnp.tile(col_mask[jc], 4)
    split = jnp.concatenate([col_mask[0], col_mask[0], col_mask[1], col_mask[1]])
    mask = jnp.repeat(jnp.stack([chunk(0), chunk(1), chunk(2), split, chunk(2)]), 8, axis=0)
    gate, mask, wire = lax.optimization_barrier((gate, mask, wire))
    sums = call(
        triangle_kernel,
        shape((128, 40, 128)),
        [VMEM],
        VMEM,
        [
            pltpu.VMEM((768, 768), BF16),
            pltpu.VMEM((768, 768), BF16),
            pltpu.VMEM((768, 768), F32),
            pltpu.VMEM((512, 512), BF16),
        ],
    )(wire)
    sums = exchange(sums, ALL)
    send, first = call(
        first_kernel,
        (shape((8, 576, 128)), shape((40, 128, 128))),
        [VMEM] * 7,
        (VMEM, VMEM),
        [pltpu.VMEM((128 * 40, 128), F32), pltpu.VMEM((40, 128), F32)],
    )(sums, pair, gate, out_weight, attn_weight, bias_weight[None, :], mask)
    held = exchange(send, COL)
    first, held = lax.optimization_barrier((first, held))
    bias = call(bias_kernel, shape((8, 48, 768)), [VMEM], VMEM, [])(held)
    bias = exchange(bias, ("x", "yh"))
    first = call(turn_kernel, shape((8, 720, 128)), [VMEM] * 3, VMEM, [], work=WORK_LATE)(
        first, attn_weight, jnp.asarray(GATE_MOVE, BF16)
    )
    first, bias = lax.optimization_barrier((first, bias))
    other = lax.ppermute(bias, "core", [(0, 1), (1, 0)])
    keyed = call(
        split_kernel, shape((6, 768, 128)), [VMEM] * 2, VMEM, [], work=WORK_SCORE
    )(held, jnp.asarray(KEY_MOVE, BF16))
    scratch = [pltpu.VMEM((384, 768), F32), pltpu.VMEM((8 * 144, 128), F32)]
    mine = call(
        attend_mine_kernel, shape((8, 144, 128)), [VMEM] * 3, VMEM, scratch, work=WORK_MINE
    )(held, keyed, bias)
    gated = call(
        attend_other_kernel, shape((8, 144, 128)), [VMEM] * 4, VMEM, scratch, work=2
    )(held, keyed, other, mine)
    gated = exchange(gated, COL)
    updated = call(
        update_kernel,
        shape((6, 8, 96, 128)),
        [VMEM, VMEM, VMEM],
        HBM,
        [
            pltpu.VMEM((128, 512), BF16),
            pltpu.VMEM((6, 8, 96, 128), BF16),
            pltpu.SemaphoreType.DMA((8,)),
        ],
        LIMIT_UPDATE,
    )(gated, first, attn_out_weight)
    return updated.reshape(48, 96, 128)


def solution(mesh):
    parts = Mesh(mesh.devices.reshape(4, 2, 2, 2, 4), ALL)
    spec = P(("x", "yh", "core"), COL, None)
    return jax.shard_map(
        body,
        mesh=parts,
        in_specs=(spec, P(), P(), P(), P(), P(), P(), P(), P()),
        out_specs=spec,
        check_vma=False,
    )
```

```python
import math

import jax
import jax.numpy as jnp
import numpy as np
from jax import lax
from jax.experimental import pallas as pl
from jax.experimental.pallas import tpu as pltpu
from jax.sharding import Mesh
from jax.sharding import PartitionSpec as P

F32 = jnp.float32
BF16 = jnp.bfloat16
LOG2E = math.log2(math.e)
PITCH = 136
UNROLL_PROJECT = 8
UNROLL_EMIT = 8
LOADS = 1
STORES = 8
WORK_MINE = 30
WORK_LATE = 1
WORK_SCORE = 100
LIMIT_OTHER = 20
LIMIT_PROJECT = 60
LIMIT_TRIANGLE = 20
LIMIT_FIRST = 20
LIMIT_UPDATE = 20
UNROLL_UNPACK = 8
UNROLL_PACK = 2
UNROLL_FIRST = 8
UNROLL_ATTEND = 6
PARTS = 2
UNROLL_UPDATE = 8
ALL = ("x", "yh", "core", "yl", "z")
COL = ("yl", "z")
VMEM = pl.BlockSpec(memory_space=pltpu.VMEM)
HBM = pl.BlockSpec(memory_space=pltpu.HBM)


def lanes_from(starts):
    row, lane = np.arange(128)[:, None], np.arange(128)[None, :]
    return (row == np.asarray(starts)[lane // 32] + lane % 32).astype(np.float32)


KEY_MOVE = lanes_from([32, 64, 64, 64])
GATE_MOVE = lanes_from([96, 96, 96, 96])


def sigmoid(values):
    return 0.5 * jnp.tanh(0.5 * values) + 0.5


def layer_norm_rows(values):
    center = values - jnp.mean(values, axis=-1, keepdims=True)
    spread = jnp.mean(center * center, axis=-1, keepdims=True)
    return center * lax.rsqrt(spread + 1e-05)


def swap_blocks(parts):
    lane = lax.broadcasted_iota(jnp.int32, parts[0].shape, 1)
    odd = jnp.bitwise_and(lane, 32) != 0
    high = lane >= 64
    v0, v1, v2, v3 = parts
    a0 = jnp.where(odd, pltpu.roll(v1, 32, 1), v0)
    a1 = jnp.where(odd, v1, pltpu.roll(v0, 96, 1))
    a2 = jnp.where(odd, pltpu.roll(v3, 32, 1), v2)
    a3 = jnp.where(odd, v3, pltpu.roll(v2, 96, 1))
    return (
        jnp.where(high, pltpu.roll(a2, 64, 1), a0),
        jnp.where(high, pltpu.roll(a3, 64, 1), a1),
        jnp.where(high, a2, pltpu.roll(a0, 64, 1)),
        jnp.where(high, a3, pltpu.roll(a1, 64, 1)),
    )


def project_kernel(
    pair_hbm, mask_ref, left_hbm, right_hbm, wire_out, held_ref, slab_ref,
    left_ref, right_ref, sides_ref, col_ref, wire_ref, sems, w_sems, out_sems,
):
    step_rows, step_channels = 8 // LOADS, 128 // STORES
    loads = []
    for q in range(LOADS):
        part = slice(step_rows * q, step_rows * q + step_rows)
        loads.append(
            pltpu.make_async_copy(pair_hbm.at[:, part], held_ref.at[:, part], sems.at[q])
        )
    weights = [
        pltpu.make_async_copy(left_hbm, left_ref, w_sems.at[0]),
        pltpu.make_async_copy(right_hbm, right_ref, w_sems.at[1]),
    ]
    for copy in weights + loads:
        copy.start()
    row_base = lax.axis_index(("x", "yh", "core")) * 48
    col_base = lax.axis_index(COL) * 96

    def mask_row(k, carry):
        col_ref[pl.ds(k, 1), :] = jnp.full((1, 128), mask_ref[col_base + k].astype(F32))
        return carry

    lax.fori_loop(0, 96, mask_row, 0, unroll=8)
    for copy in weights:
        copy.wait()
    sides_ref[0:256, :] = left_ref[...].T
    sides_ref[256:512, :] = right_ref[...].T
    lane = lax.broadcasted_iota(jnp.int32, (128, 128), 1)

    def step(ii, carry):
        values = jnp.concatenate([held_ref[s, ii] for s in range(6)], axis=0).astype(F32)
        normed = layer_norm_rows(values)
        kept = [
            (
                normed[s * 96 : s * 96 + 96]
                * (col_ref[...] * mask_ref[row_base + s * 8 + ii].astype(F32))
            ).astype(BF16)
            for s in range(6)
        ]
        piece = lambda s, kc: kept[s][kc * 32 : kc * 32 + 32]
        store = lambda row: pl.ds(pl.multiple_of(row * PITCH, 8), 128)
        blocks = [(kc, s) for kc in range(3) for s in range(4)]
        blocks += [(kc, s) for kc in range(3) for s in (4, 5, 4, 5)]
        rows = jnp.concatenate([piece(s, kc) for kc, s in blocks], axis=0)
        for n in range(6):
            if n % 2 == 0:
                pair_of = lax.dot_general(
                    sides_ref[...],
                    rows[n * 128 : n * 128 + 256],
                    (((1,), (1,)), ((), ())),
                    preferred_element_type=F32,
                )
            proj = pair_of[:, n % 2 * 128 : n % 2 * 128 + 128]
            if n < 3:
                slab_ref[store(n * 8 + ii), :] = sigmoid(proj[128:256]) * proj[0:128]
                slab_ref[store(24 + n * 8 + ii), :] = sigmoid(proj[384:512]) * proj[256:384]
            else:
                value = jnp.where(lane < 64, proj[0:128], proj[256:384])
                gating = jnp.where(lane < 64, proj[128:256], proj[384:512])
                slab_ref[store(24 + n * 8 + ii), :] = sigmoid(gating) * value
        return carry

    for q in range(LOADS):
        loads[q].wait()
        lax.fori_loop(
            step_rows * q, step_rows * q + step_rows, step, 0, unroll=UNROLL_PROJECT
        )

    def emit(ch, carry):
        wire_ref[ch] = slab_ref[pl.ds(ch, 72, stride=PITCH), :].astype(BF16)
        return carry

    stores = []
    for q in range(STORES):
        part = slice(step_channels * q, step_channels * q + step_channels)
        stores.append(
            pltpu.make_async_copy(wire_ref.at[part], wire_out.at[part], out_sems.at[q])
        )
    for q in range(STORES):
        lax.fori_loop(
            step_channels * q, step_channels * q + step_channels, emit, 0, unroll=UNROLL_EMIT
        )
        stores[q].start()
    for copy in stores:
        copy.wait()


def triangle_kernel(wire_ref, out_ref, left_ref, right_ref, sums_ref, perm_ref):
    row = lax.broadcasted_iota(jnp.int32, (128, 128), 0)
    col = lax.broadcasted_iota(jnp.int32, (128, 128), 1)
    same = jnp.bitwise_and(row, 31) == jnp.bitwise_and(col, 31)
    for z in range(4):
        for b in range(4):
            hit = same & (row >= b * 32) & (row < b * 32 + 32) & (col >= z * 32) & (col < z * 32 + 32)
            perm_ref[z * 128 : z * 128 + 128, b * 128 : b * 128 + 128] = jnp.where(
                hit, 1.0, 0.0
            ).astype(BF16)

    def unpack(c_pair, carry):
        groups = [(half, yl) for half in range(2) for yl in range(2)]
        source = lambda half, yl, z: wire_ref[(c_pair * 2 + half) * 8 + yl * 4 + z]
        rows = jnp.concatenate(
            [
                jnp.concatenate([source(half, yl, z) for z in range(4)], axis=1)
                for half, yl in groups
            ],
            axis=0,
        )
        swapped = jnp.dot(rows, perm_ref[...], preferred_element_type=F32)
        for n, (half, yl) in enumerate(groups):
            at = lambda k, base: swapped[
                n * 72 + base + kc * 8 : n * 72 + base + kc * 8 + 8, k * 128 : k * 128 + 128
            ]
            for kc in range(3):
                cols = pl.ds((yl * 3 + kc) * 128, 128)
                left = jnp.concatenate(
                    [at(s, 0) for s in range(4)] + [at(0, 48), at(1, 48)], axis=0
                ).astype(BF16)
                right = jnp.concatenate(
                    [at(s, 24) for s in range(4)] + [at(2, 48), at(3, 48)], axis=0
                ).astype(BF16)
                row = pl.multiple_of((c_pair * 2 + half) * 48, 16)
                left_ref[pl.ds(row, 48), cols] = left
                for g3 in range(3):
                    g = half * 3 + g3
                    base = ((c_pair // 4) * 3 + g // 2) * 128 + (c_pair % 4) * 32 + (g % 2) * 16
                    right_ref[pl.ds(pl.multiple_of(base, 16), 16), cols] = right[
                        g3 * 16 : g3 * 16 + 16
                    ]
        return carry

    lax.fori_loop(0, 8, unpack, 0, unroll=UNROLL_UNPACK)
    for n in range(3):
        sums_ref[:, n * 256 : (n + 1) * 256] = lax.dot_general(
            left_ref[...],
            right_ref[n * 256 : (n + 1) * 256, :],
            (((1,), (1,)), ((), ())),
            preferred_element_type=F32,
        )

    def pack(r, carry):
        base = pl.multiple_of(r * 48, 16)
        order = (
            [(s, 0) for s in range(4)],
            [(s, 1) for s in range(4)],
            [(s, 2) for s in range(4)],
            [(4, 0), (5, 0), (4, 1), (5, 1)],
            [(4, 2), (5, 2), (4, 2), (5, 2)],
        )
        for yl in range(2):
            tile = lambda s, jc: sums_ref[
                pl.ds(pl.multiple_of(base + s * 8, 8), 8),
                (yl * 3 + jc) * 128 : (yl * 3 + jc + 1) * 128,
            ]
            parts = [
                jnp.concatenate([tile(*entry[a]) for entry in order], axis=0) for a in range(4)
            ]
            outs = swap_blocks(parts)
            for z in range(4):
                out_ref[r * 8 + yl * 4 + z] = outs[z].astype(BF16)
        return carry

    lax.fori_loop(0, 16, pack, 0, unroll=UNROLL_PACK)


def slab_chunks(base):
    if base < 3:
        return [(s, base) for s in range(4)]
    if base == 3:
        return [(4, 0), (5, 0), (4, 1), (5, 1)]
    return [(4, 2), (5, 2)]


def gate_kernel(pair_ref, gate_w_ref, out_ref):
    gate_w = gate_w_ref[...].T

    def step(ii, carry):
        held = [pair_ref[s, ii] for s in range(6)]
        values = jnp.concatenate(held, axis=0).astype(F32)
        normed = layer_norm_rows(values).astype(BF16)
        for base in range(5):
            chunks = slab_chunks(base)
            chunks = chunks + chunks[: 4 - len(chunks)]
            rows = jnp.concatenate(
                [normed[s * 96 + jc * 32 : s * 96 + jc * 32 + 32] for s, jc in chunks], axis=0
            )
            gate = lax.dot_general(
                gate_w, rows, (((1,), (1,)), ((), ())), preferred_element_type=F32
            )
            out_ref[base * 8 + ii] = sigmoid(gate).astype(BF16)
        return carry

    lax.fori_loop(0, 8, step, 0)


def first_kernel(
    wire_ref, pair_ref, gate_ref, out_w_ref, attn_w_ref, bias_w_ref, mask_ref,
    send_ref, first_ref, norm_ref, bias_ref,
):
    def add(ch, total):
        return total + wire_ref[ch].astype(F32)

    zero = jnp.zeros((40, 128), F32)
    mean = lax.fori_loop(0, 128, add, zero, unroll=8) * (1.0 / 128)

    def add_square(ch, total):
        center = wire_ref[ch].astype(F32) - mean
        return total + center * center

    spread = lax.fori_loop(0, 128, add_square, zero, unroll=8) * (1.0 / 128)
    scale = lax.rsqrt(spread + 1e-05)

    def write(ch, carry):
        norm_ref[pl.ds(pl.multiple_of(ch * 40, 8), 40), :] = (
            wire_ref[ch].astype(F32) - mean
        ) * scale
        return carry

    lax.fori_loop(0, 128, write, 0, unroll=8)
    lane = lax.broadcasted_iota(jnp.int32, (1, 128), 1)
    query_scale = jnp.where(lane < 32, LOG2E / math.sqrt(32), 1.0)
    bias_w = jnp.broadcast_to(bias_w_ref[...], (16, 128))
    out_w = out_w_ref[...].T
    same = lax.broadcasted_iota(jnp.int32, (128, 128), 0) == lax.broadcasted_iota(
        jnp.int32, (128, 128), 1
    )
    unit = jnp.where(same, 1.0, 0.0).astype(BF16)

    def step(ii, carry):
        rows = [base * 8 + ii for base in range(5)]
        side = lambda values: jnp.concatenate(values, axis=1)
        tri = side([norm_ref[pl.ds(row, 128, stride=40), :].astype(BF16) for row in rows])
        update = jnp.dot(out_w, tri, preferred_element_type=F32)
        chunks = [chunk for base in range(5) for chunk in (slab_chunks(base) * 2)[:4]]
        plain = jnp.concatenate(
            [pair_ref[s, ii, jc * 32 : jc * 32 + 32, :] for s, jc in chunks], axis=0
        )
        pair = lax.dot_general(
            unit, plain, (((1,), (1,)), ((), ())), preferred_element_type=F32
        )
        first = pair + side([gate_ref[row].astype(F32) for row in rows]) * update
        center = first - jnp.mean(first, axis=0, keepdims=True)
        spread = jnp.mean(center * center, axis=0, keepdims=True)
        normed = center * lax.rsqrt(spread + 1e-05)
        bias = jnp.dot(bias_w, normed.astype(BF16), preferred_element_type=F32)
        turned = []
        for base, row in enumerate(rows):
            cols = slice(base * 128, base * 128 + 128)
            first_ref[row] = first[:, cols].astype(BF16)
            bias_ref[pl.ds(row, 1), :] = bias[0:1, cols]
            turned.append(normed[:, cols].T)
        turned = jnp.concatenate(turned, axis=0).astype(BF16)
        proj = jnp.dot(turned, attn_w_ref[...], preferred_element_type=F32)
        proj = (proj * query_scale).astype(BF16)
        for base in range(5):
            for n, (s, jc) in enumerate(slab_chunks(base)):
                at = base * 128 + n * 32
                send_ref[ii, s * 96 + jc * 32 : s * 96 + jc * 32 + 32, :] = proj[at : at + 32]
        return carry

    lax.fori_loop(0, 8, step, 0, unroll=UNROLL_FIRST)
    bias = jnp.where(mask_ref[...] > 0, bias_ref[...] * LOG2E, -1e9 * LOG2E)
    bias = jnp.concatenate([bias, jnp.zeros((8, 128), F32)], axis=0)
    wide = lax.broadcasted_iota(jnp.int32, (48, 128), 1)
    for g in range(4):
        rows = slice(g * 48, g * 48 + 48)
        part = bias if g == 3 else pltpu.roll(bias, 96 - 32 * g, 1)
        for ii in range(8):
            held = send_ref[ii, rows, :].astype(F32)
            send_ref[ii, rows, :] = jnp.where(wide < 96, held, part).astype(BF16)


def turn_kernel(slab_ref, attn_w_ref, move_ref, out_ref):
    gate_w = jnp.dot(attn_w_ref[...], move_ref[...], preferred_element_type=F32).astype(BF16)
    lane = lax.broadcasted_iota(jnp.int32, (24, 128), 1)

    def step(ii, carry):
        first = jnp.concatenate(
            [slab_ref[base * 8 + ii].astype(F32) for base in range(5)], axis=1
        )
        center = first - jnp.mean(first, axis=0, keepdims=True)
        spread = jnp.mean(center * center, axis=0, keepdims=True)
        normed = center * lax.rsqrt(spread + 1e-05)
        turned = jnp.concatenate(
            [normed[:, base * 128 : base * 128 + 128].T for base in range(5)], axis=0
        )
        gate = jnp.dot(turned.astype(BF16), gate_w, preferred_element_type=F32)
        place = {}
        for base in range(5):
            plain = first[:, base * 128 : base * 128 + 128].T.astype(BF16)
            for n, (s, jc) in enumerate(slab_chunks(base)):
                out_ref[ii, s * 96 + jc * 32 : s * 96 + jc * 32 + 32, :] = plain[
                    n * 32 : n * 32 + 32
                ]
                place[s, jc] = gate[base * 128 + n * 32 : base * 128 + n * 32 + 32]
        packed = []
        for s in range(6):
            whole = sigmoid(jnp.concatenate([place[s, jc] for jc in range(3)], axis=0))
            g = [whole[q * 24 : q * 24 + 24] for q in range(4)]
            low = jnp.where(lane < 32, g[0], g[1])
            high = jnp.where(lane < 96, g[2], g[3])
            packed.append(jnp.where(lane < 64, low, high))
        out_ref[ii, 576:720, :] = jnp.concatenate(packed, axis=0).astype(BF16)
        return carry

    lax.fori_loop(0, 8, step, 0)


def bias_kernel(held_ref, out_ref):
    wide = lax.broadcasted_iota(jnp.int32, (48, 128), 1)

    def slabs(block):
        g = [held_ref[block, q * 48 : q * 48 + 48, :].astype(F32) for q in range(4)]
        g = [pltpu.roll(g[q], 32 * q + 32, 1) for q in range(3)] + [g[3]]
        low = jnp.where(wide < 32, g[0], g[1])
        return jnp.where(wide < 64, low, jnp.where(wide < 96, g[2], g[3]))[0:40]

    both = swap_blocks(
        [jnp.concatenate([slabs(yl * 4 + z) for yl in range(2)], axis=0) for z in range(4)]
    )
    tiles = []
    for yl in range(2):
        parts = [part[yl * 40 : yl * 40 + 40] for part in both]
        tiles.append([p[0:8] for p in parts] + [parts[0][24:32], parts[1][24:32]])
        tiles.append([p[8:16] for p in parts] + [parts[2][24:32], parts[3][24:32]])
        tiles.append([p[16:24] for p in parts] + [parts[0][32:40], parts[1][32:40]])
    whole = jnp.concatenate([jnp.concatenate(t, axis=0) for t in tiles], axis=1).astype(BF16)
    for copy in range(8):
        out_ref[copy] = whole


def split_kernel(held_ref, move_ref, out_ref):
    def step(s, carry):
        turned = jnp.concatenate(
            [
                held_ref[yl * 4 + z, pl.ds(pl.multiple_of(s * 96 + jc * 32, 32), 32), :]
                for yl in range(2)
                for jc in range(3)
                for z in range(4)
            ],
            axis=0,
        )
        out_ref[s] = jnp.dot(turned, move_ref[...], preferred_element_type=F32).astype(BF16)
        return carry

    lax.fori_loop(0, 6, step, 0)


def attend_half(half, held_ref, keyed_ref, bias_ref, extra_ref, packed_ref):
    for c in range(8):
        extra_ref[c * 48 : c * 48 + 48, :] = bias_ref[c].astype(F32)
    blocks = 8 // PARTS
    size = blocks * 48
    wide = lax.broadcasted_iota(jnp.int32, (size, 128), 1)
    lane = lax.broadcasted_iota(jnp.int32, (24, 128), 1)

    def step(s, carry):
        value = jnp.concatenate([keyed_ref[s], jnp.ones((768, 128), BF16)], axis=1)
        at = pl.ds(pl.multiple_of(s * 96 + half * 48, 16), 48)
        for t in range(PARTS):
            rows = jnp.concatenate(
                [held_ref[t * blocks + c, at, :] for c in range(blocks)], axis=0
            )
            query = jnp.where(wide < 32, rows, jnp.zeros_like(rows))
            scores = lax.dot_general(
                query, keyed_ref[s], (((1,), (1,)), ((), ())), preferred_element_type=F32
            )
            scores = scores + extra_ref[t * size : (t + 1) * size, :]
            top = jnp.max(scores, axis=-1, keepdims=True)
            weights = jnp.exp2(scores - top).astype(BF16)
            summed = jnp.dot(weights, value, preferred_element_type=F32)
            result = summed[:, 0:128] / summed[:, 128:256]
            for h in range(blocks):
                row = pl.multiple_of((t * blocks + h) * 144 + s * 24, 8)
                packed_ref[pl.ds(row, 24), :] = jnp.where(
                    lane < 96, result[h * 48 : h * 48 + 24], result[h * 48 + 24 : h * 48 + 48]
                )
        return carry

    lax.fori_loop(0, 6, step, 0, unroll=UNROLL_ATTEND)


def attend_mine_kernel(held_ref, keyed_ref, bias_ref, out_ref, extra_ref, packed_ref):
    half = lax.axis_index("core")
    attend_half(half, held_ref, keyed_ref, bias_ref, extra_ref, packed_ref)
    for c in range(8):
        out_ref[c] = packed_ref[c * 144 : (c + 1) * 144, :].astype(BF16)


def attend_other_kernel(held_ref, keyed_ref, bias_ref, mine_ref, out_ref, extra_ref, packed_ref):
    half = 1 - lax.axis_index("core")
    attend_half(half, held_ref, keyed_ref, bias_ref, extra_ref, packed_ref)
    lane = lax.broadcasted_iota(jnp.int32, (144, 128), 1)
    for c in range(8):
        mine, other = mine_ref[c].astype(F32), packed_ref[c * 144 : (c + 1) * 144, :]
        low = jnp.where(half == 0, other, mine)
        high = jnp.where(half == 0, mine, other)
        out_ref[c] = jnp.where(lane < 64, pltpu.roll(low, 64, 1), high).astype(BF16)


def update_kernel(held_ref, first_ref, weight_ref, out_hbm, wide_ref, done_ref, out_sems):
    def store(ii):
        return pltpu.make_async_copy(done_ref.at[:, ii], out_hbm.at[:, ii], out_sems.at[ii])

    wide_ref[...] = jnp.zeros((128, 512), BF16)
    for g in range(4):
        wide_ref[g * 32 : g * 32 + 32, g * 128 : g * 128 + 128] = weight_ref[...]

    def step(ii, carry):
        gated = held_ref[ii].astype(F32) * first_ref[ii, 576:720, :].astype(F32)
        add = jnp.dot(gated.astype(BF16), wide_ref[...], preferred_element_type=F32)
        for s in range(6):
            rows = jnp.concatenate(
                [add[s * 24 : s * 24 + 24, g * 128 : (g + 1) * 128] for g in range(4)], axis=0
            )
            first = first_ref[ii, s * 96 : (s + 1) * 96, :].astype(F32)
            done_ref[s, ii] = (first + rows).astype(BF16)
        store(ii).start()
        return carry

    lax.fori_loop(0, 8, step, 0, unroll=UNROLL_UPDATE)
    for ii in range(8):
        store(ii).wait()


def call(kernel, outs, in_specs, out_specs, scratch, limit=LIMIT_OTHER, work=0):
    cost = pl.CostEstimate(flops=work * 10**9, bytes_accessed=work * 10**6, transcendentals=0)
    return pl.pallas_call(
        kernel,
        out_shape=outs,
        in_specs=in_specs,
        out_specs=out_specs,
        scratch_shapes=scratch,
        cost_estimate=cost if work else None,
        compiler_params=pltpu.CompilerParams(vmem_limit_bytes=limit * 1024 * 1024),
    )


def shape(dims, dtype=BF16):
    return jax.ShapeDtypeStruct(dims, dtype)


def exchange(values, axes):
    return lax.all_to_all(values, axes, 0, 0, tiled=True)


def body(
    pair,
    residue_mask,
    left_weight,
    right_weight,
    gate_weight,
    out_weight,
    attn_weight,
    bias_weight,
    attn_out_weight,
):
    pair = pair.reshape(6, 8, 96, 128)
    wire = call(
        project_kernel,
        shape((128, 72, 128)),
        [HBM, pl.BlockSpec(memory_space=pltpu.SMEM), HBM, HBM],
        HBM,
        [
            pltpu.VMEM((6, 8, 96, 128), BF16),
            pltpu.VMEM((73 * PITCH, 128), F32),
            pltpu.VMEM((128, 256), BF16),
            pltpu.VMEM((128, 256), BF16),
            pltpu.VMEM((512, 128), BF16),
            pltpu.VMEM((96, 128), F32),
            pltpu.VMEM((128, 72, 128), BF16),
            pltpu.SemaphoreType.DMA((LOADS,)),
            pltpu.SemaphoreType.DMA((2,)),
            pltpu.SemaphoreType.DMA((STORES,)),
        ],
        LIMIT_PROJECT,
    )(pair, residue_mask, left_weight, right_weight)
    wire = exchange(wire, ALL)
    gate = call(gate_kernel, shape((40, 128, 128)), [VMEM] * 2, VMEM, [], work=3)(
        pair, gate_weight
    )

    col_mask = lax.dynamic_slice_in_dim(residue_mask, lax.axis_index(COL) * 96, 96).reshape(3, 32)
    chunk = lambda jc: jnp.tile(col_mask[jc], 4)
    split = jnp.concatenate([col_mask[0], col_mask[0], col_mask[1], col_mask[1]])
    mask = jnp.repeat(jnp.stack([chunk(0), chunk(1), chunk(2), split, chunk(2)]), 8, axis=0)
    gate, mask, wire = lax.optimization_barrier((gate, mask, wire))
    sums = call(
        triangle_kernel,
        shape((128, 40, 128)),
        [VMEM],
        VMEM,
        [
            pltpu.VMEM((768, 768), BF16),
            pltpu.VMEM((768, 768), BF16),
            pltpu.VMEM((768, 768), F32),
            pltpu.VMEM((512, 512), BF16),
        ],
    )(wire)
    sums = exchange(sums, ALL)
    send, first = call(
        first_kernel,
        (shape((8, 576, 128)), shape((40, 128, 128))),
        [VMEM] * 7,
        (VMEM, VMEM),
        [pltpu.VMEM((129 * 40, 128), F32), pltpu.VMEM((40, 128), F32)],
    )(sums, pair, gate, out_weight, attn_weight, bias_weight[None, :], mask)
    held = exchange(send, COL)
    first, held = lax.optimization_barrier((first, held))
    bias = call(bias_kernel, shape((8, 48, 768)), [VMEM], VMEM, [])(held)
    bias = exchange(bias, ("x", "yh"))
    first = call(turn_kernel, shape((8, 720, 128)), [VMEM] * 3, VMEM, [], work=WORK_LATE)(
        first, attn_weight, jnp.asarray(GATE_MOVE, BF16)
    )
    first, bias = lax.optimization_barrier((first, bias))
    other = lax.ppermute(bias, "core", [(0, 1), (1, 0)])
    keyed = call(
        split_kernel, shape((6, 768, 128)), [VMEM] * 2, VMEM, [], work=WORK_SCORE
    )(held, jnp.asarray(KEY_MOVE, BF16))
    scratch = [pltpu.VMEM((384, 768), F32), pltpu.VMEM((8 * 144, 128), F32)]
    mine = call(
        attend_mine_kernel, shape((8, 144, 128)), [VMEM] * 3, VMEM, scratch, work=WORK_MINE
    )(held, keyed, bias)
    gated = call(
        attend_other_kernel, shape((8, 144, 128)), [VMEM] * 4, VMEM, scratch, work=2
    )(held, keyed, other, mine)
    gated = exchange(gated, COL)
    updated = call(
        update_kernel,
        shape((6, 8, 96, 128)),
        [VMEM, VMEM, VMEM],
        HBM,
        [
            pltpu.VMEM((128, 512), BF16),
            pltpu.VMEM((6, 8, 96, 128), BF16),
            pltpu.SemaphoreType.DMA((8,)),
        ],
        LIMIT_UPDATE,
    )(gated, first, attn_out_weight)
    return updated.reshape(48, 96, 128)


def solution(mesh):
    parts = Mesh(mesh.devices.reshape(4, 2, 2, 2, 4), ALL)
    spec = P(("x", "yh", "core"), COL, None)
    return jax.shard_map(
        body,
        mesh=parts,
        in_specs=(spec, P(), P(), P(), P(), P(), P(), P(), P()),
        out_specs=spec,
        check_vma=False,
    )
```

```python
import math

import jax
import jax.numpy as jnp
import numpy as np
from jax import lax
from jax.experimental import pallas as pl
from jax.experimental.pallas import tpu as pltpu
from jax.sharding import Mesh
from jax.sharding import PartitionSpec as P

F32 = jnp.float32
BF16 = jnp.bfloat16
LOG2E = math.log2(math.e)
PITCH = 136
UNROLL_PROJECT = 8
UNROLL_EMIT = 8
LOADS = 1
STORES = 8
WORK_MINE = 30
WORK_LATE = 1
LIMIT_OTHER = 20
LIMIT_PROJECT = 60
LIMIT_TRIANGLE = 20
LIMIT_FIRST = 20
LIMIT_UPDATE = 20
UNROLL_UNPACK = 8
UNROLL_PACK = 2
UNROLL_FIRST = 8
UNROLL_ATTEND = 6
PARTS = 2
UNROLL_UPDATE = 8
ALL = ("x", "yh", "core", "yl", "z")
COL = ("yl", "z")
VMEM = pl.BlockSpec(memory_space=pltpu.VMEM)
HBM = pl.BlockSpec(memory_space=pltpu.HBM)


def lanes_from(starts):
    row, lane = np.arange(128)[:, None], np.arange(128)[None, :]
    return (row == np.asarray(starts)[lane // 32] + lane % 32).astype(np.float32)


KEY_MOVE = lanes_from([32, 64, 64, 64])
GATE_MOVE = lanes_from([96, 96, 96, 96])


def sigmoid(values):
    return 0.5 * jnp.tanh(0.5 * values) + 0.5


def layer_norm_rows(values):
    center = values - jnp.mean(values, axis=-1, keepdims=True)
    spread = jnp.mean(center * center, axis=-1, keepdims=True)
    return center * lax.rsqrt(spread + 1e-05)


def swap_blocks(parts):
    lane = lax.broadcasted_iota(jnp.int32, parts[0].shape, 1)
    odd = jnp.bitwise_and(lane, 32) != 0
    high = lane >= 64
    v0, v1, v2, v3 = parts
    a0 = jnp.where(odd, pltpu.roll(v1, 32, 1), v0)
    a1 = jnp.where(odd, v1, pltpu.roll(v0, 96, 1))
    a2 = jnp.where(odd, pltpu.roll(v3, 32, 1), v2)
    a3 = jnp.where(odd, v3, pltpu.roll(v2, 96, 1))
    return (
        jnp.where(high, pltpu.roll(a2, 64, 1), a0),
        jnp.where(high, pltpu.roll(a3, 64, 1), a1),
        jnp.where(high, a2, pltpu.roll(a0, 64, 1)),
        jnp.where(high, a3, pltpu.roll(a1, 64, 1)),
    )


def project_kernel(
    pair_hbm, mask_ref, left_hbm, right_hbm, wire_out, held_ref, slab_ref,
    left_ref, right_ref, sides_ref, col_ref, wire_ref, sems, w_sems, out_sems,
):
    step_rows, step_channels = 8 // LOADS, 128 // STORES
    loads = []
    for q in range(LOADS):
        part = slice(step_rows * q, step_rows * q + step_rows)
        loads.append(
            pltpu.make_async_copy(pair_hbm.at[:, part], held_ref.at[:, part], sems.at[q])
        )
    weights = [
        pltpu.make_async_copy(left_hbm, left_ref, w_sems.at[0]),
        pltpu.make_async_copy(right_hbm, right_ref, w_sems.at[1]),
    ]
    for copy in weights + loads:
        copy.start()
    row_base = lax.axis_index(("x", "yh", "core")) * 48
    col_base = lax.axis_index(COL) * 96

    def mask_row(k, carry):
        col_ref[pl.ds(k, 1), :] = jnp.full((1, 128), mask_ref[col_base + k].astype(F32))
        return carry

    lax.fori_loop(0, 96, mask_row, 0, unroll=8)
    for copy in weights:
        copy.wait()
    sides_ref[0:256, :] = left_ref[...].T
    sides_ref[256:512, :] = right_ref[...].T
    lane = lax.broadcasted_iota(jnp.int32, (128, 128), 1)

    def step(ii, carry):
        values = jnp.concatenate([held_ref[s, ii] for s in range(6)], axis=0).astype(F32)
        normed = layer_norm_rows(values)
        kept = [
            (
                normed[s * 96 : s * 96 + 96]
                * (col_ref[...] * mask_ref[row_base + s * 8 + ii].astype(F32))
            ).astype(BF16)
            for s in range(6)
        ]
        piece = lambda s, kc: kept[s][kc * 32 : kc * 32 + 32]
        store = lambda row: pl.ds(pl.multiple_of(row * PITCH, 8), 128)
        blocks = [(kc, s) for kc in range(3) for s in range(4)]
        blocks += [(kc, s) for kc in range(3) for s in (4, 5, 4, 5)]
        rows = jnp.concatenate([piece(s, kc) for kc, s in blocks], axis=0)
        for n in range(6):
            if n % 2 == 0:
                pair_of = lax.dot_general(
                    sides_ref[...],
                    rows[n * 128 : n * 128 + 256],
                    (((1,), (1,)), ((), ())),
                    preferred_element_type=F32,
                )
            proj = pair_of[:, n % 2 * 128 : n % 2 * 128 + 128]
            if n < 3:
                slab_ref[store(n * 8 + ii), :] = sigmoid(proj[128:256]) * proj[0:128]
                slab_ref[store(24 + n * 8 + ii), :] = sigmoid(proj[384:512]) * proj[256:384]
            else:
                value = jnp.where(lane < 64, proj[0:128], proj[256:384])
                gating = jnp.where(lane < 64, proj[128:256], proj[384:512])
                slab_ref[store(24 + n * 8 + ii), :] = sigmoid(gating) * value
        return carry

    for q in range(LOADS):
        loads[q].wait()
        lax.fori_loop(
            step_rows * q, step_rows * q + step_rows, step, 0, unroll=UNROLL_PROJECT
        )

    def emit(ch, carry):
        wire_ref[ch] = slab_ref[pl.ds(ch, 72, stride=PITCH), :].astype(BF16)
        return carry

    stores = []
    for q in range(STORES):
        part = slice(step_channels * q, step_channels * q + step_channels)
        stores.append(
            pltpu.make_async_copy(wire_ref.at[part], wire_out.at[part], out_sems.at[q])
        )
    for q in range(STORES):
        lax.fori_loop(
            step_channels * q, step_channels * q + step_channels, emit, 0, unroll=UNROLL_EMIT
        )
        stores[q].start()
    for copy in stores:
        copy.wait()


def triangle_kernel(wire_ref, out_ref, left_ref, right_ref, sums_ref, perm_ref):
    row = lax.broadcasted_iota(jnp.int32, (128, 128), 0)
    col = lax.broadcasted_iota(jnp.int32, (128, 128), 1)
    same = jnp.bitwise_and(row, 31) == jnp.bitwise_and(col, 31)
    for z in range(4):
        for b in range(4):
            hit = same & (row >= b * 32) & (row < b * 32 + 32) & (col >= z * 32) & (col < z * 32 + 32)
            perm_ref[z * 128 : z * 128 + 128, b * 128 : b * 128 + 128] = jnp.where(
                hit, 1.0, 0.0
            ).astype(BF16)

    def unpack(c_pair, carry):
        groups = [(half, yl) for half in range(2) for yl in range(2)]
        source = lambda half, yl, z: wire_ref[(c_pair * 2 + half) * 8 + yl * 4 + z]
        rows = jnp.concatenate(
            [
                jnp.concatenate([source(half, yl, z) for z in range(4)], axis=1)
                for half, yl in groups
            ],
            axis=0,
        )
        swapped = jnp.dot(rows, perm_ref[...], preferred_element_type=F32)
        for n, (half, yl) in enumerate(groups):
            at = lambda k, base: swapped[
                n * 72 + base + kc * 8 : n * 72 + base + kc * 8 + 8, k * 128 : k * 128 + 128
            ]
            for kc in range(3):
                cols = pl.ds((yl * 3 + kc) * 128, 128)
                left = jnp.concatenate(
                    [at(s, 0) for s in range(4)] + [at(0, 48), at(1, 48)], axis=0
                ).astype(BF16)
                right = jnp.concatenate(
                    [at(s, 24) for s in range(4)] + [at(2, 48), at(3, 48)], axis=0
                ).astype(BF16)
                row = pl.multiple_of((c_pair * 2 + half) * 48, 16)
                left_ref[pl.ds(row, 48), cols] = left
                for g3 in range(3):
                    g = half * 3 + g3
                    base = ((c_pair // 4) * 3 + g // 2) * 128 + (c_pair % 4) * 32 + (g % 2) * 16
                    right_ref[pl.ds(pl.multiple_of(base, 16), 16), cols] = right[
                        g3 * 16 : g3 * 16 + 16
                    ]
        return carry

    lax.fori_loop(0, 8, unpack, 0, unroll=UNROLL_UNPACK)
    for n in range(3):
        sums_ref[:, n * 256 : (n + 1) * 256] = lax.dot_general(
            left_ref[...],
            right_ref[n * 256 : (n + 1) * 256, :],
            (((1,), (1,)), ((), ())),
            preferred_element_type=F32,
        )

    def pack(r, carry):
        base = pl.multiple_of(r * 48, 16)
        order = (
            [(s, 0) for s in range(4)],
            [(s, 1) for s in range(4)],
            [(s, 2) for s in range(4)],
            [(4, 0), (5, 0), (4, 1), (5, 1)],
            [(4, 2), (5, 2), (4, 2), (5, 2)],
        )
        for yl in range(2):
            tile = lambda s, jc: sums_ref[
                pl.ds(pl.multiple_of(base + s * 8, 8), 8),
                (yl * 3 + jc) * 128 : (yl * 3 + jc + 1) * 128,
            ]
            parts = [
                jnp.concatenate([tile(*entry[a]) for entry in order], axis=0) for a in range(4)
            ]
            outs = swap_blocks(parts)
            for z in range(4):
                out_ref[r * 8 + yl * 4 + z] = outs[z].astype(BF16)
        return carry

    lax.fori_loop(0, 16, pack, 0, unroll=UNROLL_PACK)


def slab_chunks(base):
    if base < 3:
        return [(s, base) for s in range(4)]
    if base == 3:
        return [(4, 0), (5, 0), (4, 1), (5, 1)]
    return [(4, 2), (5, 2)]


def gate_kernel(pair_ref, gate_w_ref, out_ref):
    gate_w = gate_w_ref[...].T

    def step(ii, carry):
        held = [pair_ref[s, ii] for s in range(6)]
        values = jnp.concatenate(held, axis=0).astype(F32)
        normed = layer_norm_rows(values).astype(BF16)
        for base in range(5):
            chunks = slab_chunks(base)
            chunks = chunks + chunks[: 4 - len(chunks)]
            rows = jnp.concatenate(
                [normed[s * 96 + jc * 32 : s * 96 + jc * 32 + 32] for s, jc in chunks], axis=0
            )
            gate = lax.dot_general(
                gate_w, rows, (((1,), (1,)), ((), ())), preferred_element_type=F32
            )
            out_ref[base * 8 + ii] = sigmoid(gate).astype(BF16)
        return carry

    lax.fori_loop(0, 8, step, 0)


def first_kernel(
    wire_ref, pair_ref, gate_ref, out_w_ref, attn_w_ref, bias_w_ref, mask_ref,
    send_ref, first_ref, norm_ref, bias_ref,
):
    def add(ch, total):
        return total + wire_ref[ch].astype(F32)

    zero = jnp.zeros((40, 128), F32)
    mean = lax.fori_loop(0, 128, add, zero, unroll=8) * (1.0 / 128)

    def add_square(ch, total):
        center = wire_ref[ch].astype(F32) - mean
        return total + center * center

    spread = lax.fori_loop(0, 128, add_square, zero, unroll=8) * (1.0 / 128)
    scale = lax.rsqrt(spread + 1e-05)

    def write(ch, carry):
        norm_ref[pl.ds(pl.multiple_of(ch * 40, 8), 40), :] = (
            wire_ref[ch].astype(F32) - mean
        ) * scale
        return carry

    lax.fori_loop(0, 128, write, 0, unroll=8)
    lane = lax.broadcasted_iota(jnp.int32, (1, 128), 1)
    query_scale = jnp.where(lane < 32, LOG2E / math.sqrt(32), 1.0)
    bias_w = jnp.broadcast_to(bias_w_ref[...], (16, 128))
    out_w = out_w_ref[...].T
    same = lax.broadcasted_iota(jnp.int32, (128, 128), 0) == lax.broadcasted_iota(
        jnp.int32, (128, 128), 1
    )
    unit = jnp.where(same, 1.0, 0.0).astype(BF16)

    def step(ii, carry):
        rows = [base * 8 + ii for base in range(5)]
        side = lambda values: jnp.concatenate(values, axis=1)
        tri = side([norm_ref[pl.ds(row, 128, stride=40), :].astype(BF16) for row in rows])
        update = jnp.dot(out_w, tri, preferred_element_type=F32)
        chunks = [chunk for base in range(5) for chunk in (slab_chunks(base) * 2)[:4]]
        plain = jnp.concatenate(
            [pair_ref[s, ii, jc * 32 : jc * 32 + 32, :] for s, jc in chunks], axis=0
        )
        pair = lax.dot_general(
            unit, plain, (((1,), (1,)), ((), ())), preferred_element_type=F32
        )
        first = pair + side([gate_ref[row].astype(F32) for row in rows]) * update
        center = first - jnp.mean(first, axis=0, keepdims=True)
        spread = jnp.mean(center * center, axis=0, keepdims=True)
        normed = center * lax.rsqrt(spread + 1e-05)
        bias = jnp.dot(bias_w, normed.astype(BF16), preferred_element_type=F32)
        turned = []
        for base, row in enumerate(rows):
            cols = slice(base * 128, base * 128 + 128)
            first_ref[row] = first[:, cols].astype(BF16)
            bias_ref[pl.ds(row, 1), :] = bias[0:1, cols]
            turned.append(normed[:, cols].T)
        turned = jnp.concatenate(turned, axis=0).astype(BF16)
        proj = jnp.dot(turned, attn_w_ref[...], preferred_element_type=F32)
        proj = (proj * query_scale).astype(BF16)
        for base in range(5):
            for n, (s, jc) in enumerate(slab_chunks(base)):
                at = base * 128 + n * 32
                send_ref[ii, s * 96 + jc * 32 : s * 96 + jc * 32 + 32, :] = proj[at : at + 32]
        return carry

    lax.fori_loop(0, 8, step, 0, unroll=UNROLL_FIRST)
    bias = jnp.where(mask_ref[...] > 0, bias_ref[...] * LOG2E, -1e9 * LOG2E)
    bias = jnp.concatenate([bias, jnp.zeros((8, 128), F32)], axis=0)
    wide = lax.broadcasted_iota(jnp.int32, (48, 128), 1)
    for g in range(4):
        rows = slice(g * 48, g * 48 + 48)
        part = bias if g == 3 else pltpu.roll(bias, 96 - 32 * g, 1)
        for ii in range(8):
            held = send_ref[ii, rows, :].astype(F32)
            send_ref[ii, rows, :] = jnp.where(wide < 96, held, part).astype(BF16)


def turn_kernel(slab_ref, attn_w_ref, move_ref, out_ref):
    gate_w = jnp.dot(attn_w_ref[...], move_ref[...], preferred_element_type=F32).astype(BF16)
    lane = lax.broadcasted_iota(jnp.int32, (24, 128), 1)

    def step(ii, carry):
        first = jnp.concatenate(
            [slab_ref[base * 8 + ii].astype(F32) for base in range(5)], axis=1
        )
        center = first - jnp.mean(first, axis=0, keepdims=True)
        spread = jnp.mean(center * center, axis=0, keepdims=True)
        normed = center * lax.rsqrt(spread + 1e-05)
        turned = jnp.concatenate(
            [normed[:, base * 128 : base * 128 + 128].T for base in range(5)], axis=0
        )
        gate = jnp.dot(turned.astype(BF16), gate_w, preferred_element_type=F32)
        place = {}
        for base in range(5):
            plain = first[:, base * 128 : base * 128 + 128].T.astype(BF16)
            for n, (s, jc) in enumerate(slab_chunks(base)):
                out_ref[ii, s * 96 + jc * 32 : s * 96 + jc * 32 + 32, :] = plain[
                    n * 32 : n * 32 + 32
                ]
                place[s, jc] = gate[base * 128 + n * 32 : base * 128 + n * 32 + 32]
        packed = []
        for s in range(6):
            whole = sigmoid(jnp.concatenate([place[s, jc] for jc in range(3)], axis=0))
            g = [whole[q * 24 : q * 24 + 24] for q in range(4)]
            low = jnp.where(lane < 32, g[0], g[1])
            high = jnp.where(lane < 96, g[2], g[3])
            packed.append(jnp.where(lane < 64, low, high))
        out_ref[ii, 576:720, :] = jnp.concatenate(packed, axis=0).astype(BF16)
        return carry

    lax.fori_loop(0, 8, step, 0)


def bias_kernel(held_ref, out_ref):
    wide = lax.broadcasted_iota(jnp.int32, (48, 128), 1)

    def slabs(block):
        g = [held_ref[block, q * 48 : q * 48 + 48, :].astype(F32) for q in range(4)]
        g = [pltpu.roll(g[q], 32 * q + 32, 1) for q in range(3)] + [g[3]]
        low = jnp.where(wide < 32, g[0], g[1])
        return jnp.where(wide < 64, low, jnp.where(wide < 96, g[2], g[3]))[0:40]

    both = swap_blocks(
        [jnp.concatenate([slabs(yl * 4 + z) for yl in range(2)], axis=0) for z in range(4)]
    )
    tiles = []
    for yl in range(2):
        parts = [part[yl * 40 : yl * 40 + 40] for part in both]
        tiles.append([p[0:8] for p in parts] + [parts[0][24:32], parts[1][24:32]])
        tiles.append([p[8:16] for p in parts] + [parts[2][24:32], parts[3][24:32]])
        tiles.append([p[16:24] for p in parts] + [parts[0][32:40], parts[1][32:40]])
    whole = jnp.concatenate([jnp.concatenate(t, axis=0) for t in tiles], axis=1).astype(BF16)
    for copy in range(8):
        out_ref[copy] = whole


def split(held_ref, move_ref, out_ref, s):
    turned = jnp.concatenate(
        [
            held_ref[yl * 4 + z, pl.ds(pl.multiple_of(s * 96 + jc * 32, 32), 32), :]
            for yl in range(2)
            for jc in range(3)
            for z in range(4)
        ],
        axis=0,
    )
    out_ref[s] = jnp.dot(turned, move_ref[...], preferred_element_type=F32).astype(BF16)


def attend_half(half, held_ref, keyed_ref, bias_ref, extra_ref, packed_ref, move_ref=None):
    for c in range(8):
        extra_ref[c * 48 : c * 48 + 48, :] = bias_ref[c].astype(F32)
    blocks = 8 // PARTS
    size = blocks * 48
    wide = lax.broadcasted_iota(jnp.int32, (size, 128), 1)
    lane = lax.broadcasted_iota(jnp.int32, (24, 128), 1)

    def step(s, carry):
        if move_ref is not None:
            split(held_ref, move_ref, keyed_ref, s)
        value = jnp.concatenate([keyed_ref[s], jnp.ones((768, 128), BF16)], axis=1)
        at = pl.ds(pl.multiple_of(s * 96 + half * 48, 16), 48)
        for t in range(PARTS):
            rows = jnp.concatenate(
                [held_ref[t * blocks + c, at, :] for c in range(blocks)], axis=0
            )
            query = jnp.where(wide < 32, rows, jnp.zeros_like(rows))
            scores = lax.dot_general(
                query, keyed_ref[s], (((1,), (1,)), ((), ())), preferred_element_type=F32
            )
            scores = scores + extra_ref[t * size : (t + 1) * size, :]
            top = jnp.max(scores, axis=-1, keepdims=True)
            weights = jnp.exp2(scores - top).astype(BF16)
            summed = jnp.dot(weights, value, preferred_element_type=F32)
            result = summed[:, 0:128] / summed[:, 128:256]
            for h in range(blocks):
                row = pl.multiple_of((t * blocks + h) * 144 + s * 24, 8)
                packed_ref[pl.ds(row, 24), :] = jnp.where(
                    lane < 96, result[h * 48 : h * 48 + 24], result[h * 48 + 24 : h * 48 + 48]
                )
        return carry

    lax.fori_loop(0, 6, step, 0, unroll=UNROLL_ATTEND)


def attend_mine_kernel(held_ref, move_ref, bias_ref, out_ref, keyed_ref, extra_ref, packed_ref):
    half = lax.axis_index("core")
    attend_half(half, held_ref, keyed_ref, bias_ref, extra_ref, packed_ref, move_ref)
    for c in range(8):
        out_ref[c] = packed_ref[c * 144 : (c + 1) * 144, :].astype(BF16)


def attend_other_kernel(held_ref, keyed_ref, bias_ref, mine_ref, out_ref, extra_ref, packed_ref):
    half = 1 - lax.axis_index("core")
    attend_half(half, held_ref, keyed_ref, bias_ref, extra_ref, packed_ref)
    lane = lax.broadcasted_iota(jnp.int32, (144, 128), 1)
    for c in range(8):
        mine, other = mine_ref[c].astype(F32), packed_ref[c * 144 : (c + 1) * 144, :]
        low = jnp.where(half == 0, other, mine)
        high = jnp.where(half == 0, mine, other)
        out_ref[c] = jnp.where(lane < 64, pltpu.roll(low, 64, 1), high).astype(BF16)


def update_kernel(held_ref, first_ref, weight_ref, out_hbm, wide_ref, done_ref, out_sems):
    def store(ii):
        return pltpu.make_async_copy(done_ref.at[:, ii], out_hbm.at[:, ii], out_sems.at[ii])

    wide_ref[...] = jnp.zeros((128, 512), BF16)
    for g in range(4):
        wide_ref[g * 32 : g * 32 + 32, g * 128 : g * 128 + 128] = weight_ref[...]

    def step(ii, carry):
        gated = held_ref[ii].astype(F32) * first_ref[ii, 576:720, :].astype(F32)
        add = jnp.dot(gated.astype(BF16), wide_ref[...], preferred_element_type=F32)
        for s in range(6):
            rows = jnp.concatenate(
                [add[s * 24 : s * 24 + 24, g * 128 : (g + 1) * 128] for g in range(4)], axis=0
            )
            first = first_ref[ii, s * 96 : (s + 1) * 96, :].astype(F32)
            done_ref[s, ii] = (first + rows).astype(BF16)
        store(ii).start()
        return carry

    lax.fori_loop(0, 8, step, 0, unroll=UNROLL_UPDATE)
    for ii in range(8):
        store(ii).wait()


def call(kernel, outs, in_specs, out_specs, scratch, limit=LIMIT_OTHER, work=0):
    cost = pl.CostEstimate(flops=work * 10**9, bytes_accessed=work * 10**6, transcendentals=0)
    return pl.pallas_call(
        kernel,
        out_shape=outs,
        in_specs=in_specs,
        out_specs=out_specs,
        scratch_shapes=scratch,
        cost_estimate=cost if work else None,
        compiler_params=pltpu.CompilerParams(vmem_limit_bytes=limit * 1024 * 1024),
    )


def shape(dims, dtype=BF16):
    return jax.ShapeDtypeStruct(dims, dtype)


def exchange(values, axes):
    return lax.all_to_all(values, axes, 0, 0, tiled=True)


def body(
    pair,
    residue_mask,
    left_weight,
    right_weight,
    gate_weight,
    out_weight,
    attn_weight,
    bias_weight,
    attn_out_weight,
):
    pair = pair.reshape(6, 8, 96, 128)
    wire = call(
        project_kernel,
        shape((128, 72, 128)),
        [HBM, pl.BlockSpec(memory_space=pltpu.SMEM), HBM, HBM],
        HBM,
        [
            pltpu.VMEM((6, 8, 96, 128), BF16),
            pltpu.VMEM((73 * PITCH, 128), F32),
            pltpu.VMEM((128, 256), BF16),
            pltpu.VMEM((128, 256), BF16),
            pltpu.VMEM((512, 128), BF16),
            pltpu.VMEM((96, 128), F32),
            pltpu.VMEM((128, 72, 128), BF16),
            pltpu.SemaphoreType.DMA((LOADS,)),
            pltpu.SemaphoreType.DMA((2,)),
            pltpu.SemaphoreType.DMA((STORES,)),
        ],
        LIMIT_PROJECT,
    )(pair, residue_mask, left_weight, right_weight)
    wire = exchange(wire, ALL)
    gate = call(gate_kernel, shape((40, 128, 128)), [VMEM] * 2, VMEM, [], work=3)(
        pair, gate_weight
    )

    col_mask = lax.dynamic_slice_in_dim(residue_mask, lax.axis_index(COL) * 96, 96).reshape(3, 32)
    chunk = lambda jc: jnp.tile(col_mask[jc], 4)
    split = jnp.concatenate([col_mask[0], col_mask[0], col_mask[1], col_mask[1]])
    mask = jnp.repeat(jnp.stack([chunk(0), chunk(1), chunk(2), split, chunk(2)]), 8, axis=0)
    gate, mask, wire = lax.optimization_barrier((gate, mask, wire))
    sums = call(
        triangle_kernel,
        shape((128, 40, 128)),
        [VMEM],
        VMEM,
        [
            pltpu.VMEM((768, 768), BF16),
            pltpu.VMEM((768, 768), BF16),
            pltpu.VMEM((768, 768), F32),
            pltpu.VMEM((512, 512), BF16),
        ],
    )(wire)
    sums = exchange(sums, ALL)
    send, first = call(
        first_kernel,
        (shape((8, 576, 128)), shape((40, 128, 128))),
        [VMEM] * 7,
        (VMEM, VMEM),
        [pltpu.VMEM((129 * 40, 128), F32), pltpu.VMEM((40, 128), F32)],
    )(sums, pair, gate, out_weight, attn_weight, bias_weight[None, :], mask)
    held = exchange(send, COL)
    first, held = lax.optimization_barrier((first, held))
    bias = call(bias_kernel, shape((8, 48, 768)), [VMEM], VMEM, [])(held)
    bias = exchange(bias, ("x", "yh"))
    first = call(turn_kernel, shape((8, 720, 128)), [VMEM] * 3, VMEM, [], work=WORK_LATE)(
        first, attn_weight, jnp.asarray(GATE_MOVE, BF16)
    )
    first, bias = lax.optimization_barrier((first, bias))
    other = lax.ppermute(bias, "core", [(0, 1), (1, 0)])
    scratch = [pltpu.VMEM((384, 768), F32), pltpu.VMEM((8 * 144, 128), F32)]
    mine, keyed = call(
        attend_mine_kernel,
        (shape((8, 144, 128)), shape((6, 768, 128))),
        [VMEM] * 3,
        (VMEM, VMEM),
        scratch,
        work=WORK_MINE,
    )(held, jnp.asarray(KEY_MOVE, BF16), bias)
    gated = call(
        attend_other_kernel, shape((8, 144, 128)), [VMEM] * 4, VMEM, scratch, work=2
    )(held, keyed, other, mine)
    gated = exchange(gated, COL)
    updated = call(
        update_kernel,
        shape((6, 8, 96, 128)),
        [VMEM, VMEM, VMEM],
        HBM,
        [
            pltpu.VMEM((128, 512), BF16),
            pltpu.VMEM((6, 8, 96, 128), BF16),
            pltpu.SemaphoreType.DMA((8,)),
        ],
        LIMIT_UPDATE,
    )(gated, first, attn_out_weight)
    return updated.reshape(48, 96, 128)


def solution(mesh):
    parts = Mesh(mesh.devices.reshape(4, 2, 2, 2, 4), ALL)
    spec = P(("x", "yh", "core"), COL, None)
    return jax.shard_map(
        body,
        mesh=parts,
        in_specs=(spec, P(), P(), P(), P(), P(), P(), P(), P()),
        out_specs=spec,
        check_vma=False,
    )
```
